128 devices in a mesh: dom: 32 (over y, z_lo, x), orb: 4 (over z_hi, core).
Axes of the slice: x: 4, y: 4, z: 4 (z_hi: 2, z_lo: 2; z = z_hi * 2 + z_lo), core: 2. Of those that a mesh axis runs over, the one named last changes fastest.
Arguments:
- orbitals: float32 [32, 32, 32, 24, 128], P('orb', 'dom'), may hold values from -90 to 90
- potential: float32 [32, 32, 24, 128], P('dom'), may hold values from -1 to 0.5
Outputs:
- filtered: float32 [32, 32, 32, 24, 128], P('orb', 'dom')
- correlation: float32 [32, 32], replicated
- subspace: float32 [32, 32], replicated
The draws below stay inside these ranges and needn't reach their ends.
All inputs are finite; a program needn't handle non-finite values.
Results may differ from the reference program's by a relative error of at most 0.0001.
Values sent between devices are 32-bit elements; how exact they have to be, the bound alone decides.
A program may use at most 128 MiB of HBM per device.

```python
import functools
import math
import jax
import jax.numpy as jnp
from jax import lax

NORB = 32
HALO = 6
DEG = 2
CX = 32
CY = 24
CZ = 128
PZ = 2
PY = 4
PX = 4
BLOCKS = 32


def face_mask(block_coord, block_count, length):
    position = jnp.arange(length)
    far_lower = position
    far_upper = length - 1 - position
    lower_hit = (block_coord[:, None] > 0) & (far_lower[None, :] >= HALO - 2) & (far_lower[None, :] <= HALO - 1)
    upper_hit = (block_coord[:, None] < block_count - 1) & (far_upper[None, :] >= HALO - 2) & (far_upper[None, :] <= HALO - 1)
    sign_lower = 1.0 - 2.0 * ((far_lower - HALO) % 2).astype(jnp.float32)
    sign_upper = 1.0 - 2.0 * ((far_upper - HALO) % 2).astype(jnp.float32)
    sign_field = jnp.where(lower_hit, sign_lower[None, :], sign_upper[None, :])
    return (lower_hit | upper_hit, sign_field)


def draw_orbitals(key, part):
    key = jax.random.fold_in(key, 11)
    subkeys = jax.random.split(key, 6)
    full_dims = (NORB + 1, BLOCKS, CX, CY, CZ)
    block_ids = jnp.arange(BLOCKS)
    block_x = block_ids // (PY * PZ)
    block_y = block_ids // PZ % PY
    block_z = block_ids % PZ
    fraction = (block_x[:, None] * CX + jnp.arange(CX)[None, :]).astype(jnp.float32) / (PX * CX)
    fraction = fraction[None, :, :, None, None]
    row_scale = jnp.exp(math.log(10.0) * (jax.random.uniform(subkeys[1], (BLOCKS, CX, CY, CZ), jnp.float32) - 0.5))
    col_scale = jnp.exp(math.log(10.0) * (jax.random.uniform(subkeys[2], (NORB,), jnp.float32) - 0.5))
    col_scale = col_scale[:, None, None, None, None]
    mask_x, sign_x = face_mask(block_x, PX, CX)
    mask_y, sign_y = face_mask(block_y, PY, CY)
    mask_z, sign_z = face_mask(block_z, PZ, CZ)
    boosted = mask_x[:, :, None, None] | mask_y[:, None, :, None] | mask_z[:, None, None, :]
    face_sign = jnp.where(mask_x[:, :, None, None], sign_x[:, :, None, None], jnp.where(mask_y[:, None, :, None], sign_y[:, None, :, None], sign_z[:, None, None, :]))
    orbital_sign = 2.0 * jax.random.randint(subkeys[4], (NORB, BLOCKS), 0, 2).astype(jnp.float32) - 1.0
    magnitude = 0.55 + 0.45 * jax.random.uniform(subkeys[5], (NORB, BLOCKS, CX, CY, CZ), jnp.float32, -1.0, 1.0)
    noise = jax.random.normal(subkeys[0], full_dims, jnp.float32)
    rising = 0.5 + fraction
    mixture = jnp.clip(noise[1:] + 0.6 * noise[:-1], -6.0, 6.0)
    bulk = jnp.clip(mixture * row_scale[None], -4.0, 4.0)
    face_values = 18.0 * orbital_sign[:, :, None, None, None] * face_sign[None] * magnitude
    values = jnp.where(boosted[None], face_values, bulk) * col_scale * rising
    return jnp.clip(values, -90.0, 90.0)


def block_levels(stream_key, extent, cuts, low, high):
    gain, own = 1.0, jax.random.fold_in(stream_key, 6)
    for axis_at, shards_of in cuts:
        draws = jnp.exp(jax.random.uniform(jax.random.fold_in(own, axis_at), (shards_of,), jnp.float32, low / len(cuts), high / len(cuts)))
        gain = gain * jnp.repeat(draws, extent[axis_at] // shards_of).reshape([-1 if axis == axis_at else 1 for axis in range(len(extent))])
    return gain


def setup_inputs(seed: int = 0) -> dict:
    key_of = jax.random.split(jax.random.key(seed), 3)
    return {
        "orbitals": draw_orbitals(jax.random.fold_in(key_of[2], 71), 0),
        "potential": jnp.clip(-1.0 + 1.5 * jax.random.uniform(key_of[1], (BLOCKS, CX, CY, CZ), jnp.float32) ** block_levels(key_of[1], (BLOCKS, CX, CY, CZ), ((0, 32),), -0.2, 0.2), -1.0, 0.5),
    }


SPACING = 0.5
UPPER = 44.0
CUTOFF = 4.0
LOWEST = -1.0


def stencil_weights():
    weights = []
    for offset in range(1, HALO + 1):
        weights.append(2.0 * (-1.0) ** (offset + 1) * math.factorial(HALO) ** 2
                       / (offset * offset * math.factorial(HALO - offset) * math.factorial(HALO + offset)))
    return weights


def along(extended, axis_pos, length):
    weights = stencil_weights()
    center = lax.slice_in_dim(extended, HALO, HALO + length, axis=axis_pos)
    summed = (-2.0 * sum(weights)) * center
    for offset in range(1, HALO + 1):
        ahead = lax.slice_in_dim(extended, HALO + offset, HALO + offset + length, axis=axis_pos)
        behind = lax.slice_in_dim(extended, HALO - offset, HALO - offset + length, axis=axis_pos)
        summed = summed + weights[offset - 1] * (ahead + behind)
    return summed


def hamilton(values, pot_field):
    laplace = jnp.zeros_like(values)
    for axis_pos in (1, 2, 3):
        widths = [(0, 0)] * 4
        widths[axis_pos] = (HALO, HALO)
        padded = jnp.pad(values, widths)
        laplace = laplace + along(padded, axis_pos, values.shape[axis_pos])
    return (-0.5 / SPACING ** 2) * laplace + pot_field[None] * values


def chebyshev(start, apply_fn):
    half_width = (UPPER - CUTOFF) / 2.0
    middle = (UPPER + CUTOFF) / 2.0
    sigma_now = half_width / (LOWEST - middle)
    gamma_value = 2.0 / sigma_now
    previous = start
    current = (sigma_now / half_width) * (apply_fn(start) - middle * start)
    for degree_step in range(1, DEG):
        sigma_next = 1.0 / (gamma_value - sigma_now)
        following = (2.0 * sigma_next / half_width) * (apply_fn(current) - middle * current) - (sigma_now * sigma_next) * previous
        previous, current, sigma_now = current, following, sigma_next
    return current


def to_grid(blocked):
    leading = blocked.shape[0]
    sectioned = blocked.reshape(leading, PX, PY, PZ, CX, CY, CZ)
    return sectioned.transpose(0, 1, 4, 2, 5, 3, 6).reshape(leading, PX * CX, PY * CY, PZ * CZ)


def to_blocks(grid_block):
    leading = grid_block.shape[0]
    sectioned = grid_block.reshape(leading, PX, CX, PY, CY, PZ, CZ)
    return sectioned.transpose(0, 1, 3, 5, 2, 4, 6).reshape(leading, PX * PY * PZ, CX, CY, CZ)


def reference(orbitals, potential):
    start = to_grid(orbitals)
    pot_field = to_grid(potential[None])[0]
    apply_fn = functools.partial(hamilton, pot_field=pot_field)
    result = chebyshev(start, apply_fn)
    image = apply_fn(result)
    flattened = result.reshape(NORB, -1)
    image_flat = image.reshape(NORB, -1)
    count_cells = flattened.shape[1]
    half_width = (UPPER - CUTOFF) / 2.0
    correlation = jnp.dot(flattened, flattened.T, precision=lax.Precision.HIGHEST,
                      preferred_element_type=jnp.float32) / count_cells
    subspace = jnp.dot(flattened, image_flat.T, precision=lax.Precision.HIGHEST,
                       preferred_element_type=jnp.float32) / (count_cells * half_width)
    return to_blocks(result), correlation, subspace
```

```python
import math

import jax
import jax.numpy as jnp
import numpy as np
from jax import lax
from jax.experimental import pallas as pl
from jax.experimental.pallas import tpu as pltpu
from jax.sharding import PartitionSpec as P

HALO = 6
SPACING = 0.5
UPPER = 44.0
CUTOFF = 4.0
LOWEST = -1.0
NX, NY, NZ, NO = 32, 24, 128, 8
CELLS = 3145728
CHUNK = 8
ORDER = (0, 3, 1, 2)
MESH = pl.DeviceIdType.MESH
F32, BF16 = jnp.float32, jnp.bfloat16
HIGH = lax.Precision.HIGHEST


def stencil_weights():
    return [
        2.0 * (-1.0) ** (m + 1) * math.factorial(HALO) ** 2
        / (m * m * math.factorial(HALO - m) * math.factorial(HALO + m))
        for m in range(1, HALO + 1)
    ]


WEIGHTS = stencil_weights()
KINETIC = -0.5 / SPACING**2
CENTRE = KINETIC * 3.0 * (-2.0 * sum(WEIGHTS))
HALF = (UPPER - CUTOFF) / 2.0
MIDDLE = (UPPER + CUTOFF) / 2.0
SIGMA1 = HALF / (LOWEST - MIDDLE)
SIGMA2 = 1.0 / (2.0 / SIGMA1 - SIGMA1)


def doubled(matrix):
    wide = matrix.astype(np.float32)
    hi = wide.astype(BF16)
    lo = (wide - hi.astype(np.float32)).astype(BF16)
    row = np.concatenate([hi, lo], axis=1)
    return np.concatenate([row, row], axis=0)


def z_matrices():
    own = np.zeros((NZ, NZ))
    above = np.zeros((NZ, NZ))
    below = np.zeros((NZ, NZ))
    for z in range(NZ):
        for m in range(1, HALO + 1):
            weight = KINETIC * WEIGHTS[m - 1]
            for k in (z - m, z + m):
                if 0 <= k < NZ:
                    own[k, z] = weight
                elif k >= NZ:
                    above[k - NZ, z] = weight
                else:
                    below[k + HALO, z] = weight
    return np.stack([doubled(own), doubled(above), doubled(below)])


def split_wide(v):
    hi = v.astype(BF16)
    lo = (v - hi.astype(F32)).astype(BF16)
    return jnp.concatenate([hi, lo], axis=1)


def split_tall(v):
    hi = v.astype(BF16).astype(F32)
    return jnp.concatenate([hi, v - hi], axis=0).astype(BF16)


def gram(left, right):
    rows, cols = left.shape[0], right.shape[0]
    full = lax.dot_general(
        split_tall(left), split_tall(right), (((1,), (1,)), ((), ())), preferred_element_type=F32
    )
    return (full[:rows, :cols] + full[rows:, :cols]) + (full[:rows, cols:] + full[rows:, cols:])


def flat(block):
    return jnp.concatenate([block[j] for j in range(block.shape[0])], axis=1)


def kernel(orb_hbm, pot_hbm, zmat_ref, out_hbm, cor_ref, sub_ref,
           inp, pot, e0, e1, e2, hf, zacc, potb, zf, zh, oc, oh, gb, part, ar,
           in_sem, pot_sem, out_sem,
           y_ss, y_rs, x_ss, x_rs, z_ss, z_rs, oc_ss, oc_rs, oh_ss, oh_rs, g_ss, g_rs, a_ss, a_rs):
    d = lax.axis_index("dom")
    o = lax.axis_index("orb")
    bx, by, bz = d // 8, (d // 2) % 4, d % 2
    chip, core = o // 2, o % 2
    px, pzl = d % 4, (d // 4) % 2
    other_core = (d, o + 1 - 2 * core)
    other_chip = (d, (o + 2) % 4)
    group = [(d, (o + j) % 4) for j in (1, 2, 3)]
    xs = [((d // 4) * 4 + (px + j) % 4, o) for j in (1, 2, 3)]
    ys = [((d + 8 * j) % 32, o) for j in (1, 2, 3)]
    zl = ((d + 4 - 8 * pzl), o)
    lower = {"x": (d - 8, o), "y": (d - 2, o)}
    upper = {"x": (d + 8, o), "y": (d + 2, o)}
    has_lower = {"x": bx > 0, "y": by > 0}
    has_upper = {"x": bx < 3, "y": by < 3}
    is_a, is_b = chip == 0, chip == 1

    def when(cond, fn):
        if cond is None:
            fn()
        else:
            pl.when(cond)(lambda: fn() and None)

    loads = [
        pltpu.make_async_copy(
            orb_hbm.at[:, 0, pl.ds(CHUNK * k, CHUNK)], inp.at[:, pl.ds(CHUNK * k, CHUNK)], in_sem.at[k])
        for k in range(4)
    ]
    for k in ORDER:
        loads[k].start()
    pot_load = pltpu.make_async_copy(pot_hbm.at[0], pot, pot_sem)
    pot_load.start()

    barrier = pltpu.get_barrier_semaphore()
    for dev in group + xs + ys + [zl]:
        pl.semaphore_signal(barrier, inc=1, device_id=dev, device_id_type=MESH)

    @pl.when(by == 1)
    def _():
        pl.semaphore_signal(barrier, inc=1, device_id=upper["y"], device_id_type=MESH)

    @pl.when(by == 2)
    def _():
        pl.semaphore_signal(barrier, inc=1, device_id=lower["y"], device_id_type=MESH)

    for buf in (e0, e1, e2):
        @pl.when(bx == 0)
        def _(buf=buf):
            buf[0:HALO] = jnp.zeros((HALO, NY + 12, 8, 128), F32)

        @pl.when(bx == 3)
        def _(buf=buf):
            buf[NX + HALO:] = jnp.zeros((HALO, NY + 12, 8, 128), F32)

        @pl.when(by == 0)
        def _(buf=buf):
            @pl.loop(0, NX)
            def _(x):
                buf[HALO + x, 0:HALO] = jnp.zeros((HALO, 8, 128), F32)

        @pl.when(by == 3)
        def _(buf=buf):
            @pl.loop(0, NX)
            def _(x):
                buf[HALO + x, NY + HALO:] = jnp.zeros((HALO, 8, 128), F32)

    pl.semaphore_wait(barrier, 10 + jnp.where((by == 1) | (by == 2), 1, 0))

    def y_copy(stage, buf, k, side):
        rows = pl.ds(HALO + CHUNK * k, CHUNK)
        src, dst = ((HALO, NY + HALO), (NY, 0))[side]
        return pltpu.make_async_remote_copy(
            src_ref=buf.at[rows, pl.ds(src, HALO)], dst_ref=buf.at[rows, pl.ds(dst, HALO)],
            send_sem=y_ss.at[stage, k, side], recv_sem=y_rs.at[stage, k, side],
            device_id=(lower, upper)[side]["y"], device_id_type=MESH)

    def x_copy(stage, buf, side):
        src, dst = ((HALO, NX + HALO), (NX, 0))[side]
        cols = pl.ds(HALO, NY)
        return pltpu.make_async_remote_copy(
            src_ref=buf.at[pl.ds(src, HALO), cols], dst_ref=buf.at[pl.ds(dst, HALO), cols],
            send_sem=x_ss.at[stage, side], recv_sem=x_rs.at[stage, side],
            device_id=(lower, upper)[side]["x"], device_id_type=MESH)

    def z_copy(stage):
        return pltpu.make_async_remote_copy(
            src_ref=zf.at[stage], dst_ref=zh.at[stage],
            send_sem=z_ss.at[stage], recv_sem=z_rs.at[stage],
            device_id=(d + 1 - 2 * bz, o), device_id_type=MESH)

    def sends(axis, side):
        return (has_lower, has_upper)[side][axis]

    def receives(axis, side):
        return (has_upper, has_lower)[side][axis]

    def send_y(stage, buf, k):
        for side in (0, 1):
            when(sends("y", side), lambda: y_copy(stage, buf, k, side).start())

    def wait_y(stage, buf, k):
        for side in (0, 1):
            when(receives("y", side), lambda: y_copy(stage, buf, k, side).wait_recv())

    def send_x(stage, buf, side):
        when(sends("x", side), lambda: x_copy(stage, buf, side).start())

    def wait_x(stage, buf):
        for side in (0, 1):
            when(receives("x", side), lambda: x_copy(stage, buf, side).wait_recv())

    lane = lax.broadcasted_iota(jnp.int32, (8, 128), 1)

    def pack_z(stage, buf):
        first = jnp.where(bz == 0, NZ - HALO, 0)

        @pl.loop(0, 2)
        def _(half):
            @pl.loop(0, NY)
            def _(y):
                total = None
                for x in range(16):
                    moved = pltpu.roll(
                        buf[HALO + 16 * half + x, HALO + y], lax.rem(8 * x + 128 - first, 128), axis=1)
                    total = moved if total is None else jnp.where(lane // 8 == x, moved, total)
                zf[stage, half, y] = total

    def z_own(buf):
        @pl.loop(0, NX // 4)
        def _(t):
            v = buf[pl.ds(HALO + 4 * t, 4), pl.ds(HALO, NY)].reshape(4 * NY * 8, 128)
            r = jnp.dot(split_wide(v), zmat_ref[0], preferred_element_type=F32)
            zacc[pl.ds(4 * t, 4)] = (r[:, :128] + r[:, 128:]).reshape(4, NY, 8, 128)

    def z_halo(stage):
        @pl.loop(0, NX // 4)
        def _(t):
            parts = []
            for j in range(4):
                x = 4 * t + j
                packed = zh[stage, x // 16].reshape(NY * 8, 128)
                parts.append(pltpu.roll(packed, lax.rem(128 - 8 * lax.rem(x, 16), 128), axis=1))
            v = jnp.concatenate(parts, axis=0)
            r = jnp.dot(split_wide(v), zmat_ref[1 + bz], preferred_element_type=F32)
            zacc[pl.ds(4 * t, 4)] += (r[:, :128] + r[:, 128:]).reshape(4, NY, 8, 128)

    def rows_of(src, dst, off, x, y, scale, shift, prev, prev_scale):
        def at(dx, dy):
            return src[x + HALO + dx, pl.ds(y + HALO + dy, HALO)]

        total = scale * zacc[x, pl.ds(y, HALO)]
        total += (scale * potb[x, pl.ds(y, HALO)] + (scale * CENTRE + shift)) * at(0, 0)
        for m in range(1, HALO + 1):
            near = (at(m, 0) + at(-m, 0)) + (at(0, m) + at(0, -m))
            total += (scale * KINETIC * WEIGHTS[m - 1]) * near
        if prev is not None:
            total -= prev_scale * prev[x + HALO, pl.ds(y + HALO, HALO)]
        dst[x + off, pl.ds(y + off, HALO)] = total

    def stage_rows(lo, hi, ys_, *args):
        @pl.loop(lo, hi)
        def _(x):
            for y in ys_:
                rows_of(args[0], args[1], args[2], x, y, *args[3:])

    pend = []

    def stage(n, src, dst, off, scale, shift, prev, prev_scale, after):
        args = (src, dst, off, scale, shift, prev, prev_scale)
        z_own(src)
        z_copy(n).wait_recv()
        z_halo(n)
        stage_rows(HALO, NX - HALO, (6, 12), *args)
        wait_x(n, src)
        stage_rows(0, HALO, (6, 12), *args)
        stage_rows(NX - HALO, NX, (6, 12), *args)
        for k in ORDER:
            wait_y(n, src, k)
            stage_rows(CHUNK * k, CHUNK * k + CHUNK, (0, 18), *args)
            after(k)

    def pass_on(n, buf, k):
        send_y(n, buf, k)
        if k == 0:
            send_x(n, buf, 0)
        if k == 3:
            send_x(n, buf, 1)

    flat_in = inp.reshape(NO * NX * NY, 128)
    for k in ORDER:
        loads[k].wait()

        @pl.loop(CHUNK * k, CHUNK * k + CHUNK)
        def _(x):
            for y in range(NY):
                e0[HALO + x, HALO + y] = flat_in[pl.ds(x * NY + y, 8, stride=NX * NY), :]
        pass_on(0, e0, k)
    pack_z(0, e0)
    z_copy(0).start()
    pot_load.wait()

    @pl.loop(0, NX)
    def _(x):
        for y in range(NY):
            potb[x, y] = jnp.broadcast_to(pot[x, pl.ds(y, 1)], (8, 128))

    stage(0, e0, e1, HALO, SIGMA1 / HALF, -SIGMA1 / HALF * MIDDLE, None, 0.0,
          lambda k: pass_on(1, e1, k))
    pack_z(1, e1)
    z_copy(1).start()

    def core_copy(k):
        return pltpu.make_async_remote_copy(
            src_ref=e2.at[pl.ds(HALO + CHUNK * k, CHUNK), pl.ds(HALO, NY)],
            dst_ref=oc.at[pl.ds(CHUNK * k, CHUNK)],
            send_sem=oc_ss.at[k], recv_sem=oc_rs.at[k], device_id=other_core, device_id_type=MESH)

    def chip_copy(src, y, slot, k):
        return pltpu.make_async_remote_copy(
            src_ref=src, dst_ref=gb.at[slot, pl.ds(CHUNK * k, CHUNK)],
            send_sem=g_ss.at[slot, k], recv_sem=g_rs.at[slot, k],
            device_id=other_chip, device_id_type=MESH)

    def f_rows(k, y):
        return e2.at[pl.ds(HALO + CHUNK * k, CHUNK), pl.ds(HALO + y, 8)]

    def f_copies(k):
        pass_on(2, e2, k)
        core_copy(k).start()

        @pl.when(is_a)
        def _():
            chip_copy(f_rows(k, 0), 0, 0, k).start()
            chip_copy(f_rows(k, 16), 16, 1, k).start()

        @pl.when(is_b)
        def _():
            chip_copy(f_rows(k, 8), 8, 0, k).start()

    s2 = 2.0 * SIGMA2 / HALF
    stage(1, e1, e2, HALO, s2, -s2 * MIDDLE, e0, SIGMA1 * SIGMA2, f_copies)
    pack_z(2, e2)
    z_copy(2).start()

    @pl.loop(0, NX)
    def _(x):
        for orb in range(NO):
            inp[orb, x] = e2[HALO + x, pl.ds(HALO, NY), orb]
    out_copy = pltpu.make_async_copy(inp, out_hbm.at[:, 0], out_sem)
    out_copy.start()

    def h_rows(k, y):
        return hf.at[pl.ds(CHUNK * k, CHUNK), pl.ds(y, 8)]

    def oh_copy(k, j):
        return pltpu.make_async_remote_copy(
            src_ref=h_rows(k, 16 * j), dst_ref=oh.at[pl.ds(CHUNK * k, CHUNK), pl.ds(8 * j, 8)],
            send_sem=oh_ss.at[k, j], recv_sem=oh_rs.at[k, j], device_id=other_core, device_id_type=MESH)

    def h_copies(k):
        @pl.when(is_b)
        def _():
            chip_copy(h_rows(k, 8), 8, 1, k).start()
            for j in (0, 1):
                oh_copy(k, j).start()

    stage(2, e2, hf, 0, 1.0, 0.0, None, 0.0, h_copies)

    part[...] = jnp.zeros_like(part)
    for k in range(4):
        core_copy(k).wait_recv()

    def own_f(x, y, n):
        return flat(e2[HALO + x, pl.ds(HALO + y, n)])

    def in_chip(x, total):
        left = jnp.concatenate([own_f(x, 0, NY), flat(oc[x])], axis=0)
        right = jnp.concatenate([own_f(x, 0, NY), flat(hf[x])], axis=0)
        return total + gram(left, right)

    def place(block, starts):
        n = block.shape[1]
        r = lax.broadcasted_iota(jnp.int32, (n, 128), 0)
        c = lax.broadcasted_iota(jnp.int32, (n, 128), 1)
        chosen = jnp.zeros((n, 128), jnp.bool_)
        for j, s in enumerate(starts):
            chosen = chosen | ((r // 8 == j) & (c == s + r % 8))
        return jnp.dot(block, chosen.astype(F32), precision=HIGH, preferred_element_type=F32)

    def add_rows(orbital, block):
        rows = pl.ds(pl.multiple_of(8 * orbital, 8), 8)
        part[rows, :] += block

    o_core = o + 1 - 2 * core
    o_chip = (o + 2) % 4
    local = lax.fori_loop(0, NX, in_chip, jnp.zeros((16, 16), F32))
    placed = place(local, (8 * o, 32 + 8 * o))
    add_rows(o, placed[:8])
    add_rows(o_core, placed[8:])

    @pl.when(is_a)
    def _():
        for slot in (0, 1):
            for k in range(4):
                chip_copy(f_rows(k, 8), 8, slot, k).wait_recv()

        def cross(x, total):
            left = jnp.concatenate([own_f(x, 8, 8), flat(oc[x, pl.ds(8, 8)])], axis=0)
            right = jnp.concatenate([flat(gb[0, x]), flat(gb[1, x])], axis=0)
            return total + gram(left, right)

        block = place(lax.fori_loop(0, NX, cross, jnp.zeros((16, 16), F32)), (8 * o_chip, 32 + 8 * o_chip))
        add_rows(o, block[:8])
        add_rows(o_core, block[8:])

    @pl.when(is_b)
    def _():
        for slot in (0, 1):
            for k in range(4):
                chip_copy(f_rows(k, 8), 8, slot, k).wait_recv()
        for k in range(4):
            for j in (0, 1):
                oh_copy(k, j).wait_recv()

        def cross(x, total):
            left = jnp.concatenate([flat(gb[0, x]), flat(gb[1, x])], axis=1)
            right = [
                jnp.concatenate([own_f(x, 0, 8), own_f(x, 16, 8)], axis=1),
                jnp.concatenate([flat(oc[x, pl.ds(0, 8)]), flat(oc[x, pl.ds(16, 8)])], axis=1),
                jnp.concatenate([flat(hf[x, pl.ds(0, 8)]), flat(hf[x, pl.ds(16, 8)])], axis=1),
                flat(oh[x]),
            ]
            return total + gram(left, jnp.concatenate(right, axis=0))

        block = place(lax.fori_loop(0, NX, cross, jnp.zeros((8, 32), F32)),
                      (8 * o, 8 * o_core, 32 + 8 * o, 32 + 8 * o_core))
        add_rows(o_chip, block)

    def reduce(step, mine, count, partners):
        ar[step, mine] = part[...]
        copies = []
        for j, dev in enumerate(partners):
            copies.append(pltpu.make_async_remote_copy(
                src_ref=ar.at[step, mine], dst_ref=ar.at[step, mine],
                send_sem=a_ss.at[step, j], recv_sem=a_rs.at[step, mine],
                device_id=dev, device_id_type=MESH))
            copies[-1].start()
        for j, dev in enumerate(partners):
            source = lax.rem(mine + j + 1, count)
            pltpu.make_async_remote_copy(
                src_ref=ar.at[step, source], dst_ref=ar.at[step, source],
                send_sem=a_ss.at[step, j], recv_sem=a_rs.at[step, source],
                device_id=dev, device_id_type=MESH).wait_recv()
        total = ar[step, 0]
        for j in range(1, count):
            total += ar[step, j]
        part[...] = total
        for c in copies:
            c.wait_send()

    reduce(0, o, 4, group)
    reduce(1, px, 4, xs)
    reduce(2, bx, 4, ys)
    reduce(3, pzl, 2, [zl])

    square = part[...]
    r = lax.broadcasted_iota(jnp.int32, (32, 32), 0)
    c = lax.broadcasted_iota(jnp.int32, (32, 32), 1)
    eye = (r == c).astype(F32)
    for at, ref, factor in ((0, cor_ref, 1.0 / CELLS), (32, sub_ref, 1.0 / (CELLS * HALF))):
        m = square[:, at:at + 32]
        t = lax.dot_general(m, eye, (((0,), (0,)), ((), ())), precision=HIGH, preferred_element_type=F32)
        ref[...] = jnp.where((r >= 16) & (c < 16), t, m) * factor

    out_copy.wait()
    for n, buf in ((0, e0), (1, e1), (2, e2)):
        for side in (0, 1):
            for k in range(4):
                when(sends("y", side), lambda: y_copy(n, buf, k, side).wait_send())
            when(sends("x", side), lambda: x_copy(n, buf, side).wait_send())
        z_copy(n).wait_send()
    for k in range(4):
        core_copy(k).wait_send()
        for slot in (0, 1):
            chip_copy(f_rows(k, 8), 8, slot, k).wait_send()

    @pl.when(is_b)
    def _():
        for k in range(4):
            for j in (0, 1):
                oh_copy(k, j).wait_send()


def shards(orbitals, potential):
    zmat = jnp.asarray(z_matrices())
    field = (NX + 12, NY + 12, 8, 128)
    vm = lambda *shape: pltpu.VMEM(shape, F32)
    dma = lambda *shape: pltpu.SemaphoreType.DMA(shape)
    out, cor, sub = pl.pallas_call(
        kernel,
        out_shape=(
            jax.ShapeDtypeStruct((NO, 1, NX, NY, NZ), F32),
            jax.ShapeDtypeStruct((32, 32), F32),
            jax.ShapeDtypeStruct((32, 32), F32),
        ),
        in_specs=[pl.BlockSpec(memory_space=pl.ANY)] * 2 + [pl.BlockSpec(memory_space=pltpu.VMEM)],
        out_specs=(pl.BlockSpec(memory_space=pl.ANY),) + (pl.BlockSpec(memory_space=pltpu.VMEM),) * 2,
        scratch_shapes=[
            vm(NO, NX, NY, NZ), vm(NX, NY, NZ), vm(*field), vm(*field), vm(*field),
            vm(NX, NY, 8, 128), vm(NX, NY, 8, 128), vm(NX, NY, 8, 128),
            vm(3, 2, NY, 8, 128), vm(3, 2, NY, 8, 128),
            vm(NX, NY, 8, 128), vm(NX, 16, 8, 128), vm(2, NX, 8, 8, 128),
            vm(32, 128), vm(4, 4, 32, 128),
            dma(4), pltpu.SemaphoreType.DMA, pltpu.SemaphoreType.DMA,
            dma(3, 4, 2), dma(3, 4, 2), dma(3, 2), dma(3, 2), dma(3), dma(3),
            dma(4), dma(4), dma(4, 2), dma(4, 2), dma(2, 4), dma(2, 4), dma(4, 3), dma(4, 4),
        ],
        compiler_params=pltpu.CompilerParams(
            collective_id=0, has_side_effects=True, vmem_limit_bytes=58 * 2**20),
        name="filter_and_subspace",
    )(orbitals, potential, zmat)
    return out, cor, sub


def solution(mesh):
    placed = (P("orb", "dom", None, None, None), P("dom", None, None, None))
    return jax.shard_map(
        shards,
        mesh=mesh,
        in_specs=placed,
        out_specs=(P("orb", "dom", None, None, None), P(), P()),
        check_vma=False,
    )
```

```python
import math

import jax
import jax.numpy as jnp
import numpy as np
from jax import lax
from jax.experimental import pallas as pl
from jax.experimental.pallas import tpu as pltpu
from jax.sharding import PartitionSpec as P

HALO = 6
SPACING = 0.5
UPPER = 44.0
CUTOFF = 4.0
LOWEST = -1.0
NX, NY, NZ, NO = 32, 24, 128, 8
CELLS = 3145728
CHUNK = 4
ORDERS = ((0, 1, 7, 6, 4, 5, 2, 3), (0, 4, 1, 5, 2, 6, 3, 7))
FLIGHT = 3
ROWS = ((6, 12), (0, 6), (18, 6))
MESH = pl.DeviceIdType.MESH
F32, BF16 = jnp.float32, jnp.bfloat16
HIGH = lax.Precision.HIGHEST


def stencil_weights():
    return [
        2.0 * (-1.0) ** (m + 1) * math.factorial(HALO) ** 2
        / (m * m * math.factorial(HALO - m) * math.factorial(HALO + m))
        for m in range(1, HALO + 1)
    ]


WEIGHTS = stencil_weights()
KINETIC = -0.5 / SPACING**2
CENTRE = KINETIC * 3.0 * (-2.0 * sum(WEIGHTS))
HALF = (UPPER - CUTOFF) / 2.0
MIDDLE = (UPPER + CUTOFF) / 2.0
SIGMA1 = HALF / (LOWEST - MIDDLE)
SIGMA2 = 1.0 / (2.0 / SIGMA1 - SIGMA1)


def doubled(matrix):
    wide = matrix.astype(np.float32)
    hi = wide.astype(BF16)
    lo = (wide - hi.astype(np.float32)).astype(BF16)
    row = np.concatenate([hi, lo], axis=1)
    return np.concatenate([row, row], axis=0)


def z_matrices():
    own = np.zeros((NZ, NZ))
    above = np.zeros((NZ, NZ))
    below = np.zeros((NZ, NZ))
    for z in range(NZ):
        for m in range(1, HALO + 1):
            weight = KINETIC * WEIGHTS[m - 1]
            for k in (z - m, z + m):
                if 0 <= k < NZ:
                    own[k, z] = weight
                elif k >= NZ:
                    above[k - NZ, z] = weight
                else:
                    below[k + HALO, z] = weight
    upper = np.zeros((NZ, NZ))
    top = np.zeros((NZ, NZ))
    for z in range(NZ):
        g, at = z // 64, z % 64
        for m in range(1, HALO + 1):
            weight = KINETIC * WEIGHTS[m - 1]
            if at + m < 64:
                upper[z + m, z] = weight
            else:
                top[8 * g + at + m - 64, z] = weight
    return np.stack([doubled(v) for v in (own, above, below, upper, top)])


def split_wide(v):
    hi = v.astype(BF16)
    lo = (v - hi.astype(F32)).astype(BF16)
    return jnp.concatenate([hi, lo], axis=1)


def split_tall(v):
    hi = v.astype(BF16).astype(F32)
    return jnp.concatenate([hi, v - hi], axis=0).astype(BF16)


def gram(left, right):
    rows, cols = left.shape[0], right.shape[0]
    full = lax.dot_general(
        split_tall(left), split_tall(right), (((1,), (1,)), ((), ())), preferred_element_type=F32
    )
    return (full[:rows, :cols] + full[rows:, :cols]) + (full[:rows, cols:] + full[rows:, cols:])


def flat(block):
    return jnp.concatenate([block[j] for j in range(block.shape[0])], axis=1)


def kernel(orb_hbm, pot_hbm, zmat_ref, out_hbm, cor_ref, sub_ref,
           inp, pot, e0, e1, e2, zacc, potb, zf, zh, pf, sb, ocp, hp, tx, potp, zs, zp, part, ar1, ar2,
           in_sem, pot_sem, out_sem,
           y_ss, y_rs, x_ss, x_rs, z_ss, z_rs, c_ss, c_rs, g_ss, g_rs,
           ty_ss, ty_rs, tx_ss, tx_rs, zp_ss, zp_rs, a1_ss, a1_rs, a2_ss, a2_rs):
    d = lax.axis_index("dom")
    o = lax.axis_index("orb")
    bx, by, bz = d // 8, (d // 2) % 4, d % 2
    chip, core = o // 2, o % 2
    px, pzl = d % 4, (d // 4) % 2
    other_core = (d, o + 1 - 2 * core)
    other_chip = (d, (o + 2) % 4)
    column = lambda i: ((d + 4 * (i // 4)) % 8 + 8 * bx, (o + i) % 4)
    plane = lambda i: (((bx + i // 4) % 4) * 8 + 4 * pzl + (px + i) % 4, o)
    columns = [column(i) for i in range(1, 8)]
    planes = [plane(i) for i in range(1, 16)]
    crossed = (d + 1 - 2 * bz, (o + 2) % 4)
    lower = {"x": (d - 8, o), "y": (d - 2, o)}
    upper = {"x": (d + 8, o), "y": (d + 2, o)}
    has_lower = {"x": bx > 0, "y": by > 0}
    has_upper = {"x": bx < 3, "y": by < 3}
    is_a, is_b = chip == 0, chip == 1

    def when(cond, fn):
        if cond is None:
            fn()
        else:
            pl.when(cond)(lambda: fn() and None)

    loads = [
        pltpu.make_async_copy(
            orb_hbm.at[:, 0, pl.ds(8 * k, 8)], inp.at[:, pl.ds(8 * k, 8)], in_sem.at[k])
        for k in range(4)
    ]
    for k in (0, 3, 1, 2):
        loads[k].start()
    pot_load = pltpu.make_async_copy(pot_hbm.at[0], pot, pot_sem)
    pot_load.start()

    barrier = pltpu.get_barrier_semaphore()
    for dev in columns + planes:
        pl.semaphore_signal(barrier, inc=1, device_id=dev, device_id_type=MESH)

    @pl.when(by == 1)
    def _():
        pl.semaphore_signal(barrier, inc=1, device_id=upper["y"], device_id_type=MESH)

    @pl.when(by == 2)
    def _():
        pl.semaphore_signal(barrier, inc=1, device_id=lower["y"], device_id_type=MESH)

    crosses = (is_a & (bz == 1)) | (is_b & (bz == 0))

    @pl.when(crosses)
    def _():
        pl.semaphore_signal(barrier, inc=1, device_id=crossed, device_id_type=MESH)

    for buf in (e0, e1):
        @pl.when(bx == 0)
        def _(buf=buf):
            buf[0:HALO] = jnp.zeros((HALO, NY + 12, 8, 128), F32)

        @pl.when(bx == 3)
        def _(buf=buf):
            buf[NX + HALO:] = jnp.zeros((HALO, NY + 12, 8, 128), F32)

        @pl.when(by == 0)
        def _(buf=buf):
            @pl.loop(0, NX)
            def _(x):
                buf[HALO + x, 0:HALO] = jnp.zeros((HALO, 8, 128), F32)

        @pl.when(by == 3)
        def _(buf=buf):
            @pl.loop(0, NX)
            def _(x):
                buf[HALO + x, NY + HALO:] = jnp.zeros((HALO, 8, 128), F32)

    @pl.when(bx == 3)
    def _():
        tx[...] = jnp.zeros_like(tx)

    @pl.when(by == 3)
    def _():
        @pl.loop(0, 16)
        def _(x):
            for s in (0, 1):
                pf[s, x, NY:] = jnp.zeros((HALO, 8, 128), F32)

    @pl.when(is_b & (bz == 1))
    def _():
        zp[...] = jnp.zeros_like(zp)

    pl.semaphore_wait(barrier, 22 + jnp.where((by == 1) | (by == 2), 1, 0) + jnp.where(crosses, 1, 0))

    def y_copy(stage, buf, k, side):
        rows = pl.ds(HALO + CHUNK * k, CHUNK)
        src, dst = ((HALO, NY + HALO), (NY, 0))[side]
        return pltpu.make_async_remote_copy(
            src_ref=buf.at[rows, pl.ds(src, HALO)], dst_ref=buf.at[rows, pl.ds(dst, HALO)],
            send_sem=y_ss.at[stage, k, side], recv_sem=y_rs.at[stage, k, side],
            device_id=(lower, upper)[side]["y"], device_id_type=MESH)

    def x_copy(stage, buf, side):
        src, dst = ((HALO, NX + HALO), (NX, 0))[side]
        cols = pl.ds(HALO, NY)
        return pltpu.make_async_remote_copy(
            src_ref=buf.at[pl.ds(src, HALO), cols], dst_ref=buf.at[pl.ds(dst, HALO), cols],
            send_sem=x_ss.at[stage, side], recv_sem=x_rs.at[stage, side],
            device_id=(lower, upper)[side]["x"], device_id_type=MESH)

    def z_copies(stage, part):
        return [
            pltpu.make_async_remote_copy(
                src_ref=zf.at[stage, :, pl.ds(*ROWS[r])], dst_ref=zh.at[stage, :, pl.ds(*ROWS[r])],
                send_sem=z_ss.at[stage, r], recv_sem=z_rs.at[stage, r],
                device_id=(d + 1 - 2 * bz, o), device_id_type=MESH)
            for r in ((0,), (1, 2))[part]
        ]

    def sends(axis, side):
        return (has_lower, has_upper)[side][axis]

    def receives(axis, side):
        return (has_upper, has_lower)[side][axis]

    queue = [(n, buf, k) for n, buf in ((0, e0), (1, e1)) for k in ORDERS[n]]
    sent = []

    def pump(last):
        while len(sent) <= min(last, len(queue) - 1):
            q = len(sent)
            if q >= FLIGHT:
                for side in (0, 1):
                    when(sends("y", side), lambda: y_copy(*queue[q - FLIGHT], side).wait_send())
            for side in (0, 1):
                when(sends("y", side), lambda: y_copy(*queue[q], side).start())
            sent.append(q)

    def wait_y(q):
        for side in (0, 1):
            when(receives("y", side), lambda: y_copy(*queue[q], side).wait_recv())

    def send_x(stage, buf, side):
        when(sends("x", side), lambda: x_copy(stage, buf, side).start())

    def wait_x(stage, buf):
        for side in (0, 1):
            when(receives("x", side), lambda: x_copy(stage, buf, side).wait_recv())

    lane = lax.broadcasted_iota(jnp.int32, (8, 128), 1)

    def pack_z(stage, buf, part):
        first = jnp.where(bz == 0, NZ - HALO, 0)
        shifts = [lax.rem(8 * x + 128 - first, 128) for x in range(16)]

        def rows(half, y, n):
            for j in range(n):
                total = None
                for x in range(16):
                    moved = pltpu.roll(buf[HALO + 16 * half + x, HALO + y + j], shifts[x], axis=1)
                    total = moved if total is None else jnp.where(lane // 8 == x, moved, total)
                zf[stage, half, y + j] = total

        @pl.loop(0, 4)
        def _(t):
            if part == 0:
                rows(t // 2, 6 + 6 * (t % 2), 6)
            else:
                rows(t // 2, 18 * (t % 2), 6)
        for copy in z_copies(stage, part):
            copy.start()

    def pack_top(first, dst, slot):
        @pl.loop(0, 2)
        def _(half):
            @pl.loop(0, NY // 4)
            def _(t):
                for j in range(4):
                    total = None
                    for i in range(16):
                        moved = pltpu.roll(
                            e2[HALO + 8 * half + i // 2 + 16 * (i % 2), HALO + 4 * t + j],
                            (8 * i + 128 - first) % 128, axis=1)
                        total = moved if total is None else jnp.where(lane // 8 == i, moved, total)
                    dst[slot, half, 4 * t + j] = total

    def z_own(buf):
        @pl.loop(0, NX // 4)
        def _(t):
            v = buf[pl.ds(HALO + 4 * t, 4), pl.ds(HALO, NY)].reshape(4 * NY * 8, 128)
            r = jnp.dot(split_wide(v), zmat_ref[0], preferred_element_type=F32)
            zacc[pl.ds(4 * t, 4)] = (r[:, :128] + r[:, 128:]).reshape(4, NY, 8, 128)

    def z_halo(stage, part):
        for copy in z_copies(stage, part):
            copy.wait_recv()

        @pl.loop(0, NX // 4)
        def _(t):
            parts = []
            for j in range(4):
                x = 4 * t + j
                packed = [zh[stage, x // 16, pl.ds(*ROWS[r])].reshape(ROWS[r][1] * 8, 128)
                          for r in ((0,), (1, 2))[part]]
                packed = jnp.concatenate(packed, axis=0) if part else packed[0]
                parts.append(pltpu.roll(packed, lax.rem(128 - 8 * lax.rem(x, 16), 128), axis=1))
            v = jnp.concatenate(parts, axis=0)
            r = jnp.dot(split_wide(v), zmat_ref[1 + bz], preferred_element_type=F32)
            r = (r[:, :128] + r[:, 128:]).reshape(4, 12, 8, 128)
            at = pl.ds(4 * t, 4)
            if part == 0:
                zacc[at, pl.ds(6, 12)] += r
            else:
                zacc[at, pl.ds(0, 6)] += r[:, :6]
                zacc[at, pl.ds(18, 6)] += r[:, 6:]

    def rows_of(src, dst, x, y, scale, shift, prev, prev_scale):
        def at(dx, dy):
            return src[x + HALO + dx, pl.ds(y + HALO + dy, HALO)]

        total = scale * zacc[x, pl.ds(y, HALO)]
        total += (scale * potb[x, pl.ds(y, HALO)] + (scale * CENTRE + shift)) * at(0, 0)
        for m in range(1, HALO + 1):
            near = (at(m, 0) + at(-m, 0)) + (at(0, m) + at(0, -m))
            total += (scale * KINETIC * WEIGHTS[m - 1]) * near
        if prev is not None:
            total -= prev_scale * prev[x + HALO, pl.ds(y + HALO, HALO)]
        dst[x + HALO, pl.ds(y + HALO, HALO)] = total

    def stage_rows(lo, hi, ys_, *args):
        @pl.loop(lo, hi)
        def _(x):
            for y in ys_:
                rows_of(args[0], args[1], x, y, *args[2:])

    def interior(n, src, *args):
        z_own(src)
        pump(8 * n + 4 - n)
        z_halo(n, 0)
        stage_rows(HALO, NX - HALO, (6, 12), src, *args)
        pump(8 * n + 5 - 2 * n)
        wait_x(n, src)
        stage_rows(0, HALO, (6, 12), src, *args)
        stage_rows(NX - HALO, NX, (6, 12), src, *args)

    def faces(n, *args):
        for j, k in enumerate(ORDERS[n]):
            wait_y(8 * n + j)
            stage_rows(CHUNK * k, CHUNK * k + CHUNK, (0, 18), *args)
            pump(8 * n + j + FLIGHT)
            yield j

    flat_in = inp.reshape(NO * NX * NY, 128)
    for i, k in enumerate((0, 3, 1, 2)):
        loads[k].wait()

        @pl.loop(8 * k, 8 * k + 8)
        def _(x):
            for y in range(NY):
                e0[HALO + x, HALO + y] = flat_in[pl.ds(x * NY + y, 8, stride=NX * NY), :]
        if i < 2:
            pump(i + 1)
            send_x(0, e0, i)
    pack_z(0, e0, 0)
    pack_z(0, e0, 1)
    pump(3)
    pot_load.wait()

    @pl.loop(0, NX)
    def _(x):
        for y in range(NY):
            potb[x, y] = jnp.broadcast_to(pot[x, pl.ds(y, 1)], (8, 128))

    first = (e0, e1, SIGMA1 / HALF, -SIGMA1 / HALF * MIDDLE, None, 0.0)
    interior(0, *first)
    z_halo(0, 1)
    pack_z(1, e1, 0)

    @pl.loop(0, 16)
    def _(x):
        for y in range(NY):
            one, two = potb[x, y], potb[16 + x, y]
            low = jnp.where(lane < 64, one, pltpu.roll(two, 64, axis=1))
            high = jnp.where(lane < 64, pltpu.roll(one, 64, axis=1), two)
            potp[x, y] = jnp.where(is_a, low, high)

    for j in faces(0, *first):
        if j == 1:
            send_x(1, e1, 0)
        if j == 3:
            send_x(1, e1, 1)
    pack_z(1, e1, 1)

    def pack_rows(lo, hi, rows):
        @pl.loop(lo, hi)
        def _(x):
            for y, n in rows:
                for j in range(y, y + n):
                    one, two = e2[HALO + x, HALO + j], e2[HALO + 16 + x, HALO + j]
                    low = jnp.where(lane < 64, one, pltpu.roll(two, 64, axis=1))
                    high = jnp.where(lane < 64, pltpu.roll(one, 64, axis=1), two)
                    pf[0, x, j] = jnp.where(is_a, low, high)
                    sb[x, j] = jnp.where(is_a, high, low)

    def piece(c, r):
        return pl.ds(4 * c, 4), pl.ds(*ROWS[r])

    def chip_copy(c, r):
        p = piece(c, r)
        return pltpu.make_async_remote_copy(
            src_ref=sb.at[p], dst_ref=pf.at[(1,) + p], send_sem=g_ss.at[c, r], recv_sem=g_rs.at[c, r],
            device_id=other_chip, device_id_type=MESH)

    def core_copy(s, c, r):
        p = (s,) + piece(c, r)
        return pltpu.make_async_remote_copy(
            src_ref=pf.at[p], dst_ref=ocp.at[p], send_sem=c_ss.at[s, c, r], recv_sem=c_rs.at[s, c, r],
            device_id=other_core, device_id_type=MESH)

    def ty_copy(s, c):
        xs = pl.ds(4 * c, 4)
        return pltpu.make_async_remote_copy(
            src_ref=pf.at[s, xs, pl.ds(0, HALO)], dst_ref=pf.at[s, xs, pl.ds(NY, HALO)],
            send_sem=ty_ss.at[s, c], recv_sem=ty_rs.at[s, c], device_id=lower["y"], device_id_type=MESH)

    def tx_copy(s, r):
        rows = pl.ds(*ROWS[r])
        return pltpu.make_async_remote_copy(
            src_ref=pf.at[s, pl.ds(0, HALO), rows], dst_ref=tx.at[s, :, rows],
            send_sem=tx_ss.at[s, r], recv_sem=tx_rs.at[s, r], device_id=lower["x"], device_id_type=MESH)

    def zp_copy(src, slot, dev):
        return pltpu.make_async_remote_copy(
            src_ref=zs.at[src], dst_ref=zp.at[slot], send_sem=zp_ss.at[src], recv_sem=zp_rs.at[slot],
            device_id=dev, device_id_type=MESH)

    def down(s, c, r):
        if r == 1:
            when(has_lower["y"], lambda: ty_copy(s, c).start())
        if c == 1:
            when(has_lower["x"], lambda: tx_copy(s, r).start())
        core_copy(s, c, r).start()

    def arrived(c, r):
        chip_copy(c, r).wait_recv()
        down(1, c, r)

    s2 = 2.0 * SIGMA2 / HALF
    second = (e1, e2, s2, -s2 * MIDDLE, e0, SIGMA1 * SIGMA2)
    interior(1, *second)
    pack_rows(0, 16, ROWS[:1])
    for c in range(4):
        chip_copy(c, 0).start()
    for c in range(4):
        down(0, c, 0)
    z_halo(1, 1)

    for j in faces(1, *second):
        if j % 2:
            c = j // 2
            pack_rows(4 * c, 4 * c + 4, ROWS[1:])
            for r in (1, 2):
                chip_copy(c, r).start()
            for r in (1, 2):
                down(0, c, r)
        if j == 4:
            arrived(0, 0)
            arrived(1, 0)
        if j == 6:
            arrived(2, 0)
            arrived(3, 0)
            arrived(0, 1)
            arrived(0, 2)
        if j == 7:
            arrived(1, 1)
            arrived(1, 2)

    @pl.when(is_a)
    def _():
        pack_top(64, zp, 0)

        @pl.when(bz == 1)
        def _():
            pack_top(0, zs, 1)
            zp_copy(1, 1, crossed).start()

    @pl.when(is_b)
    def _():
        pack_top(64, zs, 0)
        zp_copy(0, 1, other_chip).start()

        @pl.when(bz == 1)
        def _():
            pack_top(0, zs, 1)
            zp_copy(1, 0, (d - 1, o)).start()

    for c in (2, 3):
        for r in (1, 2):
            arrived(c, r)

    @pl.loop(0, NX)
    def _(x):
        for orb in range(NO):
            inp[orb, x] = e2[HALO + x, pl.ds(HALO, NY), orb]
    out_copy = pltpu.make_async_copy(inp, out_hbm.at[:, 0], out_sem)
    out_copy.start()

    def z_upper(s):
        @pl.loop(0, 4)
        def _(t):
            v = pf[s, pl.ds(4 * t, 4), pl.ds(0, NY)].reshape(4 * NY * 8, 128)
            parts = []
            for j in range(4):
                x = 4 * t + j
                packed = zp[s, x // 8].reshape(NY * 8, 128)
                parts.append(pltpu.roll(packed, lax.rem(128 - 16 * lax.rem(x, 8), 128), axis=1))
            r = jnp.dot(split_wide(v), zmat_ref[3], preferred_element_type=F32)
            r += jnp.dot(split_wide(jnp.concatenate(parts, axis=0)), zmat_ref[4], preferred_element_type=F32)
            zacc[pl.ds(16 * s + 4 * t, 4)] = (r[:, :128] + r[:, 128:]).reshape(4, NY, 8, 128)

    def shift_x(s):
        @pl.loop(0, HALO)
        def _(x):
            for y in range(NY):
                both = jnp.where(lane < 64, tx[s, x, y], pf[s, x, y])
                pf[s, 16 + x, y] = pltpu.roll(both, 64, axis=1)

    def half_rows(s, ys_):
        @pl.loop(0, 16)
        def _(x):
            for y in ys_:
                total = zacc[16 * s + x, pl.ds(y, HALO)]
                total += (0.5 * CENTRE + 0.5 * potp[x, pl.ds(y, HALO)]) * pf[s, x, pl.ds(y, HALO)]
                for m in range(1, HALO + 1):
                    near = pf[s, x + m, pl.ds(y, HALO)] + pf[s, x, pl.ds(y + m, HALO)]
                    total += (KINETIC * WEIGHTS[m - 1]) * near
                hp[s, x, pl.ds(y, HALO)] = total

    @pl.when(is_a)
    def _():
        zp_copy(0, 1, other_chip).wait_recv()

    @pl.when(is_b & (bz == 0))
    def _():
        zp_copy(1, 0, other_chip).wait_recv()
        zp_copy(1, 1, other_chip).wait_recv()

    for s in (0, 1):
        z_upper(s)
        for r in range(3):
            when(has_upper["x"], lambda: tx_copy(s, r).wait_recv())
        shift_x(s)
        half_rows(s, (0, 6, 12))
        for c in range(4):
            when(has_upper["y"], lambda: ty_copy(s, c).wait_recv())
        half_rows(s, (18,))

    for s in (0, 1):
        for c in range(4):
            for r in range(3):
                core_copy(s, c, r).wait_recv()

    def grams(x, total):
        mine = [flat(pf[s, x, pl.ds(0, NY)]) for s in (0, 1)]
        left = jnp.concatenate(mine + [flat(ocp[s, x]) for s in (0, 1)], axis=0)
        right = jnp.concatenate(mine + [flat(hp[s, x]) for s in (0, 1)], axis=0)
        return total + gram(left, right)

    def place(block, starts):
        n = block.shape[1]
        r = lax.broadcasted_iota(jnp.int32, (n, 128), 0)
        c = lax.broadcasted_iota(jnp.int32, (n, 128), 1)
        chosen = jnp.zeros((n, 128), jnp.bool_)
        for j, s in enumerate(starts):
            chosen = chosen | ((r // 8 == j) & (c == s + r % 8))
        return jnp.dot(block, chosen.astype(F32), precision=HIGH, preferred_element_type=F32)

    o_core = o + 1 - 2 * core
    o_chip = (o + 2) % 4
    placed = place(lax.fori_loop(0, 16, grams, jnp.zeros((32, 32), F32)),
                   (8 * o, 8 * o_chip, 32 + 8 * o, 32 + 8 * o_chip))
    for j, orbital in enumerate((o, o_chip, o_core, o_core + 2 - 4 * chip)):
        part[pl.ds(pl.multiple_of(8 * orbital, 8), 8), :] = placed[8 * j:8 * j + 8]

    def reduce(block, ar, ss, rs, mine, source, partners):
        ar[mine] = block
        copies = []
        for i, dev in enumerate(partners):
            copies.append(pltpu.make_async_remote_copy(
                src_ref=ar.at[mine], dst_ref=ar.at[mine], send_sem=ss.at[i], recv_sem=rs.at[mine],
                device_id=dev, device_id_type=MESH))
            copies[-1].start()
        for i, dev in enumerate(partners):
            at = source(i + 1)
            pltpu.make_async_remote_copy(
                src_ref=ar.at[at], dst_ref=ar.at[at], send_sem=ss.at[i], recv_sem=rs.at[at],
                device_id=dev, device_id_type=MESH).wait_recv()
        total = ar[0]
        for i in range(1, len(partners) + 1):
            total += ar[i]
        for c in copies:
            c.wait_send()
        return total

    folded = part[0:16, :] + pltpu.roll(part[16:32, :], 64, axis=1)
    folded = reduce(folded, ar1, a1_ss, a1_rs, 4 * pzl + o,
                    lambda i: 4 * ((pzl + i // 4) % 2) + (o + i) % 4, columns)
    folded = reduce(folded, ar2, a2_ss, a2_rs, 4 * bx + px,
                    lambda i: 4 * ((bx + i // 4) % 4) + (px + i) % 4, planes)
    part[0:16, :] = folded
    part[16:32, :] = pltpu.roll(folded, 64, axis=1)

    square = part[...]
    r = lax.broadcasted_iota(jnp.int32, (32, 32), 0)
    c = lax.broadcasted_iota(jnp.int32, (32, 32), 1)
    eye = (r == c).astype(F32)
    cor_ref[...] = square[:, 0:32] * (1.0 / CELLS)
    m = square[:, 32:64]
    t = lax.dot_general(m, eye, (((0,), (0,)), ((), ())), precision=HIGH, preferred_element_type=F32)
    sub_ref[...] = (m + t) * (1.0 / (CELLS * HALF))

    out_copy.wait()
    for q in range(len(queue) - FLIGHT, len(queue)):
        for side in (0, 1):
            when(sends("y", side), lambda: y_copy(*queue[q], side).wait_send())
    for n, buf in ((0, e0), (1, e1)):
        for side in (0, 1):
            when(sends("x", side), lambda: x_copy(n, buf, side).wait_send())
        for part_ in (0, 1):
            for copy in z_copies(n, part_):
                copy.wait_send()
    for c in range(4):
        for r in range(3):
            chip_copy(c, r).wait_send()
            for s in (0, 1):
                core_copy(s, c, r).wait_send()
        for s in (0, 1):
            when(has_lower["y"], lambda: ty_copy(s, c).wait_send())
    for s in (0, 1):
        for r in range(3):
            when(has_lower["x"], lambda: tx_copy(s, r).wait_send())
    when(is_b, lambda: zp_copy(0, 1, other_chip).wait_send())
    when(bz == 1, lambda: zp_copy(1, 1, other_chip).wait_send())


def shards(orbitals, potential):
    zmat = jnp.asarray(z_matrices())
    field = (NX + 12, NY + 12, 8, 128)
    vm = lambda *shape: pltpu.VMEM(shape, F32)
    dma = lambda *shape: pltpu.SemaphoreType.DMA(shape)
    out, cor, sub = pl.pallas_call(
        kernel,
        out_shape=(
            jax.ShapeDtypeStruct((NO, 1, NX, NY, NZ), F32),
            jax.ShapeDtypeStruct((32, 32), F32),
            jax.ShapeDtypeStruct((32, 32), F32),
        ),
        in_specs=[pl.BlockSpec(memory_space=pl.ANY)] * 2 + [pl.BlockSpec(memory_space=pltpu.VMEM)],
        out_specs=(pl.BlockSpec(memory_space=pl.ANY),) + (pl.BlockSpec(memory_space=pltpu.VMEM),) * 2,
        scratch_shapes=[
            vm(NO, NX, NY, NZ), vm(NX, NY, NZ), vm(*field), vm(*field), vm(*field),
            vm(NX, NY, 8, 128), vm(NX, NY, 8, 128),
            vm(2, 2, NY, 8, 128), vm(2, 2, NY, 8, 128),
            vm(2, 16 + HALO, NY + HALO, 8, 128), vm(16, NY, 8, 128), vm(2, 16, NY, 8, 128),
            vm(2, 16, NY, 8, 128), vm(2, HALO, NY, 8, 128), vm(16, NY, 8, 128),
            vm(2, 2, NY, 8, 128), vm(2, 2, NY, 8, 128),
            vm(32, 128), vm(8, 16, 128), vm(16, 16, 128),
            dma(4), pltpu.SemaphoreType.DMA, pltpu.SemaphoreType.DMA,
            dma(2, 8, 2), dma(2, 8, 2), dma(2, 2), dma(2, 2), dma(2, 3), dma(2, 3),
            dma(2, 4, 3), dma(2, 4, 3), dma(4, 3), dma(4, 3),
            dma(2, 4), dma(2, 4), dma(2, 3), dma(2, 3), dma(2), dma(2),
            dma(7), dma(8), dma(15), dma(16),
        ],
        compiler_params=pltpu.CompilerParams(
            collective_id=0, has_side_effects=True, vmem_limit_bytes=58 * 2**20),
        name="filter_and_subspace",
    )(orbitals, potential, zmat)
    return out, cor, sub


def solution(mesh):
    placed = (P("orb", "dom", None, None, None), P("dom", None, None, None))
    return jax.shard_map(
        shards,
        mesh=mesh,
        in_specs=placed,
        out_specs=(P("orb", "dom", None, None, None), P(), P()),
        check_vma=False,
    )
```

```python
import math

import jax
import jax.numpy as jnp
import numpy as np
from jax import lax
from jax.experimental import pallas as pl
from jax.experimental.pallas import tpu as pltpu
from jax.sharding import PartitionSpec as P

HALO = 6
SPACING = 0.5
UPPER = 44.0
CUTOFF = 4.0
LOWEST = -1.0
NX, NY, NZ, NO = 32, 24, 128, 8
CELLS = 3145728
CHUNK = 4
ORDERS = ((0, 1, 7, 6, 4, 5, 2, 3), (0, 4, 1, 5, 2, 6, 3, 7))
FLIGHT = 3
ROWS = ((6, 12), (0, 6), (18, 6))
MESH = pl.DeviceIdType.MESH
F32, BF16 = jnp.float32, jnp.bfloat16
HIGH = lax.Precision.HIGHEST


def stencil_weights():
    return [
        2.0 * (-1.0) ** (m + 1) * math.factorial(HALO) ** 2
        / (m * m * math.factorial(HALO - m) * math.factorial(HALO + m))
        for m in range(1, HALO + 1)
    ]


WEIGHTS = stencil_weights()
KINETIC = -0.5 / SPACING**2
CENTRE = KINETIC * 3.0 * (-2.0 * sum(WEIGHTS))
HALF = (UPPER - CUTOFF) / 2.0
MIDDLE = (UPPER + CUTOFF) / 2.0
SIGMA1 = HALF / (LOWEST - MIDDLE)
SIGMA2 = 1.0 / (2.0 / SIGMA1 - SIGMA1)


def doubled(matrix):
    wide = matrix.astype(np.float32)
    hi = wide.astype(BF16)
    lo = (wide - hi.astype(np.float32)).astype(BF16)
    row = np.concatenate([hi, lo], axis=1)
    return np.concatenate([row, row], axis=0)


def z_matrices():
    own = np.zeros((NZ, NZ))
    above = np.zeros((NZ, NZ))
    below = np.zeros((NZ, NZ))
    for z in range(NZ):
        for m in range(1, HALO + 1):
            weight = KINETIC * WEIGHTS[m - 1]
            for k in (z - m, z + m):
                if 0 <= k < NZ:
                    own[k, z] = weight
                elif k >= NZ:
                    above[k - NZ, z] = weight
                else:
                    below[k + HALO, z] = weight
    upper = np.zeros((NZ, NZ))
    top = np.zeros((NZ, NZ))
    for z in range(NZ):
        g, at = z // 64, z % 64
        for m in range(1, HALO + 1):
            weight = KINETIC * WEIGHTS[m - 1]
            if at + m < 64:
                upper[z + m, z] = weight
            else:
                top[8 * g + at + m - 64, z] = weight
    return np.stack([doubled(v) for v in (own, above, below, upper, top)])


def split_wide(v):
    hi = v.astype(BF16)
    lo = (v - hi.astype(F32)).astype(BF16)
    return jnp.concatenate([hi, lo], axis=1)


def split_tall(v):
    hi = v.astype(BF16).astype(F32)
    return jnp.concatenate([hi, v - hi], axis=0).astype(BF16)


def gram(left, right):
    rows, cols = left.shape[0], right.shape[0]
    full = lax.dot_general(
        split_tall(left), split_tall(right), (((1,), (1,)), ((), ())), preferred_element_type=F32
    )
    return (full[:rows, :cols] + full[rows:, :cols]) + (full[:rows, cols:] + full[rows:, cols:])


def flat(block):
    return jnp.concatenate([block[j] for j in range(block.shape[0])], axis=1)


def kernel(orb_hbm, pot_hbm, zmat_ref, out_hbm, cor_ref, sub_ref,
           inp, pot, e0, e1, e2, zacc, potb, zf, zh, rl, pf, sb, ocp, hp, tp, tx, potp, zs, zp, part, ar1, ar2,
           in_sem, pot_sem, out_sem,
           y_ss, y_rs, r_ss, r_rs, p_ss, x_ss, x_rs, z_ss, z_rs, c_ss, c_rs, g_ss, g_rs,
           ty_ss, ty_rs, tx_ss, tx_rs, zp_ss, zp_rs, a1_ss, a1_rs, a2_ss, a2_rs):
    d = lax.axis_index("dom")
    o = lax.axis_index("orb")
    bx, by, bz = d // 8, (d // 2) % 4, d % 2
    chip, core = o // 2, o % 2
    px, pzl = d % 4, (d // 4) % 2
    other_core = (d, o + 1 - 2 * core)
    other_chip = (d, (o + 2) % 4)
    column = lambda i: ((d + 4 * (i // 4)) % 8 + 8 * bx, (o + i) % 4)
    plane = lambda i: (((bx + i // 4) % 4) * 8 + 4 * pzl + (px + i) % 4, o)
    columns = [column(i) for i in range(1, 8)]
    planes = [plane(i) for i in range(1, 16)]
    zl = (d + 4 - 8 * pzl, o)
    crossed = (d + 1 - 2 * bz, (o + 2) % 4)
    lower = {"x": (d - 8, o), "y": (d - 2, o)}
    upper = {"x": (d + 8, o), "y": (d + 2, o)}
    has_lower = {"x": bx > 0, "y": by > 0}
    has_upper = {"x": bx < 3, "y": by < 3}
    is_a, is_b = chip == 0, chip == 1

    def when(cond, fn):
        if cond is None:
            fn()
        else:
            pl.when(cond)(lambda: fn() and None)

    loads = [
        pltpu.make_async_copy(
            orb_hbm.at[:, 0, pl.ds(8 * k, 8)], inp.at[:, pl.ds(8 * k, 8)], in_sem.at[k])
        for k in range(4)
    ]
    for k in (0, 3, 1, 2):
        loads[k].start()
    pot_load = pltpu.make_async_copy(pot_hbm.at[0], pot, pot_sem)
    pot_load.start()

    barrier = pltpu.get_barrier_semaphore()
    for dev in columns + planes:
        pl.semaphore_signal(barrier, inc=1, device_id=dev, device_id_type=MESH)

    @pl.when(by == 1)
    def _():
        pl.semaphore_signal(barrier, inc=1, device_id=upper["y"], device_id_type=MESH)

    @pl.when(by == 2)
    def _():
        pl.semaphore_signal(barrier, inc=1, device_id=lower["y"], device_id_type=MESH)

    crosses = (is_a & (bz == 1)) | (is_b & (bz == 0))

    @pl.when(crosses)
    def _():
        pl.semaphore_signal(barrier, inc=1, device_id=crossed, device_id_type=MESH)

    for buf in (e0, e1):
        @pl.when(bx == 0)
        def _(buf=buf):
            buf[0:HALO] = jnp.zeros((HALO, NY + 12, 8, 128), F32)

        @pl.when(bx == 3)
        def _(buf=buf):
            buf[NX + HALO:] = jnp.zeros((HALO, NY + 12, 8, 128), F32)

        @pl.when(by == 0)
        def _(buf=buf):
            @pl.loop(0, NX)
            def _(x):
                buf[HALO + x, 0:HALO] = jnp.zeros((HALO, 8, 128), F32)

        @pl.when(by == 3)
        def _(buf=buf):
            @pl.loop(0, NX)
            def _(x):
                buf[HALO + x, NY + HALO:] = jnp.zeros((HALO, 8, 128), F32)

    @pl.when(bx == 3)
    def _():
        tx[...] = jnp.zeros_like(tx)

    @pl.when(by == 3)
    def _():
        @pl.loop(0, 16)
        def _(x):
            for s in (0, 1):
                pf[s, x, NY:] = jnp.zeros((HALO, 8, 128), F32)

    @pl.when(is_b & (bz == 1))
    def _():
        zp[...] = jnp.zeros_like(zp)

    pl.semaphore_wait(barrier, 22 + jnp.where((by == 1) | (by == 2), 1, 0) + jnp.where(crosses, 1, 0))

    def y_copy(stage, buf, k, side):
        rows = pl.ds(HALO + CHUNK * k, CHUNK)
        src, dst = ((HALO, NY + HALO), (NY, 0))[side]
        return pltpu.make_async_remote_copy(
            src_ref=buf.at[rows, pl.ds(src, HALO)], dst_ref=buf.at[rows, pl.ds(dst, HALO)],
            send_sem=y_ss.at[stage, k, side], recv_sem=y_rs.at[stage, k, side],
            device_id=(lower, upper)[side]["y"], device_id_type=MESH)

    def x_copy(stage, buf, side):
        src, dst = ((HALO, NX + HALO), (NX, 0))[side]
        cols = pl.ds(HALO, NY)
        return pltpu.make_async_remote_copy(
            src_ref=buf.at[pl.ds(src, HALO), cols], dst_ref=buf.at[pl.ds(dst, HALO), cols],
            send_sem=x_ss.at[stage, side], recv_sem=x_rs.at[stage, side],
            device_id=(lower, upper)[side]["x"], device_id_type=MESH)

    def z_copies(stage, part):
        return [
            pltpu.make_async_remote_copy(
                src_ref=zf.at[stage, :, pl.ds(*ROWS[r])], dst_ref=zh.at[stage, :, pl.ds(*ROWS[r])],
                send_sem=z_ss.at[stage, r], recv_sem=z_rs.at[stage, r],
                device_id=(d + 1 - 2 * bz, o), device_id_type=MESH)
            for r in ((0,), (1, 2))[part]
        ]

    def sends(axis, side):
        return (has_lower, has_upper)[side][axis]

    def receives(axis, side):
        return (has_upper, has_lower)[side][axis]

    queue = [(n, buf, k) for n, buf in ((0, e0), (1, e1)) for k in ORDERS[n]]
    sent, passed = [], []

    def direct(q, side):
        if q % 2 == 0:
            return sends("y", side)
        return ((by == 1) | (by == 3), (by == 0) | (by == 2))[side]

    def relayed(q, side):
        n, buf, k = queue[q]
        return pltpu.make_async_remote_copy(
            src_ref=buf.at[pl.ds(HALO + CHUNK * k, CHUNK), pl.ds((HALO, NY)[side], HALO)],
            dst_ref=rl.at[n, q % 8 // 2], send_sem=r_ss.at[n, q % 8 // 2], recv_sem=r_rs.at[n, q % 8 // 2],
            device_id=zl, device_id_type=MESH)

    def passing(q, side):
        n, buf, k = queue[q]
        return pltpu.make_async_remote_copy(
            src_ref=rl.at[n, q % 8 // 2],
            dst_ref=buf.at[pl.ds(HALO + CHUNK * k, CHUNK), pl.ds((NY + HALO, 0)[side], HALO)],
            send_sem=p_ss.at[n, q % 8 // 2], recv_sem=y_rs.at[n, k, side],
            device_id=(upper, lower)[side]["y"], device_id_type=MESH)

    def each_send(q, act):
        for side in (0, 1):
            when(direct(q, side), lambda: act(y_copy(*queue[q], side)))
            if q % 2:
                when(by == 2 - side, lambda: act(relayed(q, side)))

    def pass_on(q):
        for side in (0, 1):
            def go():
                relayed(q, side).wait_recv()
                passing(q, side).start()
            when(by == 3 * side, go)

    def pump(last):
        while len(sent) <= min(last, len(queue) - 1):
            q = len(sent)
            if q >= FLIGHT:
                each_send(q - FLIGHT, lambda c: c.wait_send())
            each_send(q, lambda c: c.start())
            sent.append(q)
        while 2 * len(passed) + 1 < min(last, len(queue)):
            q = 2 * len(passed) + 1
            pass_on(q)
            passed.append(q)

    def wait_y(q):
        for side in (0, 1):
            when(receives("y", side), lambda: y_copy(*queue[q], side).wait_recv())

    def send_x(stage, buf, side):
        when(sends("x", side), lambda: x_copy(stage, buf, side).start())

    def wait_x(stage, buf):
        for side in (0, 1):
            when(receives("x", side), lambda: x_copy(stage, buf, side).wait_recv())

    lane = lax.broadcasted_iota(jnp.int32, (8, 128), 1)

    def pack_z(stage, buf, part):
        first = jnp.where(bz == 0, NZ - HALO, 0)
        shifts = [lax.rem(8 * x + 128 - first, 128) for x in range(16)]

        def rows(half, y, n):
            for j in range(n):
                total = None
                for x in range(16):
                    moved = pltpu.roll(buf[HALO + 16 * half + x, HALO + y + j], shifts[x], axis=1)
                    total = moved if total is None else jnp.where(lane // 8 == x, moved, total)
                zf[stage, half, y + j] = total

        @pl.loop(0, 4)
        def _(t):
            if part == 0:
                rows(t // 2, 6 + 6 * (t % 2), 6)
            else:
                rows(t // 2, 18 * (t % 2), 6)
        for copy in z_copies(stage, part):
            copy.start()

    def pack_top(first, dst, slot):
        @pl.loop(0, 2)
        def _(half):
            @pl.loop(0, NY // 4)
            def _(t):
                for j in range(4):
                    total = None
                    for i in range(16):
                        moved = pltpu.roll(
                            e2[HALO + 8 * half + i // 2 + 16 * (i % 2), HALO + 4 * t + j],
                            (8 * i + 128 - first) % 128, axis=1)
                        total = moved if total is None else jnp.where(lane // 8 == i, moved, total)
                    dst[slot, half, 4 * t + j] = total

    def z_own(buf):
        @pl.loop(0, NX // 4)
        def _(t):
            v = buf[pl.ds(HALO + 4 * t, 4), pl.ds(HALO, NY)].reshape(4 * NY * 8, 128)
            r = jnp.dot(split_wide(v), zmat_ref[0], preferred_element_type=F32)
            zacc[pl.ds(4 * t, 4)] = (r[:, :128] + r[:, 128:]).reshape(4, NY, 8, 128)

    def z_halo(stage, part):
        for copy in z_copies(stage, part):
            copy.wait_recv()

        @pl.loop(0, NX // 4)
        def _(t):
            parts = []
            for j in range(4):
                x = 4 * t + j
                packed = [zh[stage, x // 16, pl.ds(*ROWS[r])].reshape(ROWS[r][1] * 8, 128)
                          for r in ((0,), (1, 2))[part]]
                packed = jnp.concatenate(packed, axis=0) if part else packed[0]
                parts.append(pltpu.roll(packed, lax.rem(128 - 8 * lax.rem(x, 16), 128), axis=1))
            v = jnp.concatenate(parts, axis=0)
            r = jnp.dot(split_wide(v), zmat_ref[1 + bz], preferred_element_type=F32)
            r = (r[:, :128] + r[:, 128:]).reshape(4, 12, 8, 128)
            at = pl.ds(4 * t, 4)
            if part == 0:
                zacc[at, pl.ds(6, 12)] += r
            else:
                zacc[at, pl.ds(0, 6)] += r[:, :6]
                zacc[at, pl.ds(18, 6)] += r[:, 6:]

    def rows_of(src, dst, x, y, scale, shift, prev, prev_scale):
        def at(dx, dy):
            return src[x + HALO + dx, pl.ds(y + HALO + dy, HALO)]

        total = scale * zacc[x, pl.ds(y, HALO)]
        total += (scale * potb[x, pl.ds(y, HALO)] + (scale * CENTRE + shift)) * at(0, 0)
        for m in range(1, HALO + 1):
            near = (at(m, 0) + at(-m, 0)) + (at(0, m) + at(0, -m))
            total += (scale * KINETIC * WEIGHTS[m - 1]) * near
        if prev is not None:
            total -= prev_scale * prev[x + HALO, pl.ds(y + HALO, HALO)]
        dst[x + HALO, pl.ds(y + HALO, HALO)] = total

    def stage_rows(lo, hi, ys_, *args):
        @pl.loop(lo, hi)
        def _(x):
            for y in ys_:
                rows_of(args[0], args[1], x, y, *args[2:])

    def interior(n, src, *args):
        z_own(src)
        pump(8 * n + 4 - n)
        z_halo(n, 0)
        stage_rows(HALO, NX - HALO, (6, 12), src, *args)
        pump(8 * n + 5 - 2 * n)
        wait_x(n, src)
        stage_rows(0, HALO, (6, 12), src, *args)
        stage_rows(NX - HALO, NX, (6, 12), src, *args)

    def faces(n, *args):
        for j, k in enumerate(ORDERS[n]):
            wait_y(8 * n + j)
            stage_rows(CHUNK * k, CHUNK * k + CHUNK, (0, 18), *args)
            pump(8 * n + j + FLIGHT)
            yield j

    flat_in = inp.reshape(NO * NX * NY, 128)
    for i, k in enumerate((0, 3, 1, 2)):
        loads[k].wait()

        @pl.loop(8 * k, 8 * k + 8)
        def _(x):
            for y in range(NY):
                e0[HALO + x, HALO + y] = flat_in[pl.ds(x * NY + y, 8, stride=NX * NY), :]
        if i < 2:
            pump(i + 1)
            send_x(0, e0, i)
    pack_z(0, e0, 0)
    pack_z(0, e0, 1)
    pump(3)
    pot_load.wait()

    @pl.loop(0, NX)
    def _(x):
        for y in range(NY):
            potb[x, y] = jnp.broadcast_to(pot[x, pl.ds(y, 1)], (8, 128))

    first = (e0, e1, SIGMA1 / HALF, -SIGMA1 / HALF * MIDDLE, None, 0.0)
    interior(0, *first)
    z_halo(0, 1)
    pack_z(1, e1, 0)

    @pl.loop(0, 16)
    def _(x):
        for y in range(NY):
            one, two = potb[x, y], potb[16 + x, y]
            low = jnp.where(lane < 64, one, pltpu.roll(two, 64, axis=1))
            high = jnp.where(lane < 64, pltpu.roll(one, 64, axis=1), two)
            potp[x, y] = jnp.where(is_a, low, high)

    for j in faces(0, *first):
        if j == 1:
            send_x(1, e1, 0)
        if j == 3:
            send_x(1, e1, 1)
    pack_z(1, e1, 1)

    def pack_rows(lo, hi, rows):
        @pl.loop(lo, hi)
        def _(x):
            for y, n in rows:
                for j in range(y, y + n):
                    one, two = e2[HALO + x, HALO + j], e2[HALO + 16 + x, HALO + j]
                    low = jnp.where(lane < 64, one, pltpu.roll(two, 64, axis=1))
                    high = jnp.where(lane < 64, pltpu.roll(one, 64, axis=1), two)
                    pf[0, x, j] = jnp.where(is_a, low, high)
                    sb[x, j] = jnp.where(is_a, high, low)

    def piece(c, r):
        return pl.ds(4 * c, 4), pl.ds(*ROWS[r])

    def chip_copy(c, r):
        p = piece(c, r)
        return pltpu.make_async_remote_copy(
            src_ref=sb.at[p], dst_ref=pf.at[(1,) + p], send_sem=g_ss.at[c, r], recv_sem=g_rs.at[c, r],
            device_id=other_chip, device_id_type=MESH)

    def core_copy(s, c, r):
        p = (s,) + piece(c, r)
        return pltpu.make_async_remote_copy(
            src_ref=pf.at[p], dst_ref=ocp.at[p], send_sem=c_ss.at[s, c, r], recv_sem=c_rs.at[s, c, r],
            device_id=other_core, device_id_type=MESH)

    def ty_copy(s, c):
        xs = pl.ds(4 * c, 4)
        return pltpu.make_async_remote_copy(
            src_ref=pf.at[s, xs, pl.ds(0, HALO)], dst_ref=pf.at[s, xs, pl.ds(NY, HALO)],
            send_sem=ty_ss.at[s, c], recv_sem=ty_rs.at[s, c], device_id=lower["y"], device_id_type=MESH)

    PAIRS = ((6, 12), (0, 18))

    def tx_copy(s, half):
        rows = pl.ds(6 * half, 6)
        return pltpu.make_async_remote_copy(
            src_ref=tp.at[s, :, rows], dst_ref=tx.at[s, :, rows],
            send_sem=tx_ss.at[s, half], recv_sem=tx_rs.at[s, half], device_id=lower["x"], device_id_type=MESH)

    def send_tx(s, half):
        one, two = PAIRS[half]

        @pl.loop(0, HALO)
        def _(x):
            for j in range(6):
                tp[s, x, 6 * half + j] = jnp.where(
                    lane < 64, pf[s, x, one + j], pltpu.roll(pf[s, x, two + j], 64, axis=1))
        when(has_lower["x"], lambda: tx_copy(s, half).start())

    def zp_copy(src, slot, dev):
        return pltpu.make_async_remote_copy(
            src_ref=zs.at[src], dst_ref=zp.at[slot], send_sem=zp_ss.at[src], recv_sem=zp_rs.at[slot],
            device_id=dev, device_id_type=MESH)

    def down(s, c, r):
        if r == 1:
            when(has_lower["y"], lambda: ty_copy(s, c).start())
        if c == 1 and r != 1:
            send_tx(s, r // 2)
        core_copy(s, c, r).start()

    def arrived(c, r):
        chip_copy(c, r).wait_recv()
        down(1, c, r)

    s2 = 2.0 * SIGMA2 / HALF
    second = (e1, e2, s2, -s2 * MIDDLE, e0, SIGMA1 * SIGMA2)
    interior(1, *second)
    pack_rows(0, 16, ROWS[:1])
    for c in range(4):
        chip_copy(c, 0).start()
    for c in range(4):
        down(0, c, 0)
    z_halo(1, 1)

    for j in faces(1, *second):
        if j % 2:
            c = j // 2
            pack_rows(4 * c, 4 * c + 4, ROWS[1:])
            for r in (1, 2):
                chip_copy(c, r).start()
            for r in (1, 2):
                down(0, c, r)
        if j == 4:
            arrived(0, 0)
            arrived(1, 0)
        if j == 6:
            arrived(2, 0)
            arrived(3, 0)
            arrived(0, 1)
            arrived(0, 2)
        if j == 7:
            arrived(1, 1)
            arrived(1, 2)

    @pl.when(is_a)
    def _():
        pack_top(64, zp, 0)

        @pl.when(bz == 1)
        def _():
            pack_top(0, zs, 1)
            zp_copy(1, 1, crossed).start()

    @pl.when(is_b)
    def _():
        pack_top(64, zs, 0)
        zp_copy(0, 1, other_chip).start()

        @pl.when(bz == 1)
        def _():
            pack_top(0, zs, 1)
            zp_copy(1, 0, (d - 1, o)).start()

    for c in (2, 3):
        for r in (1, 2):
            arrived(c, r)

    @pl.loop(0, NX)
    def _(x):
        for orb in range(NO):
            inp[orb, x] = e2[HALO + x, pl.ds(HALO, NY), orb]
    out_copy = pltpu.make_async_copy(inp, out_hbm.at[:, 0], out_sem)
    out_copy.start()

    def z_upper(s):
        @pl.loop(0, 4)
        def _(t):
            v = pf[s, pl.ds(4 * t, 4), pl.ds(0, NY)].reshape(4 * NY * 8, 128)
            parts = []
            for j in range(4):
                x = 4 * t + j
                packed = zp[s, x // 8].reshape(NY * 8, 128)
                parts.append(pltpu.roll(packed, lax.rem(128 - 16 * lax.rem(x, 8), 128), axis=1))
            r = jnp.dot(split_wide(v), zmat_ref[3], preferred_element_type=F32)
            r += jnp.dot(split_wide(jnp.concatenate(parts, axis=0)), zmat_ref[4], preferred_element_type=F32)
            zacc[pl.ds(16 * s + 4 * t, 4)] = (r[:, :128] + r[:, 128:]).reshape(4, NY, 8, 128)

    def shift_x(s):
        @pl.loop(0, HALO)
        def _(x):
            for half, (one, two) in enumerate(PAIRS):
                for j in range(6):
                    there = tx[s, x, 6 * half + j]
                    both = jnp.where(lane < 64, there, pf[s, x, one + j])
                    pf[s, 16 + x, one + j] = pltpu.roll(both, 64, axis=1)
                    pf[s, 16 + x, two + j] = jnp.where(
                        lane < 64, pltpu.roll(pf[s, x, two + j], 64, axis=1), there)

    def half_rows(s, ys_):
        @pl.loop(0, 16)
        def _(x):
            for y in ys_:
                total = zacc[16 * s + x, pl.ds(y, HALO)]
                total += (0.5 * CENTRE + 0.5 * potp[x, pl.ds(y, HALO)]) * pf[s, x, pl.ds(y, HALO)]
                for m in range(1, HALO + 1):
                    near = pf[s, x + m, pl.ds(y, HALO)] + pf[s, x, pl.ds(y + m, HALO)]
                    total += (KINETIC * WEIGHTS[m - 1]) * near
                hp[s, x, pl.ds(y, HALO)] = total

    @pl.when(is_a)
    def _():
        zp_copy(0, 1, other_chip).wait_recv()

    @pl.when(is_b & (bz == 0))
    def _():
        zp_copy(1, 0, other_chip).wait_recv()
        zp_copy(1, 1, other_chip).wait_recv()

    for s in (0, 1):
        z_upper(s)
        for half in (0, 1):
            when(has_upper["x"], lambda: tx_copy(s, half).wait_recv())
        shift_x(s)
        half_rows(s, (0, 6, 12))

    for s in (0, 1):
        for c in range(4):
            for r in range(3):
                core_copy(s, c, r).wait_recv()

    def grams(rows):
        def body(x, total):
            mine = [flat(pf[s, x, rows]) for s in (0, 1)]
            left = jnp.concatenate(mine + [flat(ocp[s, x, rows]) for s in (0, 1)], axis=0)
            right = jnp.concatenate(mine + [flat(hp[s, x, rows]) for s in (0, 1)], axis=0)
            return total + gram(left, right)
        return body

    total = lax.fori_loop(0, 16, grams(pl.ds(0, 18)), jnp.zeros((32, 32), F32))
    for s in (0, 1):
        for c in range(4):
            when(has_upper["y"], lambda: ty_copy(s, c).wait_recv())
        half_rows(s, (18,))
    total = lax.fori_loop(0, 16, grams(pl.ds(18, 6)), total)

    def place(block, starts):
        n = block.shape[1]
        r = lax.broadcasted_iota(jnp.int32, (n, 128), 0)
        c = lax.broadcasted_iota(jnp.int32, (n, 128), 1)
        chosen = jnp.zeros((n, 128), jnp.bool_)
        for j, s in enumerate(starts):
            chosen = chosen | ((r // 8 == j) & (c == s + r % 8))
        return jnp.dot(block, chosen.astype(F32), precision=HIGH, preferred_element_type=F32)

    o_core = o + 1 - 2 * core
    o_chip = (o + 2) % 4
    placed = place(total, (8 * o, 8 * o_chip, 32 + 8 * o, 32 + 8 * o_chip))
    for j, orbital in enumerate((o, o_chip, o_core, o_core + 2 - 4 * chip)):
        part[pl.ds(pl.multiple_of(8 * orbital, 8), 8), :] = placed[8 * j:8 * j + 8]

    def reduce(block, ar, ss, rs, mine, source, partners):
        ar[mine] = block
        copies = []
        for i, dev in enumerate(partners):
            copies.append(pltpu.make_async_remote_copy(
                src_ref=ar.at[mine], dst_ref=ar.at[mine], send_sem=ss.at[i], recv_sem=rs.at[mine],
                device_id=dev, device_id_type=MESH))
            copies[-1].start()
        for i, dev in enumerate(partners):
            at = source(i + 1)
            pltpu.make_async_remote_copy(
                src_ref=ar.at[at], dst_ref=ar.at[at], send_sem=ss.at[i], recv_sem=rs.at[at],
                device_id=dev, device_id_type=MESH).wait_recv()
        total = ar[0]
        for i in range(1, len(partners) + 1):
            total += ar[i]
        for c in copies:
            c.wait_send()
        return total

    folded = part[0:16, :] + pltpu.roll(part[16:32, :], 64, axis=1)
    folded = reduce(folded, ar1, a1_ss, a1_rs, 4 * pzl + o,
                    lambda i: 4 * ((pzl + i // 4) % 2) + (o + i) % 4, columns)
    folded = reduce(folded, ar2, a2_ss, a2_rs, 4 * bx + px,
                    lambda i: 4 * ((bx + i // 4) % 4) + (px + i) % 4, planes)
    part[0:16, :] = folded
    part[16:32, :] = pltpu.roll(folded, 64, axis=1)

    square = part[...]
    r = lax.broadcasted_iota(jnp.int32, (32, 32), 0)
    c = lax.broadcasted_iota(jnp.int32, (32, 32), 1)
    eye = (r == c).astype(F32)
    cor_ref[...] = square[:, 0:32] * (1.0 / CELLS)
    m = square[:, 32:64]
    t = lax.dot_general(m, eye, (((0,), (0,)), ((), ())), precision=HIGH, preferred_element_type=F32)
    sub_ref[...] = (m + t) * (1.0 / (CELLS * HALF))

    out_copy.wait()
    for q in range(len(queue) - FLIGHT, len(queue)):
        each_send(q, lambda c: c.wait_send())
    for q in passed:
        for side in (0, 1):
            when(by == 3 * side, lambda: passing(q, side).wait_send())
    for n, buf in ((0, e0), (1, e1)):
        for side in (0, 1):
            when(sends("x", side), lambda: x_copy(n, buf, side).wait_send())
        for part_ in (0, 1):
            for copy in z_copies(n, part_):
                copy.wait_send()
    for c in range(4):
        for r in range(3):
            chip_copy(c, r).wait_send()
            for s in (0, 1):
                core_copy(s, c, r).wait_send()
        for s in (0, 1):
            when(has_lower["y"], lambda: ty_copy(s, c).wait_send())
    for s in (0, 1):
        for half in (0, 1):
            when(has_lower["x"], lambda: tx_copy(s, half).wait_send())
    when(is_b, lambda: zp_copy(0, 1, other_chip).wait_send())
    when(bz == 1, lambda: zp_copy(1, 1, other_chip).wait_send())


def shards(orbitals, potential):
    zmat = jnp.asarray(z_matrices())
    field = (NX + 12, NY + 12, 8, 128)
    vm = lambda *shape: pltpu.VMEM(shape, F32)
    dma = lambda *shape: pltpu.SemaphoreType.DMA(shape)
    out, cor, sub = pl.pallas_call(
        kernel,
        out_shape=(
            jax.ShapeDtypeStruct((NO, 1, NX, NY, NZ), F32),
            jax.ShapeDtypeStruct((32, 32), F32),
            jax.ShapeDtypeStruct((32, 32), F32),
        ),
        in_specs=[pl.BlockSpec(memory_space=pl.ANY)] * 2 + [pl.BlockSpec(memory_space=pltpu.VMEM)],
        out_specs=(pl.BlockSpec(memory_space=pl.ANY),) + (pl.BlockSpec(memory_space=pltpu.VMEM),) * 2,
        scratch_shapes=[
            vm(NO, NX, NY, NZ), vm(NX, NY, NZ), vm(*field), vm(*field), vm(*field),
            vm(NX, NY, 8, 128), vm(NX, NY, 8, 128),
            vm(2, 2, NY, 8, 128), vm(2, 2, NY, 8, 128), vm(2, 4, CHUNK, HALO, 8, 128),
            vm(2, 16 + HALO, NY + HALO, 8, 128), vm(16, NY, 8, 128), vm(2, 16, NY, 8, 128),
            vm(2, 16, NY, 8, 128), vm(2, HALO, 12, 8, 128), vm(2, HALO, 12, 8, 128), vm(16, NY, 8, 128),
            vm(2, 2, NY, 8, 128), vm(2, 2, NY, 8, 128),
            vm(32, 128), vm(8, 16, 128), vm(16, 16, 128),
            dma(4), pltpu.SemaphoreType.DMA, pltpu.SemaphoreType.DMA,
            dma(2, 8, 2), dma(2, 8, 2), dma(2, 4), dma(2, 4), dma(2, 4), dma(2, 2), dma(2, 2), dma(2, 3), dma(2, 3),
            dma(2, 4, 3), dma(2, 4, 3), dma(4, 3), dma(4, 3),
            dma(2, 4), dma(2, 4), dma(2, 3), dma(2, 3), dma(2), dma(2),
            dma(7), dma(8), dma(15), dma(16),
        ],
        compiler_params=pltpu.CompilerParams(
            collective_id=0, has_side_effects=True, vmem_limit_bytes=58 * 2**20),
        name="filter_and_subspace",
    )(orbitals, potential, zmat)
    return out, cor, sub


def solution(mesh):
    placed = (P("orb", "dom", None, None, None), P("dom", None, None, None))
    return jax.shard_map(
        shards,
        mesh=mesh,
        in_specs=placed,
        out_specs=(P("orb", "dom", None, None, None), P(), P()),
        check_vma=False,
    )
```

```python
import math

import jax
import jax.numpy as jnp
import numpy as np
from jax import lax
from jax.experimental import pallas as pl
from jax.experimental.pallas import tpu as pltpu
from jax.sharding import PartitionSpec as P

HALO = 6
SPACING = 0.5
UPPER = 44.0
CUTOFF = 4.0
LOWEST = -1.0
NX, NY, NZ, NO = 32, 24, 128, 8
CELLS = 3145728
CHUNK = 4
ORDERS = ((3, 7, 2, 6, 0, 4, 1, 5), (0, 4, 1, 5, 3, 7, 2, 6))
FLIGHT = 4
LOADS = (1, 3, 0, 2)
ROWS = ((6, 12), (0, 6), (18, 6))
PARTS = ((0,), (1, 2))
MESH = pl.DeviceIdType.MESH
F32, BF16 = jnp.float32, jnp.bfloat16
HIGH = lax.Precision.HIGHEST


def stencil_weights():
    return [
        2.0 * (-1.0) ** (m + 1) * math.factorial(HALO) ** 2
        / (m * m * math.factorial(HALO - m) * math.factorial(HALO + m))
        for m in range(1, HALO + 1)
    ]


WEIGHTS = stencil_weights()
KINETIC = -0.5 / SPACING**2
CENTRE = KINETIC * 3.0 * (-2.0 * sum(WEIGHTS))
HALF = (UPPER - CUTOFF) / 2.0
MIDDLE = (UPPER + CUTOFF) / 2.0
SIGMA1 = HALF / (LOWEST - MIDDLE)
SIGMA2 = 1.0 / (2.0 / SIGMA1 - SIGMA1)


def doubled(matrix):
    wide = matrix.astype(np.float32)
    hi = wide.astype(BF16)
    lo = (wide - hi.astype(np.float32)).astype(BF16)
    row = np.concatenate([hi, lo], axis=1)
    return np.concatenate([row, row], axis=0)


def z_matrices():
    own = np.zeros((NZ, NZ))
    above = np.zeros((NZ, NZ))
    below = np.zeros((NZ, NZ))
    for z in range(NZ):
        for m in range(1, HALO + 1):
            weight = KINETIC * WEIGHTS[m - 1]
            for k in (z - m, z + m):
                if 0 <= k < NZ:
                    own[k, z] = weight
                elif k >= NZ:
                    above[k - NZ, z] = weight
                else:
                    below[k + HALO, z] = weight
    upper = np.zeros((NZ, NZ))
    top = np.zeros((NZ, NZ))
    for z in range(NZ):
        g, at = z // 64, z % 64
        for m in range(1, HALO + 1):
            weight = KINETIC * WEIGHTS[m - 1]
            if at + m < 64:
                upper[z + m, z] = weight
            else:
                top[8 * g + at + m - 64, z] = weight
    return np.stack([doubled(v) for v in (own, above, below, upper, top)])


def split_wide(v):
    hi = v.astype(BF16)
    lo = (v - hi.astype(F32)).astype(BF16)
    return jnp.concatenate([hi, lo], axis=1)


def flat(block):
    return jnp.concatenate([block[j] for j in range(block.shape[0])], axis=1)


def kernel(orb_hbm, pot_hbm, zmat_ref, out_hbm, cor_ref, sub_ref,
           inp, pot, e0, e1, e2, zacc, potb, zf, zh, rl, pf, sb, ocp, hp, tp, tx, potp, zs, zp, part, ar1, ar2,
           in_sem, pot_sem, out_sem,
           y_ss, y_rs, r_ss, r_rs, p_ss, x_ss, x_rs, z_ss, z_rs, c_ss, c_rs, g_ss, g_rs,
           ty_ss, ty_rs, tx_ss, tx_rs, zp_ss, zp_rs, a1_ss, a1_rs, a2_ss, a2_rs):
    d = lax.axis_index("dom")
    o = lax.axis_index("orb")
    bx, by, bz = d // 8, (d // 2) % 4, d % 2
    chip, core = o // 2, o % 2
    px, pzl = d % 4, (d // 4) % 2
    other_core = (d, o + 1 - 2 * core)
    other_chip = (d, (o + 2) % 4)
    column = lambda i: ((d + 4 * (i // 4)) % 8 + 8 * bx, (o + i) % 4)
    plane = lambda i: (((bx + i // 4) % 4) * 8 + 4 * pzl + (px + i) % 4, o)
    columns = [column(i) for i in range(1, 8)]
    planes = [plane(i) for i in range(1, 16)]
    zl = (d + 4 - 8 * pzl, o)
    crossed = (d + 1 - 2 * bz, (o + 2) % 4)
    lower = {"x": (d - 8, o), "y": (d - 2, o)}
    upper = {"x": (d + 8, o), "y": (d + 2, o)}
    has_lower = {"x": bx > 0, "y": by > 0}
    has_upper = {"x": bx < 3, "y": by < 3}
    is_a, is_b = chip == 0, chip == 1

    def when(cond, fn):
        if cond is None:
            fn()
        else:
            pl.when(cond)(lambda: fn() and None)

    loads = [
        pltpu.make_async_copy(
            orb_hbm.at[:, 0, pl.ds(8 * k, 8)], inp.at[:, pl.ds(8 * k, 8)], in_sem.at[k])
        for k in range(4)
    ]
    for k in LOADS:
        loads[k].start()
    pot_load = pltpu.make_async_copy(pot_hbm.at[0], pot, pot_sem)
    pot_load.start()

    barrier = pltpu.get_barrier_semaphore()
    for dev in columns + planes:
        pl.semaphore_signal(barrier, inc=1, device_id=dev, device_id_type=MESH)

    @pl.when(by == 1)
    def _():
        pl.semaphore_signal(barrier, inc=1, device_id=upper["y"], device_id_type=MESH)

    @pl.when(by == 2)
    def _():
        pl.semaphore_signal(barrier, inc=1, device_id=lower["y"], device_id_type=MESH)

    crosses = (is_a & (bz == 1)) | (is_b & (bz == 0))

    @pl.when(crosses)
    def _():
        pl.semaphore_signal(barrier, inc=1, device_id=crossed, device_id_type=MESH)

    for buf in (e0, e1):
        @pl.when(bx == 0)
        def _(buf=buf):
            buf[0:HALO] = jnp.zeros((HALO, NY + 12, 8, 128), F32)

        @pl.when(bx == 3)
        def _(buf=buf):
            buf[NX + HALO:] = jnp.zeros((HALO, NY + 12, 8, 128), F32)

        @pl.when(by == 0)
        def _(buf=buf):
            @pl.loop(0, NX)
            def _(x):
                buf[HALO + x, 0:HALO] = jnp.zeros((HALO, 8, 128), F32)

        @pl.when(by == 3)
        def _(buf=buf):
            @pl.loop(0, NX)
            def _(x):
                buf[HALO + x, NY + HALO:] = jnp.zeros((HALO, 8, 128), F32)

    @pl.when(bx == 3)
    def _():
        tx[...] = jnp.zeros_like(tx)

    @pl.when(by == 3)
    def _():
        @pl.loop(0, 16)
        def _(x):
            for s in (0, 1):
                pf[s, x, NY:] = jnp.zeros((HALO, 8, 128), F32)

    @pl.when(is_b & (bz == 1))
    def _():
        zp[...] = jnp.zeros_like(zp)

    pl.semaphore_wait(barrier, 22 + jnp.where((by == 1) | (by == 2), 1, 0) + jnp.where(crosses, 1, 0))

    def y_copy(stage, buf, k, side):
        rows = pl.ds(HALO + CHUNK * k, CHUNK)
        src, dst = ((HALO, NY + HALO), (NY, 0))[side]
        return pltpu.make_async_remote_copy(
            src_ref=buf.at[rows, pl.ds(src, HALO)], dst_ref=buf.at[rows, pl.ds(dst, HALO)],
            send_sem=y_ss.at[stage, k, side], recv_sem=y_rs.at[stage, k, side],
            device_id=(lower, upper)[side]["y"], device_id_type=MESH)

    def x_copy(stage, buf, side, r):
        src, dst = ((HALO, NX + HALO), (NX, 0))[side]
        cols = pl.ds(HALO + ROWS[r][0], ROWS[r][1])
        return pltpu.make_async_remote_copy(
            src_ref=buf.at[pl.ds(src, HALO), cols], dst_ref=buf.at[pl.ds(dst, HALO), cols],
            send_sem=x_ss.at[stage, side, r], recv_sem=x_rs.at[stage, side, r],
            device_id=(lower, upper)[side]["x"], device_id_type=MESH)

    def z_copies(stage, part):
        return [
            pltpu.make_async_remote_copy(
                src_ref=zf.at[stage, :, pl.ds(*ROWS[r])], dst_ref=zh.at[stage, :, pl.ds(*ROWS[r])],
                send_sem=z_ss.at[stage, r], recv_sem=z_rs.at[stage, r],
                device_id=(d + 1 - 2 * bz, o), device_id_type=MESH)
            for r in PARTS[part]
        ]

    def sends(axis, side):
        return (has_lower, has_upper)[side][axis]

    def receives(axis, side):
        return (has_upper, has_lower)[side][axis]

    queue = [(n, buf, k) for n, buf in ((0, e0), (1, e1)) for k in ORDERS[n]]
    sent, passed = [], []

    def direct(q, side):
        if q % 2 == 0:
            return sends("y", side)
        return ((by == 1) | (by == 3), (by == 0) | (by == 2))[side]

    def relayed(q, side):
        n, buf, k = queue[q]
        return pltpu.make_async_remote_copy(
            src_ref=buf.at[pl.ds(HALO + CHUNK * k, CHUNK), pl.ds((HALO, NY)[side], HALO)],
            dst_ref=rl.at[n, q % 8 // 2], send_sem=r_ss.at[n, q % 8 // 2], recv_sem=r_rs.at[n, q % 8 // 2],
            device_id=zl, device_id_type=MESH)

    def passing(q, side):
        n, buf, k = queue[q]
        return pltpu.make_async_remote_copy(
            src_ref=rl.at[n, q % 8 // 2],
            dst_ref=buf.at[pl.ds(HALO + CHUNK * k, CHUNK), pl.ds((NY + HALO, 0)[side], HALO)],
            send_sem=p_ss.at[n, q % 8 // 2], recv_sem=y_rs.at[n, k, side],
            device_id=(upper, lower)[side]["y"], device_id_type=MESH)

    def each_send(q, act):
        for side in (0, 1):
            when(direct(q, side), lambda: act(y_copy(*queue[q], side)))
            if q % 2:
                when(by == 2 - side, lambda: act(relayed(q, side)))

    def pass_on(q):
        for side in (0, 1):
            def go():
                relayed(q, side).wait_recv()
                passing(q, side).start()
            when(by == 3 * side, go)

    def pump(last, done=-1):
        while len(sent) <= min(last, len(queue) - 1):
            q = len(sent)
            if q >= 8 and ORDERS[0].index(queue[q][2]) > done:
                break
            if q >= FLIGHT:
                each_send(q - FLIGHT, lambda c: c.wait_send())
            each_send(q, lambda c: c.start())
            sent.append(q)
        while 2 * len(passed) + 1 < min(len(sent) - 1, last) or (
                last >= len(queue) and len(sent) == len(queue) and len(passed) < 8):
            q = 2 * len(passed) + 1
            pass_on(q)
            passed.append(q)

    def wait_y(q):
        for side in (0, 1):
            when(receives("y", side), lambda: y_copy(*queue[q], side).wait_recv())

    def send_x(stage, buf, side, part):
        for r in PARTS[part]:
            when(sends("x", side), lambda: x_copy(stage, buf, side, r).start())

    def wait_x(stage, buf, part):
        for side in (0, 1):
            for r in PARTS[part]:
                when(receives("x", side), lambda: x_copy(stage, buf, side, r).wait_recv())

    lane = lax.broadcasted_iota(jnp.int32, (8, 128), 1)

    def pack_z(stage, buf, part):
        first = jnp.where(bz == 0, NZ - HALO, 0)
        shifts = [lax.rem(8 * x + 128 - first, 128) for x in range(16)]

        def rows(half, y, n):
            for j in range(n):
                total = None
                for x in range(16):
                    moved = pltpu.roll(buf[HALO + 16 * half + x, HALO + y + j], shifts[x], axis=1)
                    total = moved if total is None else jnp.where(lane // 8 == x, moved, total)
                zf[stage, half, y + j] = total

        @pl.loop(0, 4)
        def _(t):
            if part == 0:
                rows(t // 2, 6 + 6 * (t % 2), 6)
            else:
                rows(t // 2, 18 * (t % 2), 6)
        for copy in z_copies(stage, part):
            copy.start()

    def pack_top(first, dst, slot, half):
        @pl.loop(0, NY // 4)
        def _(t):
            for j in range(4):
                total = None
                for i in range(16):
                    moved = pltpu.roll(
                        e2[8 * half + i // 2 + 16 * (i % 2), 4 * t + j],
                        (8 * i + 128 - first) % 128, axis=1)
                    total = moved if total is None else jnp.where(lane // 8 == i, moved, total)
                dst[slot, half, 4 * t + j] = total

    def z_own(buf, part):
        @pl.loop(0, NX // 4)
        def _(t):
            at = pl.ds(4 * t, 4)
            v = [buf[pl.ds(HALO + 4 * t, 4), pl.ds(HALO + ROWS[r][0], ROWS[r][1])] for r in PARTS[part]]
            v = jnp.concatenate(v, axis=1) if part else v[0]
            r = jnp.dot(split_wide(v.reshape(4 * 12 * 8, 128)), zmat_ref[0], preferred_element_type=F32)
            r = (r[:, :128] + r[:, 128:]).reshape(4, 12, 8, 128)
            if part == 0:
                zacc[at, pl.ds(6, 12)] = r
            else:
                zacc[at, pl.ds(0, 6)] = r[:, :6]
                zacc[at, pl.ds(18, 6)] = r[:, 6:]

    def z_halo(stage, part):
        for copy in z_copies(stage, part):
            copy.wait_recv()

        @pl.loop(0, NX // 4)
        def _(t):
            parts = []
            for j in range(4):
                x = 4 * t + j
                packed = [zh[stage, x // 16, pl.ds(*ROWS[r])].reshape(ROWS[r][1] * 8, 128)
                          for r in PARTS[part]]
                packed = jnp.concatenate(packed, axis=0) if part else packed[0]
                parts.append(pltpu.roll(packed, lax.rem(128 - 8 * lax.rem(x, 16), 128), axis=1))
            v = jnp.concatenate(parts, axis=0)
            r = jnp.dot(split_wide(v), zmat_ref[1 + bz], preferred_element_type=F32)
            r = (r[:, :128] + r[:, 128:]).reshape(4, 12, 8, 128)
            at = pl.ds(4 * t, 4)
            if part == 0:
                zacc[at, pl.ds(6, 12)] += r
            else:
                zacc[at, pl.ds(0, 6)] += r[:, :6]
                zacc[at, pl.ds(18, 6)] += r[:, 6:]

    def rows_of(src, dst, off, x, y, scale, shift, prev, prev_scale):
        def at(dx, dy):
            return src[x + HALO + dx, pl.ds(y + HALO + dy, HALO)]

        total = scale * zacc[x, pl.ds(y, HALO)]
        total += (scale * potb[x, pl.ds(y, HALO)] + (scale * CENTRE + shift)) * at(0, 0)
        for m in range(1, HALO + 1):
            near = (at(m, 0) + at(-m, 0)) + (at(0, m) + at(0, -m))
            total += (scale * KINETIC * WEIGHTS[m - 1]) * near
        if prev is not None:
            total -= prev_scale * prev[x + HALO, pl.ds(y + HALO, HALO)]
        dst[x + off, pl.ds(y + off, HALO)] = total

    def stage_rows(lo, hi, ys_, *args):
        @pl.loop(lo, hi)
        def _(x):
            for y in ys_:
                rows_of(*args[:3], x, y, *args[3:])

    def faces(n, *args):
        for j, k in enumerate(ORDERS[n]):
            wait_y(8 * n + j)
            stage_rows(CHUNK * k, CHUNK * k + CHUNK, (0, 18), *args)
            pump(8 * n + j + FLIGHT, 8 * n + j)
            yield j, k

    flat_in = inp.reshape(NO * NX * NY, 128)
    for i, k in enumerate(LOADS):
        loads[k].wait()

        @pl.loop(8 * k, 8 * k + 8)
        def _(x):
            for y in range(NY):
                e0[HALO + x, HALO + y] = flat_in[pl.ds(x * NY + y, 8, stride=NX * NY), :]
        if i < 2:
            pump(i)
    for side in (0, 1):
        for part_ in (0, 1):
            send_x(0, e0, side, part_)
    pump(2)
    pack_z(0, e0, 0)
    pack_z(0, e0, 1)
    pump(3)
    pot_load.wait()

    @pl.loop(0, NX)
    def _(x):
        for y in range(NY):
            potb[x, y] = jnp.broadcast_to(pot[x, pl.ds(y, 1)], (8, 128))

    first = (e0, e1, HALO, SIGMA1 / HALF, -SIGMA1 / HALF * MIDDLE, None, 0.0)
    z_own(e0, 0)
    z_own(e0, 1)
    z_halo(0, 0)
    stage_rows(HALO, NX - HALO, (6, 12), *first)
    pump(4)
    wait_x(0, e0, 0)
    stage_rows(0, HALO, (6, 12), *first)
    stage_rows(NX - HALO, NX, (6, 12), *first)
    send_x(1, e1, 0, 0)
    send_x(1, e1, 1, 0)
    pack_z(1, e1, 0)
    z_own(e1, 0)
    z_halo(0, 1)

    @pl.loop(0, 16)
    def _(x):
        for y in range(NY):
            one, two = potb[x, y], potb[16 + x, y]
            low = jnp.where(lane < 64, one, pltpu.roll(two, 64, axis=1))
            high = jnp.where(lane < 64, pltpu.roll(one, 64, axis=1), two)
            potp[x, y] = jnp.where(is_a, low, high)

    wait_x(0, e0, 1)
    z_halo(1, 0)
    wait_x(1, e1, 0)

    def pack_rows(lo, hi, rows):
        @pl.loop(lo, hi)
        def _(x):
            for y, n in rows:
                for j in range(y, y + n):
                    one, two = e2[x, j], e2[16 + x, j]
                    low = jnp.where(lane < 64, one, pltpu.roll(two, 64, axis=1))
                    high = jnp.where(lane < 64, pltpu.roll(one, 64, axis=1), two)
                    pf[0, x, j] = jnp.where(is_a, low, high)
                    sb[x, j] = jnp.where(is_a, high, low)

    def piece(c, r):
        return pl.ds(4 * c, 4), pl.ds(*ROWS[r])

    def chip_copy(c, r):
        p = piece(c, r)
        return pltpu.make_async_remote_copy(
            src_ref=sb.at[p], dst_ref=pf.at[(1,) + p], send_sem=g_ss.at[c, r], recv_sem=g_rs.at[c, r],
            device_id=other_chip, device_id_type=MESH)

    def core_copy(s, c, r):
        p = (s,) + piece(c, r)
        return pltpu.make_async_remote_copy(
            src_ref=pf.at[p], dst_ref=ocp.at[p], send_sem=c_ss.at[s, c, r], recv_sem=c_rs.at[s, c, r],
            device_id=other_core, device_id_type=MESH)

    def ty_copy(s, c):
        xs = pl.ds(4 * c, 4)
        return pltpu.make_async_remote_copy(
            src_ref=pf.at[s, xs, pl.ds(0, HALO)], dst_ref=pf.at[s, xs, pl.ds(NY, HALO)],
            send_sem=ty_ss.at[s, c], recv_sem=ty_rs.at[s, c], device_id=lower["y"], device_id_type=MESH)

    PAIRS = ((6, 12), (0, 18))

    def tx_copy(s, half):
        rows = pl.ds(6 * half, 6)
        return pltpu.make_async_remote_copy(
            src_ref=tp.at[s, :, rows], dst_ref=tx.at[s, :, rows],
            send_sem=tx_ss.at[s, half], recv_sem=tx_rs.at[s, half], device_id=lower["x"], device_id_type=MESH)

    def send_tx(s, half):
        one, two = PAIRS[half]

        @pl.loop(0, HALO)
        def _(x):
            for j in range(6):
                tp[s, x, 6 * half + j] = jnp.where(
                    lane < 64, pf[s, x, one + j], pltpu.roll(pf[s, x, two + j], 64, axis=1))
        when(has_lower["x"], lambda: tx_copy(s, half).start())

    def zp_copy(src, slot, dev):
        return pltpu.make_async_remote_copy(
            src_ref=zs.at[src], dst_ref=zp.at[slot], send_sem=zp_ss.at[src], recv_sem=zp_rs.at[slot],
            device_id=dev, device_id_type=MESH)

    def down(s, c, r):
        if r == 1:
            when(has_lower["y"], lambda: ty_copy(s, c).start())
        if c == 1 and r != 1:
            send_tx(s, r // 2)
        core_copy(s, c, r).start()

    def arrived(c, r):
        chip_copy(c, r).wait_recv()
        down(1, c, r)

    s2 = 2.0 * SIGMA2 / HALF
    second = (e1, e2, 0, s2, -s2 * MIDDLE, e0, SIGMA1 * SIGMA2)
    for j, k in faces(0, *first):
        stage_rows(CHUNK * k, CHUNK * k + CHUNK, (6, 12), *second)
        if j % 2:
            c = k % 4
            pack_rows(4 * c, 4 * c + 4, ROWS[:1])
            chip_copy(c, 0).start()
            down(0, c, 0)
        if j == 3:
            send_x(1, e1, 1, 1)
        if j == 6:
            send_x(1, e1, 0, 1)

    def tops(half):
        @pl.when(is_a)
        def _():
            pack_top(64, zp, 0, half)

            @pl.when(bz == 1)
            def _():
                pack_top(0, zs, 1, half)

        @pl.when(is_b)
        def _():
            pack_top(64, zs, 0, half)

            @pl.when(bz == 1)
            def _():
                pack_top(0, zs, 1, half)

    def leave(c):
        @pl.loop(0, 2)
        def _(g):
            @pl.loop(0, CHUNK)
            def _(x):
                at = 16 * g + 4 * c + x
                for orb in range(NO):
                    inp[orb, at] = e2[at, :, orb]

    pack_z(1, e1, 1)
    z_own(e1, 1)
    wait_x(1, e1, 1)
    z_halo(1, 1)
    early = [(3, 0), (2, 0), (0, 0), (1, 0), (0, 1), (0, 2), (1, 1), (1, 2), (3, 1), (3, 2), (2, 1), (2, 2)]
    for j, k in faces(1, *second):
        if j % 2:
            c = k % 4
            pack_rows(4 * c, 4 * c + 4, ROWS[1:])
            for r in (1, 2):
                chip_copy(c, r).start()
            for r in (1, 2):
                down(0, c, r)
            for _ in range(2):
                arrived(*early.pop(0))

            if c != 2:
                leave(c)
        if j == 3:
            tops(0)
    tops(1)

    @pl.when(is_a & (bz == 1))
    def _():
        zp_copy(1, 1, crossed).start()

    @pl.when(is_b)
    def _():
        zp_copy(0, 1, other_chip).start()

    @pl.when(is_b & (bz == 1))
    def _():
        zp_copy(1, 0, (d - 1, o)).start()

    def z_upper(s):
        @pl.loop(0, 4)
        def _(t):
            v = pf[s, pl.ds(4 * t, 4), pl.ds(0, NY)].reshape(4 * NY * 8, 128)
            parts = []
            for j in range(4):
                x = 4 * t + j
                packed = zp[s, x // 8].reshape(NY * 8, 128)
                parts.append(pltpu.roll(packed, lax.rem(128 - 16 * lax.rem(x, 8), 128), axis=1))
            r = jnp.dot(split_wide(v), zmat_ref[3], preferred_element_type=F32)
            r += jnp.dot(split_wide(jnp.concatenate(parts, axis=0)), zmat_ref[4], preferred_element_type=F32)
            zacc[pl.ds(16 * s + 4 * t, 4)] = (r[:, :128] + r[:, 128:]).reshape(4, NY, 8, 128)

    def shift_x(s):
        @pl.loop(0, HALO)
        def _(x):
            for half, (one, two) in enumerate(PAIRS):
                for j in range(6):
                    there = tx[s, x, 6 * half + j]
                    both = jnp.where(lane < 64, there, pf[s, x, one + j])
                    pf[s, 16 + x, one + j] = pltpu.roll(both, 64, axis=1)
                    pf[s, 16 + x, two + j] = jnp.where(
                        lane < 64, pltpu.roll(pf[s, x, two + j], 64, axis=1), there)

    def half_rows(s, ys_):
        @pl.loop(0, 16)
        def _(x):
            for y in ys_:
                total = zacc[16 * s + x, pl.ds(y, HALO)]
                total += (0.5 * CENTRE + 0.5 * potp[x, pl.ds(y, HALO)]) * pf[s, x, pl.ds(y, HALO)]
                for m in range(1, HALO + 1):
                    near = pf[s, x + m, pl.ds(y, HALO)] + pf[s, x, pl.ds(y + m, HALO)]
                    total += (KINETIC * WEIGHTS[m - 1]) * near
                hp[s, x, pl.ds(y, HALO)] = total

    @pl.when(is_a)
    def _():
        zp_copy(0, 1, other_chip).wait_recv()

    @pl.when(is_b & (bz == 0))
    def _():
        zp_copy(1, 0, other_chip).wait_recv()
        zp_copy(1, 1, other_chip).wait_recv()

    def upper_rows(s):
        for half in (0, 1):
            when(has_upper["x"], lambda: tx_copy(s, half).wait_recv())
        shift_x(s)
        half_rows(s, (0, 6, 12))

    z_upper(0)
    while early:
        arrived(*early.pop(0))
    leave(2)
    out_copy = pltpu.make_async_copy(inp, out_hbm.at[:, 0], out_sem)
    out_copy.start()
    upper_rows(0)
    z_upper(1)
    upper_rows(1)

    for s in (0, 1):
        for c in range(4):
            for r in range(3):
                core_copy(s, c, r).wait_recv()

    def grams(rows):
        def halves(ref, x):
            v = jnp.concatenate([flat(ref[s, x, rows]) for s in (0, 1)], axis=0)
            hi = v.astype(BF16)
            return hi, (v - hi.astype(F32)).astype(BF16)

        def body(x, total):
            (mh, ml), (oh, ol), (hh, hl) = halves(pf, x), halves(ocp, x), halves(hp, x)
            left = jnp.concatenate([mh, oh, ml, ol], axis=0)
            right = jnp.concatenate([mh, hh, ml, hl], axis=0)
            full = lax.dot_general(left, right, (((1,), (1,)), ((), ())), preferred_element_type=F32)
            return total + ((full[:32, :32] + full[32:, :32]) + (full[:32, 32:] + full[32:, 32:]))
        return body

    total = lax.fori_loop(0, 16, grams(pl.ds(0, 18)), jnp.zeros((32, 32), F32))
    for s in (0, 1):
        for c in range(4):
            when(has_upper["y"], lambda: ty_copy(s, c).wait_recv())
        half_rows(s, (18,))
    total = lax.fori_loop(0, 16, grams(pl.ds(18, 6)), total)

    def place(block, starts):
        n = block.shape[1]
        r = lax.broadcasted_iota(jnp.int32, (n, 128), 0)
        c = lax.broadcasted_iota(jnp.int32, (n, 128), 1)
        chosen = jnp.zeros((n, 128), jnp.bool_)
        for j, s in enumerate(starts):
            chosen = chosen | ((r // 8 == j) & (c == s + r % 8))
        return jnp.dot(block, chosen.astype(F32), precision=HIGH, preferred_element_type=F32)

    o_core = o + 1 - 2 * core
    o_chip = (o + 2) % 4
    placed = place(total, (8 * o, 8 * o_chip, 32 + 8 * o, 32 + 8 * o_chip))
    for j, orbital in enumerate((o, o_chip, o_core, o_core + 2 - 4 * chip)):
        part[pl.ds(pl.multiple_of(8 * orbital, 8), 8), :] = placed[8 * j:8 * j + 8]

    def reduce(block, ar, ss, rs, mine, source, partners):
        ar[mine] = block
        copies = []
        for i, dev in enumerate(partners):
            copies.append(pltpu.make_async_remote_copy(
                src_ref=ar.at[mine], dst_ref=ar.at[mine], send_sem=ss.at[i], recv_sem=rs.at[mine],
                device_id=dev, device_id_type=MESH))
            copies[-1].start()
        for i, dev in enumerate(partners):
            at = source(i + 1)
            pltpu.make_async_remote_copy(
                src_ref=ar.at[at], dst_ref=ar.at[at], send_sem=ss.at[i], recv_sem=rs.at[at],
                device_id=dev, device_id_type=MESH).wait_recv()
        total = ar[0]
        for i in range(1, len(partners) + 1):
            total += ar[i]
        for c in copies:
            c.wait_send()
        return total

    folded = part[0:16, :] + pltpu.roll(part[16:32, :], 64, axis=1)
    folded = reduce(folded, ar1, a1_ss, a1_rs, 4 * pzl + o,
                    lambda i: 4 * ((pzl + i // 4) % 2) + (o + i) % 4, columns)
    folded = reduce(folded, ar2, a2_ss, a2_rs, 4 * bx + px,
                    lambda i: 4 * ((bx + i // 4) % 4) + (px + i) % 4, planes)
    part[0:16, :] = folded
    part[16:32, :] = pltpu.roll(folded, 64, axis=1)

    square = part[...]
    r = lax.broadcasted_iota(jnp.int32, (32, 32), 0)
    c = lax.broadcasted_iota(jnp.int32, (32, 32), 1)
    eye = (r == c).astype(F32)
    cor_ref[...] = square[:, 0:32] * (1.0 / CELLS)
    m = square[:, 32:64]
    t = lax.dot_general(m, eye, (((0,), (0,)), ((), ())), precision=HIGH, preferred_element_type=F32)
    sub_ref[...] = (m + t) * (1.0 / (CELLS * HALF))

    out_copy.wait()
    for q in range(len(queue) - FLIGHT, len(queue)):
        each_send(q, lambda c: c.wait_send())
    for q in passed:
        for side in (0, 1):
            when(by == 3 * side, lambda: passing(q, side).wait_send())
    for n, buf in ((0, e0), (1, e1)):
        for side in (0, 1):
            for r in range(3):
                when(sends("x", side), lambda: x_copy(n, buf, side, r).wait_send())
        for part_ in (0, 1):
            for copy in z_copies(n, part_):
                copy.wait_send()
    for c in range(4):
        for r in range(3):
            chip_copy(c, r).wait_send()
            for s in (0, 1):
                core_copy(s, c, r).wait_send()
        for s in (0, 1):
            when(has_lower["y"], lambda: ty_copy(s, c).wait_send())
    for s in (0, 1):
        for half in (0, 1):
            when(has_lower["x"], lambda: tx_copy(s, half).wait_send())
    when(is_b, lambda: zp_copy(0, 1, other_chip).wait_send())
    when(bz == 1, lambda: zp_copy(1, 1, other_chip).wait_send())


def shards(orbitals, potential):
    zmat = jnp.asarray(z_matrices())
    field = (NX + 12, NY + 12, 8, 128)
    vm = lambda *shape: pltpu.VMEM(shape, F32)
    dma = lambda *shape: pltpu.SemaphoreType.DMA(shape)
    out, cor, sub = pl.pallas_call(
        kernel,
        out_shape=(
            jax.ShapeDtypeStruct((NO, 1, NX, NY, NZ), F32),
            jax.ShapeDtypeStruct((32, 32), F32),
            jax.ShapeDtypeStruct((32, 32), F32),
        ),
        in_specs=[pl.BlockSpec(memory_space=pl.ANY)] * 2 + [pl.BlockSpec(memory_space=pltpu.VMEM)],
        out_specs=(pl.BlockSpec(memory_space=pl.ANY),) + (pl.BlockSpec(memory_space=pltpu.VMEM),) * 2,
        scratch_shapes=[
            vm(NO, NX, NY, NZ), vm(NX, NY, NZ), vm(*field), vm(*field), vm(NX, NY, 8, 128),
            vm(NX, NY, 8, 128), vm(NX, NY, 8, 128),
            vm(2, 2, NY, 8, 128), vm(2, 2, NY, 8, 128), vm(2, 4, CHUNK, HALO, 8, 128),
            vm(2, 16 + HALO, NY + HALO, 8, 128), vm(16, NY, 8, 128), vm(2, 16, NY, 8, 128),
            vm(2, 16, NY, 8, 128), vm(2, HALO, 12, 8, 128), vm(2, HALO, 12, 8, 128), vm(16, NY, 8, 128),
            vm(2, 2, NY, 8, 128), vm(2, 2, NY, 8, 128),
            vm(32, 128), vm(8, 16, 128), vm(16, 16, 128),
            dma(4), pltpu.SemaphoreType.DMA, pltpu.SemaphoreType.DMA,
            dma(2, 8, 2), dma(2, 8, 2), dma(2, 4), dma(2, 4), dma(2, 4), dma(2, 2, 3), dma(2, 2, 3), dma(2, 3), dma(2, 3),
            dma(2, 4, 3), dma(2, 4, 3), dma(4, 3), dma(4, 3),
            dma(2, 4), dma(2, 4), dma(2, 3), dma(2, 3), dma(2), dma(2),
            dma(7), dma(8), dma(15), dma(16),
        ],
        compiler_params=pltpu.CompilerParams(
            collective_id=0, has_side_effects=True, vmem_limit_bytes=58 * 2**20),
        name="filter_and_subspace",
    )(orbitals, potential, zmat)
    return out, cor, sub


def solution(mesh):
    placed = (P("orb", "dom", None, None, None), P("dom", None, None, None))
    return jax.shard_map(
        shards,
        mesh=mesh,
        in_specs=placed,
        out_specs=(P("orb", "dom", None, None, None), P(), P()),
        check_vma=False,
    )
```

```python
import math

import jax
import jax.numpy as jnp
import numpy as np
from jax import lax
from jax.experimental import pallas as pl
from jax.experimental.pallas import tpu as pltpu
from jax.sharding import PartitionSpec as P

HALO = 6
SPACING = 0.5
UPPER = 44.0
CUTOFF = 4.0
LOWEST = -1.0
NX, NY, NZ, NO = 32, 24, 128, 8
CELLS = 3145728
CHUNK = 4
ORDERS = ((3, 7, 2, 6, 0, 4, 1, 5), (0, 4, 1, 5, 3, 7, 2, 6))
FLIGHT = 4
LOADS = (1, 3, 0, 2)
ROWS = ((6, 12), (0, 6), (18, 6))
PARTS = ((0,), (1, 2))
MESH = pl.DeviceIdType.MESH
F32, BF16 = jnp.float32, jnp.bfloat16
HIGH = lax.Precision.HIGHEST


def stencil_weights():
    return [
        2.0 * (-1.0) ** (m + 1) * math.factorial(HALO) ** 2
        / (m * m * math.factorial(HALO - m) * math.factorial(HALO + m))
        for m in range(1, HALO + 1)
    ]


WEIGHTS = stencil_weights()
KINETIC = -0.5 / SPACING**2
CENTRE = KINETIC * 3.0 * (-2.0 * sum(WEIGHTS))
HALF = (UPPER - CUTOFF) / 2.0
MIDDLE = (UPPER + CUTOFF) / 2.0
SIGMA1 = HALF / (LOWEST - MIDDLE)
SIGMA2 = 1.0 / (2.0 / SIGMA1 - SIGMA1)


def doubled(matrix):
    wide = matrix.astype(np.float32)
    hi = wide.astype(BF16)
    lo = (wide - hi.astype(np.float32)).astype(BF16)
    row = np.concatenate([hi, lo], axis=1)
    return np.concatenate([row, row], axis=0)


def z_matrices():
    own = np.zeros((NZ, NZ))
    above = np.zeros((NZ, NZ))
    below = np.zeros((NZ, NZ))
    for z in range(NZ):
        for m in range(1, HALO + 1):
            weight = KINETIC * WEIGHTS[m - 1]
            for k in (z - m, z + m):
                if 0 <= k < NZ:
                    own[k, z] = weight
                elif k >= NZ:
                    above[k - NZ, z] = weight
                else:
                    below[k + HALO, z] = weight
    upper = np.zeros((NZ, NZ))
    top = np.zeros((NZ, NZ))
    for z in range(NZ):
        g, at = z // 64, z % 64
        for m in range(1, HALO + 1):
            weight = KINETIC * WEIGHTS[m - 1]
            if at + m < 64:
                upper[z + m, z] = weight
            else:
                top[8 * g + at + m - 64, z] = weight
    return np.stack([doubled(v) for v in (own, above, below, upper, top)])


def split_wide(v):
    hi = v.astype(BF16)
    lo = (v - hi.astype(F32)).astype(BF16)
    return jnp.concatenate([hi, lo], axis=1)


def flat(block):
    return jnp.concatenate([block[j] for j in range(block.shape[0])], axis=1)


def kernel(orb_hbm, pot_hbm, zmat_ref, out_hbm, cor_ref, sub_ref,
           inp, pot, e0, e1, e2, zacc, potb, zf, zh, rl, pf, sb, ocp, hp, tp, tx, potp, zs, zp, part, ar1, ar2,
           in_sem, pot_sem, out_sem,
           y_ss, y_rs, r_ss, r_rs, p_ss, x_ss, x_rs, z_ss, z_rs, c_ss, c_rs, g_ss, g_rs,
           ty_ss, ty_rs, tx_ss, tx_rs, zp_ss, zp_rs, a1_ss, a1_rs, a2_ss, a2_rs):
    d = lax.axis_index("dom")
    o = lax.axis_index("orb")
    bx, by, bz = d // 8, (d // 2) % 4, d % 2
    chip, core = o // 2, o % 2
    px, pzl = d % 4, (d // 4) % 2
    other_core = (d, o + 1 - 2 * core)
    other_chip = (d, (o + 2) % 4)
    column = lambda i: ((d + 4 * (i // 4)) % 8 + 8 * bx, (o + i) % 4)
    plane = lambda i: (((bx + i // 4) % 4) * 8 + 4 * pzl + (px + i) % 4, o)
    columns = [column(i) for i in range(1, 8)]
    planes = [plane(i) for i in range(1, 16)]
    zl = (d + 4 - 8 * pzl, o)
    crossed = (d + 1 - 2 * bz, (o + 2) % 4)
    lower = {"x": (d - 8, o), "y": (d - 2, o)}
    upper = {"x": (d + 8, o), "y": (d + 2, o)}
    has_lower = {"x": bx > 0, "y": by > 0}
    has_upper = {"x": bx < 3, "y": by < 3}
    is_a, is_b = chip == 0, chip == 1

    def when(cond, fn):
        if cond is None:
            fn()
        else:
            pl.when(cond)(lambda: fn() and None)

    loads = [
        pltpu.make_async_copy(
            orb_hbm.at[:, 0, pl.ds(8 * k, 8)], inp.at[:, pl.ds(8 * k, 8)], in_sem.at[k])
        for k in range(4)
    ]
    for k in LOADS:
        loads[k].start()
    pot_load = pltpu.make_async_copy(pot_hbm.at[0], pot, pot_sem)
    pot_load.start()

    barrier = pltpu.get_barrier_semaphore()
    for dev in columns + planes:
        pl.semaphore_signal(barrier, inc=1, device_id=dev, device_id_type=MESH)

    @pl.when(by == 1)
    def _():
        pl.semaphore_signal(barrier, inc=1, device_id=upper["y"], device_id_type=MESH)

    @pl.when(by == 2)
    def _():
        pl.semaphore_signal(barrier, inc=1, device_id=lower["y"], device_id_type=MESH)

    crosses = (is_a & (bz == 1)) | (is_b & (bz == 0))

    @pl.when(crosses)
    def _():
        pl.semaphore_signal(barrier, inc=1, device_id=crossed, device_id_type=MESH)

    for buf in (e0, e1):
        @pl.when(bx == 0)
        def _(buf=buf):
            buf[0:HALO] = jnp.zeros((HALO, NY + 12, 8, 128), F32)

        @pl.when(bx == 3)
        def _(buf=buf):
            buf[NX + HALO:] = jnp.zeros((HALO, NY + 12, 8, 128), F32)

        @pl.when(by == 0)
        def _(buf=buf):
            @pl.loop(0, NX)
            def _(x):
                buf[HALO + x, 0:HALO] = jnp.zeros((HALO, 8, 128), F32)

        @pl.when(by == 3)
        def _(buf=buf):
            @pl.loop(0, NX)
            def _(x):
                buf[HALO + x, NY + HALO:] = jnp.zeros((HALO, 8, 128), F32)

    @pl.when(bx == 3)
    def _():
        tx[...] = jnp.zeros_like(tx)

    @pl.when(by == 3)
    def _():
        @pl.loop(0, 16)
        def _(x):
            for s in (0, 1):
                pf[s, x, NY:] = jnp.zeros((HALO, 8, 128), F32)

    @pl.when(is_b & (bz == 1))
    def _():
        zp[...] = jnp.zeros_like(zp)

    pl.semaphore_wait(barrier, 22 + jnp.where((by == 1) | (by == 2), 1, 0) + jnp.where(crosses, 1, 0))

    def y_copy(stage, buf, k, side):
        rows = pl.ds(HALO + CHUNK * k, CHUNK)
        src, dst = ((HALO, NY + HALO), (NY, 0))[side]
        return pltpu.make_async_remote_copy(
            src_ref=buf.at[rows, pl.ds(src, HALO)], dst_ref=buf.at[rows, pl.ds(dst, HALO)],
            send_sem=y_ss.at[stage, k, side], recv_sem=y_rs.at[stage, k, side],
            device_id=(lower, upper)[side]["y"], device_id_type=MESH)

    def x_copy(stage, buf, side, r):
        src, dst = ((HALO, NX + HALO), (NX, 0))[side]
        cols = pl.ds(HALO + ROWS[r][0], ROWS[r][1])
        return pltpu.make_async_remote_copy(
            src_ref=buf.at[pl.ds(src, HALO), cols], dst_ref=buf.at[pl.ds(dst, HALO), cols],
            send_sem=x_ss.at[stage, side, r], recv_sem=x_rs.at[stage, side, r],
            device_id=(lower, upper)[side]["x"], device_id_type=MESH)

    def z_copies(stage, part):
        return [
            pltpu.make_async_remote_copy(
                src_ref=zf.at[stage, :, pl.ds(*ROWS[r])], dst_ref=zh.at[stage, :, pl.ds(*ROWS[r])],
                send_sem=z_ss.at[stage, r], recv_sem=z_rs.at[stage, r],
                device_id=(d + 1 - 2 * bz, o), device_id_type=MESH)
            for r in PARTS[part]
        ]

    def sends(axis, side):
        return (has_lower, has_upper)[side][axis]

    def receives(axis, side):
        return (has_upper, has_lower)[side][axis]

    queue = [(n, buf, k) for n, buf in ((0, e0), (1, e1)) for k in ORDERS[n]]
    sent, passed = [], []

    def direct(q, side):
        if q % 2 == 0:
            return sends("y", side)
        return ((by == 1) | (by == 3), (by == 0) | (by == 2))[side]

    def relayed(q, side):
        n, buf, k = queue[q]
        return pltpu.make_async_remote_copy(
            src_ref=buf.at[pl.ds(HALO + CHUNK * k, CHUNK), pl.ds((HALO, NY)[side], HALO)],
            dst_ref=rl.at[n, q % 8 // 2], send_sem=r_ss.at[n, q % 8 // 2], recv_sem=r_rs.at[n, q % 8 // 2],
            device_id=zl, device_id_type=MESH)

    def passing(q, side):
        n, buf, k = queue[q]
        return pltpu.make_async_remote_copy(
            src_ref=rl.at[n, q % 8 // 2],
            dst_ref=buf.at[pl.ds(HALO + CHUNK * k, CHUNK), pl.ds((NY + HALO, 0)[side], HALO)],
            send_sem=p_ss.at[n, q % 8 // 2], recv_sem=y_rs.at[n, k, side],
            device_id=(upper, lower)[side]["y"], device_id_type=MESH)

    def each_send(q, act):
        for side in (0, 1):
            when(direct(q, side), lambda: act(y_copy(*queue[q], side)))
            if q % 2:
                when(by == 2 - side, lambda: act(relayed(q, side)))

    def pass_on(q):
        for side in (0, 1):
            def go():
                relayed(q, side).wait_recv()
                passing(q, side).start()
            when(by == 3 * side, go)

    def pump(last, done=-1):
        while len(sent) <= min(last, len(queue) - 1):
            q = len(sent)
            if q >= 8 and ORDERS[0].index(queue[q][2]) > done:
                break
            if q >= FLIGHT:
                each_send(q - FLIGHT, lambda c: c.wait_send())
            each_send(q, lambda c: c.start())
            sent.append(q)
        while 2 * len(passed) + 1 < min(len(sent) - 1, last) or (
                last >= len(queue) and len(sent) == len(queue) and len(passed) < 8):
            q = 2 * len(passed) + 1
            pass_on(q)
            passed.append(q)

    def wait_y(q):
        for side in (0, 1):
            when(receives("y", side), lambda: y_copy(*queue[q], side).wait_recv())

    def send_x(stage, buf, side, part):
        for r in PARTS[part]:
            when(sends("x", side), lambda: x_copy(stage, buf, side, r).start())

    def wait_x(stage, buf, part):
        for side in (0, 1):
            for r in PARTS[part]:
                when(receives("x", side), lambda: x_copy(stage, buf, side, r).wait_recv())

    lane = lax.broadcasted_iota(jnp.int32, (8, 128), 1)

    def pack_z(stage, buf, part):
        first = jnp.where(bz == 0, NZ - HALO, 0)
        shifts = [lax.rem(8 * x + 128 - first, 128) for x in range(16)]

        def rows(half, y, n):
            for j in range(n):
                total = None
                for x in range(16):
                    moved = pltpu.roll(buf[HALO + 16 * half + x, HALO + y + j], shifts[x], axis=1)
                    total = moved if total is None else jnp.where(lane // 8 == x, moved, total)
                zf[stage, half, y + j] = total

        @pl.loop(0, 4)
        def _(t):
            if part == 0:
                rows(t // 2, 6 + 6 * (t % 2), 6)
            else:
                rows(t // 2, 18 * (t % 2), 6)
        for copy in z_copies(stage, part):
            copy.start()

    def pack_top(first, dst, slot, half):
        @pl.loop(0, NY // 4)
        def _(t):
            for j in range(4):
                total = None
                for i in range(16):
                    moved = pltpu.roll(
                        e2[8 * half + i // 2 + 16 * (i % 2), 4 * t + j],
                        (8 * i + 128 - first) % 128, axis=1)
                    total = moved if total is None else jnp.where(lane // 8 == i, moved, total)
                dst[slot, half, 4 * t + j] = total

    def z_own(buf, part):
        @pl.loop(0, NX // 4)
        def _(t):
            at = pl.ds(4 * t, 4)
            v = [buf[pl.ds(HALO + 4 * t, 4), pl.ds(HALO + ROWS[r][0], ROWS[r][1])] for r in PARTS[part]]
            v = jnp.concatenate(v, axis=1) if part else v[0]
            r = jnp.dot(split_wide(v.reshape(4 * 12 * 8, 128)), zmat_ref[0], preferred_element_type=F32)
            r = (r[:, :128] + r[:, 128:]).reshape(4, 12, 8, 128)
            if part == 0:
                zacc[at, pl.ds(6, 12)] = r
            else:
                zacc[at, pl.ds(0, 6)] = r[:, :6]
                zacc[at, pl.ds(18, 6)] = r[:, 6:]

    def z_halo(stage, part):
        for copy in z_copies(stage, part):
            copy.wait_recv()

        @pl.loop(0, NX // 4)
        def _(t):
            parts = []
            for j in range(4):
                x = 4 * t + j
                packed = [zh[stage, x // 16, pl.ds(*ROWS[r])].reshape(ROWS[r][1] * 8, 128)
                          for r in PARTS[part]]
                packed = jnp.concatenate(packed, axis=0) if part else packed[0]
                parts.append(pltpu.roll(packed, lax.rem(128 - 8 * lax.rem(x, 16), 128), axis=1))
            v = jnp.concatenate(parts, axis=0)
            r = jnp.dot(split_wide(v), zmat_ref[1 + bz], preferred_element_type=F32)
            r = (r[:, :128] + r[:, 128:]).reshape(4, 12, 8, 128)
            at = pl.ds(4 * t, 4)
            if part == 0:
                zacc[at, pl.ds(6, 12)] += r
            else:
                zacc[at, pl.ds(0, 6)] += r[:, :6]
                zacc[at, pl.ds(18, 6)] += r[:, 6:]

    def rows_of(src, dst, off, x, y, scale, shift, prev, prev_scale):
        def at(dx, dy):
            return src[x + HALO + dx, pl.ds(y + HALO + dy, HALO)]

        total = scale * zacc[x, pl.ds(y, HALO)]
        total += (scale * potb[x, pl.ds(y, HALO)] + (scale * CENTRE + shift)) * at(0, 0)
        for m in range(1, HALO + 1):
            near = (at(m, 0) + at(-m, 0)) + (at(0, m) + at(0, -m))
            total += (scale * KINETIC * WEIGHTS[m - 1]) * near
        if prev is not None:
            total -= prev_scale * prev[x + HALO, pl.ds(y + HALO, HALO)]
        dst[x + off, pl.ds(y + off, HALO)] = total

    def stage_rows(lo, hi, ys_, *args):
        @pl.loop(lo, hi)
        def _(x):
            for y in ys_:
                rows_of(*args[:3], x, y, *args[3:])

    def faces(n, *args):
        for j, k in enumerate(ORDERS[n]):
            wait_y(8 * n + j)
            stage_rows(CHUNK * k, CHUNK * k + CHUNK, (0, 18), *args)
            pump(8 * n + j + FLIGHT, 8 * n + j)
            yield j, k

    flat_in = inp.reshape(NO * NX * NY, 128)
    for i, k in enumerate(LOADS):
        loads[k].wait()

        @pl.loop(8 * k, 8 * k + 8)
        def _(x):
            for y in range(NY):
                e0[HALO + x, HALO + y] = flat_in[pl.ds(x * NY + y, 8, stride=NX * NY), :]
        if i < 2:
            pump(i)
    for side in (0, 1):
        for part_ in (0, 1):
            send_x(0, e0, side, part_)
    pump(2)
    pack_z(0, e0, 0)
    pack_z(0, e0, 1)
    pump(3)
    pot_load.wait()

    @pl.loop(0, NX)
    def _(x):
        for y in range(NY):
            potb[x, y] = jnp.broadcast_to(pot[x, pl.ds(y, 1)], (8, 128))

    first = (e0, e1, HALO, SIGMA1 / HALF, -SIGMA1 / HALF * MIDDLE, None, 0.0)
    z_own(e0, 0)
    z_own(e0, 1)
    z_halo(0, 0)
    stage_rows(HALO, NX - HALO, (6, 12), *first)
    pump(4)
    wait_x(0, e0, 0)
    stage_rows(0, HALO, (6, 12), *first)
    stage_rows(NX - HALO, NX, (6, 12), *first)
    send_x(1, e1, 0, 0)
    send_x(1, e1, 1, 0)
    pack_z(1, e1, 0)
    z_own(e1, 0)
    z_halo(0, 1)

    @pl.loop(0, 16)
    def _(x):
        for y in range(NY):
            one, two = potb[x, y], potb[16 + x, y]
            low = jnp.where(lane < 64, one, pltpu.roll(two, 64, axis=1))
            high = jnp.where(lane < 64, pltpu.roll(one, 64, axis=1), two)
            potp[x, y] = jnp.where(is_a, low, high)

    wait_x(0, e0, 1)
    z_halo(1, 0)
    wait_x(1, e1, 0)

    def pack_rows(lo, hi, rows):
        @pl.loop(lo, hi)
        def _(x):
            for y, n in rows:
                for j in range(y, y + n):
                    one, two = e2[x, j], e2[16 + x, j]
                    low = jnp.where(lane < 64, one, pltpu.roll(two, 64, axis=1))
                    high = jnp.where(lane < 64, pltpu.roll(one, 64, axis=1), two)
                    pf[0, x, j] = jnp.where(is_a, low, high)
                    sb[x, j] = jnp.where(is_a, high, low)

    def piece(c, r):
        return pl.ds(4 * c, 4), pl.ds(*ROWS[r])

    def chip_copy(c, r):
        p = piece(c, r)
        return pltpu.make_async_remote_copy(
            src_ref=sb.at[p], dst_ref=pf.at[(1,) + p], send_sem=g_ss.at[c, r], recv_sem=g_rs.at[c, r],
            device_id=other_chip, device_id_type=MESH)

    def core_copy(s, c, r):
        p = (s,) + piece(c, r)
        return pltpu.make_async_remote_copy(
            src_ref=pf.at[p], dst_ref=ocp.at[p], send_sem=c_ss.at[s, c, r], recv_sem=c_rs.at[s, c, r],
            device_id=other_core, device_id_type=MESH)

    def ty_copy(s, c):
        xs = pl.ds(4 * c, 4)
        return pltpu.make_async_remote_copy(
            src_ref=pf.at[s, xs, pl.ds(0, HALO)], dst_ref=pf.at[s, xs, pl.ds(NY, HALO)],
            send_sem=ty_ss.at[s, c], recv_sem=ty_rs.at[s, c], device_id=lower["y"], device_id_type=MESH)

    PAIRS = ((6, 12), (0, 18))

    def tx_copy(s, half):
        rows = pl.ds(6 * half, 6)
        return pltpu.make_async_remote_copy(
            src_ref=tp.at[s, :, rows], dst_ref=tx.at[s, :, rows],
            send_sem=tx_ss.at[s, half], recv_sem=tx_rs.at[s, half], device_id=lower["x"], device_id_type=MESH)

    def send_tx(s, half):
        one, two = PAIRS[half]

        @pl.loop(0, HALO)
        def _(x):
            for j in range(6):
                tp[s, x, 6 * half + j] = jnp.where(
                    lane < 64, pf[s, x, one + j], pltpu.roll(pf[s, x, two + j], 64, axis=1))
        when(has_lower["x"], lambda: tx_copy(s, half).start())

    def zp_copy(src, slot, dev):
        return pltpu.make_async_remote_copy(
            src_ref=zs.at[src], dst_ref=zp.at[slot], send_sem=zp_ss.at[src], recv_sem=zp_rs.at[slot],
            device_id=dev, device_id_type=MESH)

    def down(s, c, r):
        if r == 1:
            when(has_lower["y"], lambda: ty_copy(s, c).start())
        if c == 1 and r != 1:
            send_tx(s, r // 2)
        core_copy(s, c, r).start()

    def arrived(c, r):
        chip_copy(c, r).wait_recv()
        down(1, c, r)

    s2 = 2.0 * SIGMA2 / HALF
    second = (e1, e2, 0, s2, -s2 * MIDDLE, e0, SIGMA1 * SIGMA2)
    for j, k in faces(0, *first):
        stage_rows(CHUNK * k, CHUNK * k + CHUNK, (6, 12), *second)
        if j % 2:
            c = k % 4
            pack_rows(4 * c, 4 * c + 4, ROWS[:1])
            chip_copy(c, 0).start()
            down(0, c, 0)
        if j == 3:
            send_x(1, e1, 1, 1)
        if j == 6:
            send_x(1, e1, 0, 1)

    def tops(half):
        @pl.when(is_a)
        def _():
            pack_top(64, zp, 0, half)

            @pl.when(bz == 1)
            def _():
                pack_top(0, zs, 1, half)

        @pl.when(is_b)
        def _():
            pack_top(64, zs, 0, half)

            @pl.when(bz == 1)
            def _():
                pack_top(0, zs, 1, half)

    def leave(c):
        @pl.loop(0, 2)
        def _(g):
            @pl.loop(0, CHUNK)
            def _(x):
                at = 16 * g + 4 * c + x
                for orb in range(NO):
                    inp[orb, at] = e2[at, :, orb]

    pack_z(1, e1, 1)
    z_own(e1, 1)
    wait_x(1, e1, 1)
    z_halo(1, 1)
    early = [(3, 0), (2, 0), (0, 0), (1, 0), (0, 1), (0, 2), (1, 1), (1, 2), (3, 1), (3, 2), (2, 1), (2, 2)]
    for j, k in faces(1, *second):
        if j % 2:
            c = k % 4
            pack_rows(4 * c, 4 * c + 4, ROWS[1:])
            for r in (1, 2):
                chip_copy(c, r).start()
            for r in (1, 2):
                down(0, c, r)
            for _ in range(2):
                arrived(*early.pop(0))

            if c != 2:
                leave(c)
        if j == 3:
            tops(0)
    tops(1)

    @pl.when(is_a & (bz == 1))
    def _():
        zp_copy(1, 1, crossed).start()

    @pl.when(is_b)
    def _():
        zp_copy(0, 1, other_chip).start()

    @pl.when(is_b & (bz == 1))
    def _():
        zp_copy(1, 0, (d - 1, o)).start()

    def z_upper(s):
        @pl.loop(0, 4)
        def _(t):
            v = pf[s, pl.ds(4 * t, 4), pl.ds(0, NY)].reshape(4 * NY * 8, 128)
            parts = []
            for j in range(4):
                x = 4 * t + j
                packed = zp[s, x // 8].reshape(NY * 8, 128)
                parts.append(pltpu.roll(packed, lax.rem(128 - 16 * lax.rem(x, 8), 128), axis=1))
            r = jnp.dot(split_wide(v), zmat_ref[3], preferred_element_type=F32)
            r += jnp.dot(split_wide(jnp.concatenate(parts, axis=0)), zmat_ref[4], preferred_element_type=F32)
            zacc[pl.ds(16 * s + 4 * t, 4)] = (r[:, :128] + r[:, 128:]).reshape(4, NY, 8, 128)

    def shift_x(s):
        @pl.loop(0, HALO)
        def _(x):
            for half, (one, two) in enumerate(PAIRS):
                for j in range(6):
                    there = tx[s, x, 6 * half + j]
                    both = jnp.where(lane < 64, there, pf[s, x, one + j])
                    pf[s, 16 + x, one + j] = pltpu.roll(both, 64, axis=1)
                    pf[s, 16 + x, two + j] = jnp.where(
                        lane < 64, pltpu.roll(pf[s, x, two + j], 64, axis=1), there)

    def half_rows(s, ys_):
        @pl.loop(0, 16)
        def _(x):
            for y in ys_:
                total = zacc[16 * s + x, pl.ds(y, HALO)]
                total += (0.5 * CENTRE + 0.5 * potp[x, pl.ds(y, HALO)]) * pf[s, x, pl.ds(y, HALO)]
                for m in range(1, HALO + 1):
                    near = pf[s, x + m, pl.ds(y, HALO)] + pf[s, x, pl.ds(y + m, HALO)]
                    total += (KINETIC * WEIGHTS[m - 1]) * near
                hp[s, x, pl.ds(y, HALO)] = total

    @pl.when(is_a)
    def _():
        zp_copy(0, 1, other_chip).wait_recv()

    @pl.when(is_b & (bz == 0))
    def _():
        zp_copy(1, 0, other_chip).wait_recv()
        zp_copy(1, 1, other_chip).wait_recv()

    def upper_rows(s):
        for half in (0, 1):
            when(has_upper["x"], lambda: tx_copy(s, half).wait_recv())
        shift_x(s)
        half_rows(s, (0, 6, 12))

    z_upper(0)
    while early:
        arrived(*early.pop(0))
    leave(2)
    out_copy = pltpu.make_async_copy(inp, out_hbm.at[:, 0], out_sem)
    out_copy.start()
    upper_rows(0)
    z_upper(1)
    upper_rows(1)

    for s in (0, 1):
        for c in range(4):
            for r in range(3):
                core_copy(s, c, r).wait_recv()

    def grams(rows):
        def halves(ref, x):
            v = jnp.concatenate([flat(ref[s, x, rows]) for s in (0, 1)], axis=0)
            hi = v.astype(BF16)
            return hi, (v - hi.astype(F32)).astype(BF16)

        def body(x, total):
            (mh, ml), (oh, ol), (hh, hl) = halves(pf, x), halves(ocp, x), halves(hp, x)
            left = jnp.concatenate([mh, oh, ml, ol], axis=0)
            right = jnp.concatenate([mh, hh, ml, hl], axis=0)
            full = lax.dot_general(left, right, (((1,), (1,)), ((), ())), preferred_element_type=F32)
            return total + ((full[:32, :32] + full[32:, :32]) + (full[:32, 32:] + full[32:, 32:]))
        return body

    total = lax.fori_loop(0, 16, grams(pl.ds(0, 18)), jnp.zeros((32, 32), F32))
    for s in (0, 1):
        for c in range(4):
            when(has_upper["y"], lambda: ty_copy(s, c).wait_recv())
        half_rows(s, (18,))
    total = lax.fori_loop(0, 16, grams(pl.ds(18, 6)), total)

    def place(block, starts):
        n = block.shape[1]
        r = lax.broadcasted_iota(jnp.int32, (n, 128), 0)
        c = lax.broadcasted_iota(jnp.int32, (n, 128), 1)
        chosen = jnp.zeros((n, 128), jnp.bool_)
        for j, s in enumerate(starts):
            chosen = chosen | ((r // 8 == j) & (c == s + r % 8))
        return jnp.dot(block, chosen.astype(F32), precision=HIGH, preferred_element_type=F32)

    o_core = o + 1 - 2 * core
    o_chip = (o + 2) % 4
    placed = place(total, (8 * o, 8 * o_chip, 32 + 8 * o, 32 + 8 * o_chip))
    for j, orbital in enumerate((o, o_chip, o_core, o_core + 2 - 4 * chip)):
        part[pl.ds(pl.multiple_of(8 * orbital, 8), 8), :] = placed[8 * j:8 * j + 8]

    def reduce(block, ar, ss, rs, mine, source, partners):
        ar[mine] = block
        copies = []
        for i, dev in enumerate(partners):
            copies.append(pltpu.make_async_remote_copy(
                src_ref=ar.at[mine], dst_ref=ar.at[mine], send_sem=ss.at[i], recv_sem=rs.at[mine],
                device_id=dev, device_id_type=MESH))
            copies[-1].start()
        for i, dev in enumerate(partners):
            at = source(i + 1)
            pltpu.make_async_remote_copy(
                src_ref=ar.at[at], dst_ref=ar.at[at], send_sem=ss.at[i], recv_sem=rs.at[at],
                device_id=dev, device_id_type=MESH).wait_recv()
        total = ar[0]
        for i in range(1, len(partners) + 1):
            total += ar[i]
        for c in copies:
            c.wait_send()
        return total

    folded = part[0:16, :] + pltpu.roll(part[16:32, :], 64, axis=1)
    folded = reduce(folded, ar1, a1_ss, a1_rs, 4 * pzl + o,
                    lambda i: 4 * ((pzl + i // 4) % 2) + (o + i) % 4, columns)
    folded = reduce(folded, ar2, a2_ss, a2_rs, 4 * bx + px,
                    lambda i: 4 * ((bx + i // 4) % 4) + (px + i) % 4, planes)
    part[0:16, :] = folded
    part[16:32, :] = pltpu.roll(folded, 64, axis=1)

    square = part[...]
    r = lax.broadcasted_iota(jnp.int32, (32, 32), 0)
    c = lax.broadcasted_iota(jnp.int32, (32, 32), 1)
    eye = (r == c).astype(F32)
    cor_ref[...] = square[:, 0:32] * (1.0 / CELLS)
    m = square[:, 32:64]
    t = lax.dot_general(m, eye, (((0,), (0,)), ((), ())), precision=HIGH, preferred_element_type=F32)
    sub_ref[...] = (m + t) * (1.0 / (CELLS * HALF))

    out_copy.wait()
    for q in range(len(queue) - FLIGHT, len(queue)):
        each_send(q, lambda c: c.wait_send())
    for q in passed:
        for side in (0, 1):
            when(by == 3 * side, lambda: passing(q, side).wait_send())
    for n, buf in ((0, e0), (1, e1)):
        for side in (0, 1):
            for r in range(3):
                when(sends("x", side), lambda: x_copy(n, buf, side, r).wait_send())
        for part_ in (0, 1):
            for copy in z_copies(n, part_):
                copy.wait_send()
    for c in range(4):
        for r in range(3):
            chip_copy(c, r).wait_send()
            for s in (0, 1):
                core_copy(s, c, r).wait_send()
        for s in (0, 1):
            when(has_lower["y"], lambda: ty_copy(s, c).wait_send())
    for s in (0, 1):
        for half in (0, 1):
            when(has_lower["x"], lambda: tx_copy(s, half).wait_send())
    when(is_b, lambda: zp_copy(0, 1, other_chip).wait_send())
    when(bz == 1, lambda: zp_copy(1, 1, other_chip).wait_send())


def shards(orbitals, potential):
    zmat = jnp.asarray(z_matrices())
    field = (NX + 12, NY + 12, 8, 128)
    vm = lambda *shape: pltpu.VMEM(shape, F32)
    dma = lambda *shape: pltpu.SemaphoreType.DMA(shape)
    out, cor, sub = pl.pallas_call(
        kernel,
        out_shape=(
            jax.ShapeDtypeStruct((NO, 1, NX, NY, NZ), F32),
            jax.ShapeDtypeStruct((32, 32), F32),
            jax.ShapeDtypeStruct((32, 32), F32),
        ),
        in_specs=[pl.BlockSpec(memory_space=pl.ANY)] * 2 + [pl.BlockSpec(memory_space=pltpu.VMEM)],
        out_specs=(pl.BlockSpec(memory_space=pl.ANY),) + (pl.BlockSpec(memory_space=pltpu.VMEM),) * 2,
        scratch_shapes=[
            vm(NO, NX, NY, NZ), vm(NX, NY, NZ), vm(*field), vm(*field), vm(NX, NY, 8, 128),
            vm(NX, NY, 8, 128), vm(NX, NY, 8, 128),
            vm(2, 2, NY, 8, 128), vm(2, 2, NY, 8, 128), vm(2, 4, CHUNK, HALO, 8, 128),
            vm(2, 16 + HALO, NY + HALO, 8, 128), vm(16, NY, 8, 128), vm(2, 16, NY, 8, 128),
            vm(2, 16, NY, 8, 128), vm(2, HALO, 12, 8, 128), vm(2, HALO, 12, 8, 128), vm(16, NY, 8, 128),
            vm(2, 2, NY, 8, 128), vm(2, 2, NY, 8, 128),
            vm(32, 128), vm(8, 16, 128), vm(16, 16, 128),
            dma(4), pltpu.SemaphoreType.DMA, pltpu.SemaphoreType.DMA,
            dma(2, 8, 2), dma(2, 8, 2), dma(2, 4), dma(2, 4), dma(2, 4), dma(2, 2, 3), dma(2, 2, 3), dma(2, 3), dma(2, 3),
            dma(2, 4, 3), dma(2, 4, 3), dma(4, 3), dma(4, 3),
            dma(2, 4), dma(2, 4), dma(2, 3), dma(2, 3), dma(2), dma(2),
            dma(7), dma(8), dma(15), dma(16),
        ],
        compiler_params=pltpu.CompilerParams(
            collective_id=0, has_side_effects=True, vmem_limit_bytes=47 * 2**20),
        name="filter_and_subspace",
    )(orbitals, potential, zmat)
    return out, cor, sub


def solution(mesh):
    placed = (P("orb", "dom", None, None, None), P("dom", None, None, None))
    return jax.shard_map(
        shards,
        mesh=mesh,
        in_specs=placed,
        out_specs=(P("orb", "dom", None, None, None), P(), P()),
        check_vma=False,
    )
```

```python
import math

import jax
import jax.numpy as jnp
import numpy as np
from jax import lax
from jax.experimental import pallas as pl
from jax.experimental.pallas import tpu as pltpu
from jax.sharding import PartitionSpec as P

HALO = 6
SPACING = 0.5
UPPER = 44.0
CUTOFF = 4.0
LOWEST = -1.0
NX, NY, NZ, NO = 32, 24, 128, 8
CELLS = 3145728
CHUNK = 4
ORDERS = ((3, 7, 2, 6, 0, 4, 1, 5), (0, 4, 1, 5, 3, 7, 2, 6))
FLIGHT = 4
LOADS = (1, 3, 0, 2)
ROWS = ((6, 12), (0, 6), (18, 6))
PARTS = ((0,), (1, 2))
MESH = pl.DeviceIdType.MESH
F32, BF16 = jnp.float32, jnp.bfloat16
HIGH = lax.Precision.HIGHEST


def stencil_weights():
    return [
        2.0 * (-1.0) ** (m + 1) * math.factorial(HALO) ** 2
        / (m * m * math.factorial(HALO - m) * math.factorial(HALO + m))
        for m in range(1, HALO + 1)
    ]


WEIGHTS = stencil_weights()
KINETIC = -0.5 / SPACING**2
CENTRE = KINETIC * 3.0 * (-2.0 * sum(WEIGHTS))
HALF = (UPPER - CUTOFF) / 2.0
MIDDLE = (UPPER + CUTOFF) / 2.0
SIGMA1 = HALF / (LOWEST - MIDDLE)
SIGMA2 = 1.0 / (2.0 / SIGMA1 - SIGMA1)


def doubled(matrix):
    wide = matrix.astype(np.float32)
    hi = wide.astype(BF16)
    lo = (wide - hi.astype(np.float32)).astype(BF16)
    row = np.concatenate([hi, lo], axis=1)
    return np.concatenate([row, row], axis=0)


def z_matrices():
    own = np.zeros((NZ, NZ))
    above = np.zeros((NZ, NZ))
    below = np.zeros((NZ, NZ))
    for z in range(NZ):
        for m in range(1, HALO + 1):
            weight = KINETIC * WEIGHTS[m - 1]
            for k in (z - m, z + m):
                if 0 <= k < NZ:
                    own[k, z] = weight
                elif k >= NZ:
                    above[k - NZ, z] = weight
                else:
                    below[k + HALO, z] = weight
    upper = np.zeros((NZ, NZ))
    top = np.zeros((NZ, NZ))
    for z in range(NZ):
        g, at = z // 64, z % 64
        for m in range(1, HALO + 1):
            weight = KINETIC * WEIGHTS[m - 1]
            if at + m < 64:
                upper[z + m, z] = weight
            else:
                top[8 * g + at + m - 64, z] = weight
    return np.stack([doubled(v) for v in (own, above, below, upper, top)])


def split_wide(v):
    hi = v.astype(BF16)
    lo = (v - hi.astype(F32)).astype(BF16)
    return jnp.concatenate([hi, lo], axis=1)


def flat(block):
    return jnp.concatenate([block[j] for j in range(block.shape[0])], axis=1)


def kernel(orb_hbm, pot_hbm, zmat_ref, out_hbm, cor_ref, sub_ref,
           inp, pot, e0, e1, e2, zacc, potb, zf, zh, rl, pf, sb, ocp, hp, tp, tx, potp, zs, zp, part, ar1, ar2,
           in_sem, pot_sem, out_sem,
           y_ss, y_rs, r_ss, r_rs, p_ss, x_ss, x_rs, z_ss, z_rs, c_ss, c_rs, g_ss, g_rs,
           ty_ss, ty_rs, tx_ss, tx_rs, zp_ss, zp_rs, a1_ss, a1_rs, a2_ss, a2_rs):
    d = lax.axis_index("dom")
    o = lax.axis_index("orb")
    bx, by, bz = d // 8, (d // 2) % 4, d % 2
    chip, core = o // 2, o % 2
    px, pzl = d % 4, (d // 4) % 2
    other_core = (d, o + 1 - 2 * core)
    other_chip = (d, (o + 2) % 4)
    column = lambda i: ((d + 4 * (i // 4)) % 8 + 8 * bx, (o + i) % 4)
    plane = lambda i: (((bx + i // 4) % 4) * 8 + 4 * pzl + (px + i) % 4, o)
    columns = [column(i) for i in range(1, 8)]
    planes = [plane(i) for i in range(1, 16)]
    zl = (d + 4 - 8 * pzl, o)
    crossed = (d + 1 - 2 * bz, (o + 2) % 4)
    lower = {"x": (d - 8, o), "y": (d - 2, o)}
    upper = {"x": (d + 8, o), "y": (d + 2, o)}
    has_lower = {"x": bx > 0, "y": by > 0}
    has_upper = {"x": bx < 3, "y": by < 3}
    is_a, is_b = chip == 0, chip == 1

    def when(cond, fn):
        if cond is None:
            fn()
        else:
            pl.when(cond)(lambda: fn() and None)

    loads = [
        pltpu.make_async_copy(
            orb_hbm.at[:, 0, pl.ds(8 * k, 8)], inp.at[:, pl.ds(8 * k, 8)], in_sem.at[k])
        for k in range(4)
    ]
    for k in LOADS:
        loads[k].start()
    pot_load = pltpu.make_async_copy(pot_hbm.at[0], pot, pot_sem)
    pot_load.start()

    barrier = pltpu.get_barrier_semaphore()
    for dev in columns + planes:
        pl.semaphore_signal(barrier, inc=1, device_id=dev, device_id_type=MESH)

    @pl.when(by == 1)
    def _():
        pl.semaphore_signal(barrier, inc=1, device_id=upper["y"], device_id_type=MESH)

    @pl.when(by == 2)
    def _():
        pl.semaphore_signal(barrier, inc=1, device_id=lower["y"], device_id_type=MESH)

    crosses = (is_a & (bz == 1)) | (is_b & (bz == 0))

    @pl.when(crosses)
    def _():
        pl.semaphore_signal(barrier, inc=1, device_id=crossed, device_id_type=MESH)

    for buf in (e0, e1):
        @pl.when(bx == 0)
        def _(buf=buf):
            buf[0:HALO] = jnp.zeros((HALO, NY + 12, 8, 128), F32)

        @pl.when(bx == 3)
        def _(buf=buf):
            buf[NX + HALO:] = jnp.zeros((HALO, NY + 12, 8, 128), F32)

        @pl.when(by == 0)
        def _(buf=buf):
            @pl.loop(0, NX)
            def _(x):
                buf[HALO + x, 0:HALO] = jnp.zeros((HALO, 8, 128), F32)

        @pl.when(by == 3)
        def _(buf=buf):
            @pl.loop(0, NX)
            def _(x):
                buf[HALO + x, NY + HALO:] = jnp.zeros((HALO, 8, 128), F32)

    @pl.when(bx == 3)
    def _():
        tx[...] = jnp.zeros_like(tx)

    @pl.when(by == 3)
    def _():
        @pl.loop(0, 16)
        def _(x):
            for s in (0, 1):
                pf[s, x, NY:] = jnp.zeros((HALO, 8, 128), F32)

    @pl.when(is_b & (bz == 1))
    def _():
        zp[...] = jnp.zeros_like(zp)

    pl.semaphore_wait(barrier, 22 + jnp.where((by == 1) | (by == 2), 1, 0) + jnp.where(crosses, 1, 0))

    def y_copy(stage, buf, k, side):
        rows = pl.ds(HALO + CHUNK * k, CHUNK)
        src, dst = ((HALO, NY + HALO), (NY, 0))[side]
        return pltpu.make_async_remote_copy(
            src_ref=buf.at[rows, pl.ds(src, HALO)], dst_ref=buf.at[rows, pl.ds(dst, HALO)],
            send_sem=y_ss.at[stage, k, side], recv_sem=y_rs.at[stage, k, side],
            device_id=(lower, upper)[side]["y"], device_id_type=MESH)

    def x_copy(stage, buf, side, r):
        src, dst = ((HALO, NX + HALO), (NX, 0))[side]
        cols = pl.ds(HALO + ROWS[r][0], ROWS[r][1])
        return pltpu.make_async_remote_copy(
            src_ref=buf.at[pl.ds(src, HALO), cols], dst_ref=buf.at[pl.ds(dst, HALO), cols],
            send_sem=x_ss.at[stage, side, r], recv_sem=x_rs.at[stage, side, r],
            device_id=(lower, upper)[side]["x"], device_id_type=MESH)

    def z_copies(stage, part):
        return [
            pltpu.make_async_remote_copy(
                src_ref=zf.at[stage, :, pl.ds(*ROWS[r])], dst_ref=zh.at[stage, :, pl.ds(*ROWS[r])],
                send_sem=z_ss.at[stage, r], recv_sem=z_rs.at[stage, r],
                device_id=(d + 1 - 2 * bz, o), device_id_type=MESH)
            for r in PARTS[part]
        ]

    def sends(axis, side):
        return (has_lower, has_upper)[side][axis]

    def receives(axis, side):
        return (has_upper, has_lower)[side][axis]

    queue = [(n, buf, k) for n, buf in ((0, e0), (1, e1)) for k in ORDERS[n]]
    sent, passed = [], []

    def direct(q, side):
        if q % 2 == 0:
            return sends("y", side)
        return ((by == 1) | (by == 3), (by == 0) | (by == 2))[side]

    def relayed(q, side):
        n, buf, k = queue[q]
        return pltpu.make_async_remote_copy(
            src_ref=buf.at[pl.ds(HALO + CHUNK * k, CHUNK), pl.ds((HALO, NY)[side], HALO)],
            dst_ref=rl.at[n, q % 8 // 2], send_sem=r_ss.at[n, q % 8 // 2], recv_sem=r_rs.at[n, q % 8 // 2],
            device_id=zl, device_id_type=MESH)

    def passing(q, side):
        n, buf, k = queue[q]
        return pltpu.make_async_remote_copy(
            src_ref=rl.at[n, q % 8 // 2],
            dst_ref=buf.at[pl.ds(HALO + CHUNK * k, CHUNK), pl.ds((NY + HALO, 0)[side], HALO)],
            send_sem=p_ss.at[n, q % 8 // 2], recv_sem=y_rs.at[n, k, side],
            device_id=(upper, lower)[side]["y"], device_id_type=MESH)

    def each_send(q, act):
        for side in (0, 1):
            when(direct(q, side), lambda: act(y_copy(*queue[q], side)))
            if q % 2:
                when(by == 2 - side, lambda: act(relayed(q, side)))

    def pass_on(q):
        for side in (0, 1):
            def go():
                relayed(q, side).wait_recv()
                passing(q, side).start()
            when(by == 3 * side, go)

    def pump(last, done=-1):
        while len(sent) <= min(last, len(queue) - 1):
            q = len(sent)
            if q >= 8 and ORDERS[0].index(queue[q][2]) > done:
                break
            if q >= FLIGHT:
                each_send(q - FLIGHT, lambda c: c.wait_send())
            each_send(q, lambda c: c.start())
            sent.append(q)
        while 2 * len(passed) + 1 < min(len(sent) - 1, last) or (
                last >= len(queue) and len(sent) == len(queue) and len(passed) < 8):
            q = 2 * len(passed) + 1
            pass_on(q)
            passed.append(q)

    def wait_y(q):
        for side in (0, 1):
            when(receives("y", side), lambda: y_copy(*queue[q], side).wait_recv())

    def send_x(stage, buf, side, part):
        for r in PARTS[part]:
            when(sends("x", side), lambda: x_copy(stage, buf, side, r).start())

    def wait_x(stage, buf, part):
        for side in (0, 1):
            for r in PARTS[part]:
                when(receives("x", side), lambda: x_copy(stage, buf, side, r).wait_recv())

    lane = lax.broadcasted_iota(jnp.int32, (8, 128), 1)

    def pack_z(stage, buf, part):
        first = jnp.where(bz == 0, NZ - HALO, 0)
        shifts = [lax.rem(8 * x + 128 - first, 128) for x in range(16)]

        def rows(half, y, n):
            for j in range(n):
                total = None
                for x in range(16):
                    moved = pltpu.roll(buf[HALO + 16 * half + x, HALO + y + j], shifts[x], axis=1)
                    total = moved if total is None else jnp.where(lane // 8 == x, moved, total)
                zf[stage, half, y + j] = total

        @pl.loop(0, 4)
        def _(t):
            if part == 0:
                rows(t // 2, 6 + 6 * (t % 2), 6)
            else:
                rows(t // 2, 18 * (t % 2), 6)
        for copy in z_copies(stage, part):
            copy.start()

    def pack_top(first, dst, slot, half):
        @pl.loop(0, NY // 4)
        def _(t):
            for j in range(4):
                total = None
                for i in range(16):
                    moved = pltpu.roll(
                        e2[8 * half + i // 2 + 16 * (i % 2), 4 * t + j],
                        (8 * i + 128 - first) % 128, axis=1)
                    total = moved if total is None else jnp.where(lane // 8 == i, moved, total)
                dst[slot, half, 4 * t + j] = total

    def z_own(buf, part):
        @pl.loop(0, NX // 4)
        def _(t):
            at = pl.ds(4 * t, 4)
            v = [buf[pl.ds(HALO + 4 * t, 4), pl.ds(HALO + ROWS[r][0], ROWS[r][1])] for r in PARTS[part]]
            v = jnp.concatenate(v, axis=1) if part else v[0]
            r = jnp.dot(split_wide(v.reshape(4 * 12 * 8, 128)), zmat_ref[0], preferred_element_type=F32)
            r = (r[:, :128] + r[:, 128:]).reshape(4, 12, 8, 128)
            if part == 0:
                zacc[at, pl.ds(6, 12)] = r
            else:
                zacc[at, pl.ds(0, 6)] = r[:, :6]
                zacc[at, pl.ds(18, 6)] = r[:, 6:]

    def z_halo(stage, part):
        for copy in z_copies(stage, part):
            copy.wait_recv()

        @pl.loop(0, NX // 4)
        def _(t):
            parts = []
            for j in range(4):
                x = 4 * t + j
                packed = [zh[stage, x // 16, pl.ds(*ROWS[r])].reshape(ROWS[r][1] * 8, 128)
                          for r in PARTS[part]]
                packed = jnp.concatenate(packed, axis=0) if part else packed[0]
                parts.append(pltpu.roll(packed, lax.rem(128 - 8 * lax.rem(x, 16), 128), axis=1))
            v = jnp.concatenate(parts, axis=0)
            r = jnp.dot(split_wide(v), zmat_ref[1 + bz], preferred_element_type=F32)
            r = (r[:, :128] + r[:, 128:]).reshape(4, 12, 8, 128)
            at = pl.ds(4 * t, 4)
            if part == 0:
                zacc[at, pl.ds(6, 12)] += r
            else:
                zacc[at, pl.ds(0, 6)] += r[:, :6]
                zacc[at, pl.ds(18, 6)] += r[:, 6:]

    def rows_of(src, dst, off, x, y, scale, shift, prev, prev_scale):
        def at(dx, dy):
            return src[x + HALO + dx, pl.ds(y + HALO + dy, HALO)]

        total = scale * zacc[x, pl.ds(y, HALO)]
        total += (scale * potb[x, pl.ds(y, HALO)] + (scale * CENTRE + shift)) * at(0, 0)
        for m in range(1, HALO + 1):
            near = (at(m, 0) + at(-m, 0)) + (at(0, m) + at(0, -m))
            total += (scale * KINETIC * WEIGHTS[m - 1]) * near
        if prev is not None:
            total -= prev_scale * prev[x + HALO, pl.ds(y + HALO, HALO)]
        dst[x + off, pl.ds(y + off, HALO)] = total

    def stage_rows(lo, hi, ys_, *args):
        @pl.loop(lo, hi)
        def _(x):
            for y in ys_:
                rows_of(*args[:3], x, y, *args[3:])

    def faces(n, *args):
        for j, k in enumerate(ORDERS[n]):
            wait_y(8 * n + j)
            stage_rows(CHUNK * k, CHUNK * k + CHUNK, (0, 18), *args)
            pump(8 * n + j + FLIGHT, 8 * n + j)
            yield j, k

    flat_in = inp.reshape(NO * NX * NY, 128)
    for i, k in enumerate(LOADS):
        loads[k].wait()

        @pl.loop(8 * k, 8 * k + 8)
        def _(x):
            for y in range(NY):
                e0[HALO + x, HALO + y] = flat_in[pl.ds(x * NY + y, 8, stride=NX * NY), :]
        if i < 2:
            pump(i)
    for side in (0, 1):
        for part_ in (0, 1):
            send_x(0, e0, side, part_)
    pump(2)
    pack_z(0, e0, 0)
    pack_z(0, e0, 1)
    pump(3)
    pot_load.wait()

    @pl.loop(0, NX)
    def _(x):
        for y in range(NY):
            potb[x, y] = jnp.broadcast_to(pot[x, pl.ds(y, 1)], (8, 128))

    first = (e0, e1, HALO, SIGMA1 / HALF, -SIGMA1 / HALF * MIDDLE, None, 0.0)
    z_own(e0, 0)
    z_own(e0, 1)
    z_halo(0, 0)
    stage_rows(HALO, NX - HALO, (6, 12), *first)
    pump(4)
    wait_x(0, e0, 0)
    stage_rows(0, HALO, (6, 12), *first)
    stage_rows(NX - HALO, NX, (6, 12), *first)
    send_x(1, e1, 0, 0)
    send_x(1, e1, 1, 0)
    pump(5)
    pack_z(1, e1, 0)
    z_own(e1, 0)
    z_halo(0, 1)

    @pl.loop(0, 16)
    def _(x):
        for y in range(NY):
            one, two = potb[x, y], potb[16 + x, y]
            low = jnp.where(lane < 64, one, pltpu.roll(two, 64, axis=1))
            high = jnp.where(lane < 64, pltpu.roll(one, 64, axis=1), two)
            potp[x, y] = jnp.where(is_a, low, high)

    pump(6)
    wait_x(0, e0, 1)
    z_halo(1, 0)
    pump(7)
    wait_x(1, e1, 0)

    def pack_rows(lo, hi, rows):
        @pl.loop(lo, hi)
        def _(x):
            for y, n in rows:
                for j in range(y, y + n):
                    one, two = e2[x, j], e2[16 + x, j]
                    low = jnp.where(lane < 64, one, pltpu.roll(two, 64, axis=1))
                    high = jnp.where(lane < 64, pltpu.roll(one, 64, axis=1), two)
                    pf[0, x, j] = jnp.where(is_a, low, high)
                    sb[x, j] = jnp.where(is_a, high, low)

    def piece(c, r):
        return pl.ds(4 * c, 4), pl.ds(*ROWS[r])

    def chip_copy(c, r):
        p = piece(c, r)
        return pltpu.make_async_remote_copy(
            src_ref=sb.at[p], dst_ref=pf.at[(1,) + p], send_sem=g_ss.at[c, r], recv_sem=g_rs.at[c, r],
            device_id=other_chip, device_id_type=MESH)

    def core_copy(s, c, r):
        p = (s,) + piece(c, r)
        return pltpu.make_async_remote_copy(
            src_ref=pf.at[p], dst_ref=ocp.at[p], send_sem=c_ss.at[s, c, r], recv_sem=c_rs.at[s, c, r],
            device_id=other_core, device_id_type=MESH)

    def ty_copy(s, c):
        xs = pl.ds(4 * c, 4)
        return pltpu.make_async_remote_copy(
            src_ref=pf.at[s, xs, pl.ds(0, HALO)], dst_ref=pf.at[s, xs, pl.ds(NY, HALO)],
            send_sem=ty_ss.at[s, c], recv_sem=ty_rs.at[s, c], device_id=lower["y"], device_id_type=MESH)

    PAIRS = ((6, 12), (0, 18))

    def tx_copy(s, half):
        rows = pl.ds(6 * half, 6)
        return pltpu.make_async_remote_copy(
            src_ref=tp.at[s, :, rows], dst_ref=tx.at[s, :, rows],
            send_sem=tx_ss.at[s, half], recv_sem=tx_rs.at[s, half], device_id=lower["x"], device_id_type=MESH)

    def send_tx(s, half):
        one, two = PAIRS[half]

        @pl.loop(0, HALO)
        def _(x):
            for j in range(6):
                tp[s, x, 6 * half + j] = jnp.where(
                    lane < 64, pf[s, x, one + j], pltpu.roll(pf[s, x, two + j], 64, axis=1))
        when(has_lower["x"], lambda: tx_copy(s, half).start())

    def zp_copy(src, slot, dev):
        return pltpu.make_async_remote_copy(
            src_ref=zs.at[src], dst_ref=zp.at[slot], send_sem=zp_ss.at[src], recv_sem=zp_rs.at[slot],
            device_id=dev, device_id_type=MESH)

    def down(s, c, r):
        if r == 1:
            when(has_lower["y"], lambda: ty_copy(s, c).start())
        if c == 1 and r != 1:
            send_tx(s, r // 2)
        core_copy(s, c, r).start()

    def arrived(c, r):
        chip_copy(c, r).wait_recv()
        down(1, c, r)

    s2 = 2.0 * SIGMA2 / HALF
    second = (e1, e2, 0, s2, -s2 * MIDDLE, e0, SIGMA1 * SIGMA2)
    for j, k in faces(0, *first):
        stage_rows(CHUNK * k, CHUNK * k + CHUNK, (6, 12), *second)
        if j % 2:
            c = k % 4
            pack_rows(4 * c, 4 * c + 4, ROWS[:1])
            chip_copy(c, 0).start()
            down(0, c, 0)
        if j == 3:
            send_x(1, e1, 1, 1)
        if j == 6:
            send_x(1, e1, 0, 1)

    def tops(half):
        @pl.when(is_a)
        def _():
            pack_top(64, zp, 0, half)

            @pl.when(bz == 1)
            def _():
                pack_top(0, zs, 1, half)

        @pl.when(is_b)
        def _():
            pack_top(64, zs, 0, half)

            @pl.when(bz == 1)
            def _():
                pack_top(0, zs, 1, half)

    def leave(c):
        @pl.loop(0, 2)
        def _(g):
            @pl.loop(0, CHUNK)
            def _(x):
                at = 16 * g + 4 * c + x
                for orb in range(NO):
                    inp[orb, at] = e2[at, :, orb]

    pack_z(1, e1, 1)
    pump(12, 7)
    z_own(e1, 1)
    pump(13, 7)
    wait_x(1, e1, 1)
    z_halo(1, 1)
    early = [(3, 0), (2, 0), (0, 0), (1, 0), (0, 1), (0, 2), (1, 1), (1, 2), (3, 1), (3, 2), (2, 1), (2, 2)]
    for j, k in faces(1, *second):
        if j % 2:
            c = k % 4
            pack_rows(4 * c, 4 * c + 4, ROWS[1:])
            for r in (1, 2):
                chip_copy(c, r).start()
            for r in (1, 2):
                down(0, c, r)
            for _ in range(2):
                arrived(*early.pop(0))

            if c != 2:
                leave(c)
        if j == 3:
            tops(0)
    tops(1)

    @pl.when(is_a & (bz == 1))
    def _():
        zp_copy(1, 1, crossed).start()

    @pl.when(is_b)
    def _():
        zp_copy(0, 1, other_chip).start()

    @pl.when(is_b & (bz == 1))
    def _():
        zp_copy(1, 0, (d - 1, o)).start()

    def z_upper(s):
        @pl.loop(0, 4)
        def _(t):
            v = pf[s, pl.ds(4 * t, 4), pl.ds(0, NY)].reshape(4 * NY * 8, 128)
            parts = []
            for j in range(4):
                x = 4 * t + j
                packed = zp[s, x // 8].reshape(NY * 8, 128)
                parts.append(pltpu.roll(packed, lax.rem(128 - 16 * lax.rem(x, 8), 128), axis=1))
            r = jnp.dot(split_wide(v), zmat_ref[3], preferred_element_type=F32)
            r += jnp.dot(split_wide(jnp.concatenate(parts, axis=0)), zmat_ref[4], preferred_element_type=F32)
            zacc[pl.ds(16 * s + 4 * t, 4)] = (r[:, :128] + r[:, 128:]).reshape(4, NY, 8, 128)

    def shift_x(s):
        @pl.loop(0, HALO)
        def _(x):
            for half, (one, two) in enumerate(PAIRS):
                for j in range(6):
                    there = tx[s, x, 6 * half + j]
                    both = jnp.where(lane < 64, there, pf[s, x, one + j])
                    pf[s, 16 + x, one + j] = pltpu.roll(both, 64, axis=1)
                    pf[s, 16 + x, two + j] = jnp.where(
                        lane < 64, pltpu.roll(pf[s, x, two + j], 64, axis=1), there)

    def half_rows(s, ys_):
        @pl.loop(0, 16)
        def _(x):
            for y in ys_:
                total = zacc[16 * s + x, pl.ds(y, HALO)]
                total += (0.5 * CENTRE + 0.5 * potp[x, pl.ds(y, HALO)]) * pf[s, x, pl.ds(y, HALO)]
                for m in range(1, HALO + 1):
                    near = pf[s, x + m, pl.ds(y, HALO)] + pf[s, x, pl.ds(y + m, HALO)]
                    total += (KINETIC * WEIGHTS[m - 1]) * near
                hp[s, x, pl.ds(y, HALO)] = total

    @pl.when(is_a)
    def _():
        zp_copy(0, 1, other_chip).wait_recv()

    @pl.when(is_b & (bz == 0))
    def _():
        zp_copy(1, 0, other_chip).wait_recv()
        zp_copy(1, 1, other_chip).wait_recv()

    def upper_rows(s):
        for half in (0, 1):
            when(has_upper["x"], lambda: tx_copy(s, half).wait_recv())
        shift_x(s)
        half_rows(s, (0, 6, 12))

    z_upper(0)
    while early:
        arrived(*early.pop(0))
    leave(2)
    out_copy = pltpu.make_async_copy(inp, out_hbm.at[:, 0], out_sem)
    out_copy.start()
    upper_rows(0)
    z_upper(1)
    upper_rows(1)

    for s in (0, 1):
        for c in range(4):
            for r in range(3):
                core_copy(s, c, r).wait_recv()

    def grams(rows):
        def halves(ref, x):
            v = jnp.concatenate([flat(ref[s, x, rows]) for s in (0, 1)], axis=0)
            hi = v.astype(BF16)
            return hi, (v - hi.astype(F32)).astype(BF16)

        def body(x, total):
            (mh, ml), (oh, ol), (hh, hl) = halves(pf, x), halves(ocp, x), halves(hp, x)
            left = jnp.concatenate([mh, oh, ml, ol], axis=0)
            right = jnp.concatenate([mh, hh, ml, hl], axis=0)
            full = lax.dot_general(left, right, (((1,), (1,)), ((), ())), preferred_element_type=F32)
            return total + ((full[:32, :32] + full[32:, :32]) + (full[:32, 32:] + full[32:, 32:]))
        return body

    total = lax.fori_loop(0, 16, grams(pl.ds(0, 18)), jnp.zeros((32, 32), F32))
    for s in (0, 1):
        for c in range(4):
            when(has_upper["y"], lambda: ty_copy(s, c).wait_recv())
        half_rows(s, (18,))
    total = lax.fori_loop(0, 16, grams(pl.ds(18, 6)), total)

    def place(block, starts):
        n = block.shape[1]
        r = lax.broadcasted_iota(jnp.int32, (n, 128), 0)
        c = lax.broadcasted_iota(jnp.int32, (n, 128), 1)
        chosen = jnp.zeros((n, 128), jnp.bool_)
        for j, s in enumerate(starts):
            chosen = chosen | ((r // 8 == j) & (c == s + r % 8))
        return jnp.dot(block, chosen.astype(F32), precision=HIGH, preferred_element_type=F32)

    o_core = o + 1 - 2 * core
    o_chip = (o + 2) % 4
    placed = place(total, (8 * o, 8 * o_chip, 32 + 8 * o, 32 + 8 * o_chip))
    for j, orbital in enumerate((o, o_chip, o_core, o_core + 2 - 4 * chip)):
        part[pl.ds(pl.multiple_of(8 * orbital, 8), 8), :] = placed[8 * j:8 * j + 8]

    def reduce(block, ar, ss, rs, mine, source, partners):
        ar[mine] = block
        copies = []
        for i, dev in enumerate(partners):
            copies.append(pltpu.make_async_remote_copy(
                src_ref=ar.at[mine], dst_ref=ar.at[mine], send_sem=ss.at[i], recv_sem=rs.at[mine],
                device_id=dev, device_id_type=MESH))
            copies[-1].start()
        for i, dev in enumerate(partners):
            at = source(i + 1)
            pltpu.make_async_remote_copy(
                src_ref=ar.at[at], dst_ref=ar.at[at], send_sem=ss.at[i], recv_sem=rs.at[at],
                device_id=dev, device_id_type=MESH).wait_recv()
        total = ar[0]
        for i in range(1, len(partners) + 1):
            total += ar[i]
        for c in copies:
            c.wait_send()
        return total

    folded = part[0:16, :] + pltpu.roll(part[16:32, :], 64, axis=1)
    folded = reduce(folded, ar1, a1_ss, a1_rs, 4 * pzl + o,
                    lambda i: 4 * ((pzl + i // 4) % 2) + (o + i) % 4, columns)
    folded = reduce(folded, ar2, a2_ss, a2_rs, 4 * bx + px,
                    lambda i: 4 * ((bx + i // 4) % 4) + (px + i) % 4, planes)
    part[0:16, :] = folded
    part[16:32, :] = pltpu.roll(folded, 64, axis=1)

    square = part[...]
    r = lax.broadcasted_iota(jnp.int32, (32, 32), 0)
    c = lax.broadcasted_iota(jnp.int32, (32, 32), 1)
    eye = (r == c).astype(F32)
    cor_ref[...] = square[:, 0:32] * (1.0 / CELLS)
    m = square[:, 32:64]
    t = lax.dot_general(m, eye, (((0,), (0,)), ((), ())), precision=HIGH, preferred_element_type=F32)
    sub_ref[...] = (m + t) * (1.0 / (CELLS * HALF))

    out_copy.wait()
    for q in range(len(queue) - FLIGHT, len(queue)):
        each_send(q, lambda c: c.wait_send())
    for q in passed:
        for side in (0, 1):
            when(by == 3 * side, lambda: passing(q, side).wait_send())
    for n, buf in ((0, e0), (1, e1)):
        for side in (0, 1):
            for r in range(3):
                when(sends("x", side), lambda: x_copy(n, buf, side, r).wait_send())
        for part_ in (0, 1):
            for copy in z_copies(n, part_):
                copy.wait_send()
    for c in range(4):
        for r in range(3):
            chip_copy(c, r).wait_send()
            for s in (0, 1):
                core_copy(s, c, r).wait_send()
        for s in (0, 1):
            when(has_lower["y"], lambda: ty_copy(s, c).wait_send())
    for s in (0, 1):
        for half in (0, 1):
            when(has_lower["x"], lambda: tx_copy(s, half).wait_send())
    when(is_b, lambda: zp_copy(0, 1, other_chip).wait_send())
    when(bz == 1, lambda: zp_copy(1, 1, other_chip).wait_send())


def shards(orbitals, potential):
    zmat = jnp.asarray(z_matrices())
    field = (NX + 12, NY + 12, 8, 128)
    vm = lambda *shape: pltpu.VMEM(shape, F32)
    dma = lambda *shape: pltpu.SemaphoreType.DMA(shape)
    out, cor, sub = pl.pallas_call(
        kernel,
        out_shape=(
            jax.ShapeDtypeStruct((NO, 1, NX, NY, NZ), F32),
            jax.ShapeDtypeStruct((32, 32), F32),
            jax.ShapeDtypeStruct((32, 32), F32),
        ),
        in_specs=[pl.BlockSpec(memory_space=pl.ANY)] * 2 + [pl.BlockSpec(memory_space=pltpu.VMEM)],
        out_specs=(pl.BlockSpec(memory_space=pl.ANY),) + (pl.BlockSpec(memory_space=pltpu.VMEM),) * 2,
        scratch_shapes=[
            vm(NO, NX, NY, NZ), vm(NX, NY, NZ), vm(*field), vm(*field), vm(NX, NY, 8, 128),
            vm(NX, NY, 8, 128), vm(NX, NY, 8, 128),
            vm(2, 2, NY, 8, 128), vm(2, 2, NY, 8, 128), vm(2, 4, CHUNK, HALO, 8, 128),
            vm(2, 16 + HALO, NY + HALO, 8, 128), vm(16, NY, 8, 128), vm(2, 16, NY, 8, 128),
            vm(2, 16, NY, 8, 128), vm(2, HALO, 12, 8, 128), vm(2, HALO, 12, 8, 128), vm(16, NY, 8, 128),
            vm(2, 2, NY, 8, 128), vm(2, 2, NY, 8, 128),
            vm(32, 128), vm(8, 16, 128), vm(16, 16, 128),
            dma(4), pltpu.SemaphoreType.DMA, pltpu.SemaphoreType.DMA,
            dma(2, 8, 2), dma(2, 8, 2), dma(2, 4), dma(2, 4), dma(2, 4), dma(2, 2, 3), dma(2, 2, 3), dma(2, 3), dma(2, 3),
            dma(2, 4, 3), dma(2, 4, 3), dma(4, 3), dma(4, 3),
            dma(2, 4), dma(2, 4), dma(2, 3), dma(2, 3), dma(2), dma(2),
            dma(7), dma(8), dma(15), dma(16),
        ],
        compiler_params=pltpu.CompilerParams(
            collective_id=0, has_side_effects=True, vmem_limit_bytes=47 * 2**20),
        name="filter_and_subspace",
    )(orbitals, potential, zmat)
    return out, cor, sub


def solution(mesh):
    placed = (P("orb", "dom", None, None, None), P("dom", None, None, None))
    return jax.shard_map(
        shards,
        mesh=mesh,
        in_specs=placed,
        out_specs=(P("orb", "dom", None, None, None), P(), P()),
        check_vma=False,
    )
```

```python
import math

import jax
import jax.numpy as jnp
import numpy as np
from jax import lax
from jax.experimental import pallas as pl
from jax.experimental.pallas import tpu as pltpu
from jax.sharding import PartitionSpec as P

HALO = 6
SPACING = 0.5
UPPER = 44.0
CUTOFF = 4.0
LOWEST = -1.0
NX, NY, NZ, NO = 32, 24, 128, 8
CELLS = 3145728
CHUNK = 4
ORDERS = ((3, 7, 2, 6, 0, 4, 1, 5), (0, 4, 1, 5, 3, 7, 2, 6))
FLIGHT = 4
LOADS = (1, 3, 0, 2)
ROWS = ((6, 12), (0, 6), (18, 6))
PARTS = ((0,), (1, 2))
MESH = pl.DeviceIdType.MESH
F32, BF16 = jnp.float32, jnp.bfloat16
HIGH = lax.Precision.HIGHEST


def stencil_weights():
    return [
        2.0 * (-1.0) ** (m + 1) * math.factorial(HALO) ** 2
        / (m * m * math.factorial(HALO - m) * math.factorial(HALO + m))
        for m in range(1, HALO + 1)
    ]


WEIGHTS = stencil_weights()
KINETIC = -0.5 / SPACING**2
CENTRE = KINETIC * 3.0 * (-2.0 * sum(WEIGHTS))
HALF = (UPPER - CUTOFF) / 2.0
MIDDLE = (UPPER + CUTOFF) / 2.0
SIGMA1 = HALF / (LOWEST - MIDDLE)
SIGMA2 = 1.0 / (2.0 / SIGMA1 - SIGMA1)


def doubled(matrix):
    wide = matrix.astype(np.float32)
    hi = wide.astype(BF16)
    lo = (wide - hi.astype(np.float32)).astype(BF16)
    row = np.concatenate([hi, lo], axis=1)
    return np.concatenate([row, row], axis=0)


def z_matrices():
    own = np.zeros((NZ, NZ))
    above = np.zeros((NZ, NZ))
    below = np.zeros((NZ, NZ))
    for z in range(NZ):
        for m in range(1, HALO + 1):
            weight = KINETIC * WEIGHTS[m - 1]
            for k in (z - m, z + m):
                if 0 <= k < NZ:
                    own[k, z] = weight
                elif k >= NZ:
                    above[k - NZ, z] = weight
                else:
                    below[k + HALO, z] = weight
    upper = np.zeros((NZ, NZ))
    top = np.zeros((NZ, NZ))
    for z in range(NZ):
        g, at = z // 64, z % 64
        for m in range(1, HALO + 1):
            weight = KINETIC * WEIGHTS[m - 1]
            if at + m < 64:
                upper[z + m, z] = weight
            else:
                top[8 * g + at + m - 64, z] = weight
    return np.stack([doubled(v) for v in (own, above, below, upper, top)])


def split_wide(v):
    hi = v.astype(BF16)
    lo = (v - hi.astype(F32)).astype(BF16)
    return jnp.concatenate([hi, lo], axis=1)


def flat(block):
    return jnp.concatenate([block[j] for j in range(block.shape[0])], axis=1)


def kernel(orb_hbm, pot_hbm, zmat_ref, out_hbm, cor_ref, sub_ref,
           inp, pot, e0, e1, e2, zacc, potb, zf, zh, rl, pf, sb, ocp, hp, tp, tx, potp, zs, zp, part, ar1, ar2,
           in_sem, pot_sem, out_sem,
           y_ss, y_rs, r_ss, r_rs, p_ss, x_ss, x_rs, z_ss, z_rs, c_ss, c_rs, g_ss, g_rs,
           ty_ss, ty_rs, tx_ss, tx_rs, zp_ss, zp_rs, a1_ss, a1_rs, a2_ss, a2_rs):
    d = lax.axis_index("dom")
    o = lax.axis_index("orb")
    bx, by, bz = d // 8, (d // 2) % 4, d % 2
    chip, core = o // 2, o % 2
    px, pzl = d % 4, (d // 4) % 2
    other_core = (d, o + 1 - 2 * core)
    other_chip = (d, (o + 2) % 4)
    column = lambda i: ((d + 4 * (i // 4)) % 8 + 8 * bx, (o + i) % 4)
    plane = lambda i: (((bx + i // 4) % 4) * 8 + 4 * pzl + (px + i) % 4, o)
    columns = [column(i) for i in range(1, 8)]
    planes = [plane(i) for i in range(1, 16)]
    zl = (d + 4 - 8 * pzl, o)
    crossed = (d + 1 - 2 * bz, (o + 2) % 4)
    lower = {"x": (d - 8, o), "y": (d - 2, o)}
    upper = {"x": (d + 8, o), "y": (d + 2, o)}
    has_lower = {"x": bx > 0, "y": by > 0}
    has_upper = {"x": bx < 3, "y": by < 3}
    is_a, is_b = chip == 0, chip == 1

    def when(cond, fn):
        if cond is None:
            fn()
        else:
            pl.when(cond)(lambda: fn() and None)

    loads = [
        pltpu.make_async_copy(
            orb_hbm.at[:, 0, pl.ds(8 * k, 8)], inp.at[:, pl.ds(8 * k, 8)], in_sem.at[k])
        for k in range(4)
    ]
    for k in LOADS:
        loads[k].start()
    pot_load = pltpu.make_async_copy(pot_hbm.at[0], pot, pot_sem)
    pot_load.start()

    barrier = pltpu.get_barrier_semaphore()
    for dev in columns + planes:
        pl.semaphore_signal(barrier, inc=1, device_id=dev, device_id_type=MESH)

    @pl.when(by == 1)
    def _():
        pl.semaphore_signal(barrier, inc=1, device_id=upper["y"], device_id_type=MESH)

    @pl.when(by == 2)
    def _():
        pl.semaphore_signal(barrier, inc=1, device_id=lower["y"], device_id_type=MESH)

    crosses = (is_a & (bz == 1)) | (is_b & (bz == 0))

    @pl.when(crosses)
    def _():
        pl.semaphore_signal(barrier, inc=1, device_id=crossed, device_id_type=MESH)

    for buf in (e0, e1):
        @pl.when(bx == 0)
        def _(buf=buf):
            buf[0:HALO] = jnp.zeros((HALO, NY + 12, 8, 128), F32)

        @pl.when(bx == 3)
        def _(buf=buf):
            buf[NX + HALO:] = jnp.zeros((HALO, NY + 12, 8, 128), F32)

        @pl.when(by == 0)
        def _(buf=buf):
            @pl.loop(0, NX)
            def _(x):
                buf[HALO + x, 0:HALO] = jnp.zeros((HALO, 8, 128), F32)

        @pl.when(by == 3)
        def _(buf=buf):
            @pl.loop(0, NX)
            def _(x):
                buf[HALO + x, NY + HALO:] = jnp.zeros((HALO, 8, 128), F32)

    @pl.when(bx == 3)
    def _():
        tx[...] = jnp.zeros_like(tx)

    @pl.when(by == 3)
    def _():
        @pl.loop(0, 16)
        def _(x):
            for s in (0, 1):
                pf[s, x, NY:] = jnp.zeros((HALO, 8, 128), F32)

    @pl.when(is_b & (bz == 1))
    def _():
        zp[...] = jnp.zeros_like(zp)

    pl.semaphore_wait(barrier, 22 + jnp.where((by == 1) | (by == 2), 1, 0) + jnp.where(crosses, 1, 0))

    def y_copy(stage, buf, k, side):
        rows = pl.ds(HALO + CHUNK * k, CHUNK)
        src, dst = ((HALO, NY + HALO), (NY, 0))[side]
        return pltpu.make_async_remote_copy(
            src_ref=buf.at[rows, pl.ds(src, HALO)], dst_ref=buf.at[rows, pl.ds(dst, HALO)],
            send_sem=y_ss.at[stage, k, side], recv_sem=y_rs.at[stage, k, side],
            device_id=(lower, upper)[side]["y"], device_id_type=MESH)

    def x_copy(stage, buf, side, r):
        src, dst = ((HALO, NX + HALO), (NX, 0))[side]
        cols = pl.ds(HALO + ROWS[r][0], ROWS[r][1])
        return pltpu.make_async_remote_copy(
            src_ref=buf.at[pl.ds(src, HALO), cols], dst_ref=buf.at[pl.ds(dst, HALO), cols],
            send_sem=x_ss.at[stage, side, r], recv_sem=x_rs.at[stage, side, r],
            device_id=(lower, upper)[side]["x"], device_id_type=MESH)

    def z_copies(stage, part):
        return [
            pltpu.make_async_remote_copy(
                src_ref=zf.at[stage, :, pl.ds(*ROWS[r])], dst_ref=zh.at[stage, :, pl.ds(*ROWS[r])],
                send_sem=z_ss.at[stage, r], recv_sem=z_rs.at[stage, r],
                device_id=(d + 1 - 2 * bz, o), device_id_type=MESH)
            for r in PARTS[part]
        ]

    def sends(axis, side):
        return (has_lower, has_upper)[side][axis]

    def receives(axis, side):
        return (has_upper, has_lower)[side][axis]

    queue = [(n, buf, k) for n, buf in ((0, e0), (1, e1)) for k in ORDERS[n]]
    sent, passed = [], []

    def direct(q, side):
        if q % 2 == 0:
            return sends("y", side)
        return ((by == 1) | (by == 3), (by == 0) | (by == 2))[side]

    def relayed(q, side):
        n, buf, k = queue[q]
        return pltpu.make_async_remote_copy(
            src_ref=buf.at[pl.ds(HALO + CHUNK * k, CHUNK), pl.ds((HALO, NY)[side], HALO)],
            dst_ref=rl.at[n, q % 8 // 2], send_sem=r_ss.at[n, q % 8 // 2], recv_sem=r_rs.at[n, q % 8 // 2],
            device_id=zl, device_id_type=MESH)

    def passing(q, side):
        n, buf, k = queue[q]
        return pltpu.make_async_remote_copy(
            src_ref=rl.at[n, q % 8 // 2],
            dst_ref=buf.at[pl.ds(HALO + CHUNK * k, CHUNK), pl.ds((NY + HALO, 0)[side], HALO)],
            send_sem=p_ss.at[n, q % 8 // 2], recv_sem=y_rs.at[n, k, side],
            device_id=(upper, lower)[side]["y"], device_id_type=MESH)

    def each_send(q, act):
        for side in (0, 1):
            when(direct(q, side), lambda: act(y_copy(*queue[q], side)))
            if q % 2:
                when(by == 2 - side, lambda: act(relayed(q, side)))

    def pass_on(q):
        for side in (0, 1):
            def go():
                relayed(q, side).wait_recv()
                passing(q, side).start()
            when(by == 3 * side, go)

    def pump(last, done=-1):
        while len(sent) <= min(last, len(queue) - 1):
            q = len(sent)
            if q >= 8 and ORDERS[0].index(queue[q][2]) > done:
                break
            if q >= FLIGHT:
                each_send(q - FLIGHT, lambda c: c.wait_send())
            each_send(q, lambda c: c.start())
            sent.append(q)
        while 2 * len(passed) + 1 < min(len(sent) - 1, last) or (
                last >= len(queue) and len(sent) == len(queue) and len(passed) < 8):
            q = 2 * len(passed) + 1
            pass_on(q)
            passed.append(q)

    def wait_y(q):
        for side in (0, 1):
            when(receives("y", side), lambda: y_copy(*queue[q], side).wait_recv())

    def send_x(stage, buf, side, part):
        for r in PARTS[part]:
            when(sends("x", side), lambda: x_copy(stage, buf, side, r).start())

    def wait_x(stage, buf, part):
        for side in (0, 1):
            for r in PARTS[part]:
                when(receives("x", side), lambda: x_copy(stage, buf, side, r).wait_recv())

    lane = lax.broadcasted_iota(jnp.int32, (8, 128), 1)

    def pack_z(stage, buf, part):
        first = jnp.where(bz == 0, NZ - HALO, 0)
        shifts = [lax.rem(8 * x + 128 - first, 128) for x in range(16)]

        def rows(half, y, n):
            for j in range(n):
                total = None
                for x in range(16):
                    moved = pltpu.roll(buf[HALO + 16 * half + x, HALO + y + j], shifts[x], axis=1)
                    total = moved if total is None else jnp.where(lane // 8 == x, moved, total)
                zf[stage, half, y + j] = total

        @pl.loop(0, 4)
        def _(t):
            if part == 0:
                rows(t // 2, 6 + 6 * (t % 2), 6)
            else:
                rows(t // 2, 18 * (t % 2), 6)
        for copy in z_copies(stage, part):
            copy.start()

    def pack_top(first, dst, slot, half):
        @pl.loop(0, NY // 4)
        def _(t):
            for j in range(4):
                total = None
                for i in range(16):
                    moved = pltpu.roll(
                        e2[8 * half + i // 2 + 16 * (i % 2), 4 * t + j],
                        (8 * i + 128 - first) % 128, axis=1)
                    total = moved if total is None else jnp.where(lane // 8 == i, moved, total)
                dst[slot, half, 4 * t + j] = total

    def z_own(buf, part):
        @pl.loop(0, NX // 4)
        def _(t):
            at = pl.ds(4 * t, 4)
            v = [buf[pl.ds(HALO + 4 * t, 4), pl.ds(HALO + ROWS[r][0], ROWS[r][1])] for r in PARTS[part]]
            v = jnp.concatenate(v, axis=1) if part else v[0]
            r = jnp.dot(split_wide(v.reshape(4 * 12 * 8, 128)), zmat_ref[0], preferred_element_type=F32)
            r = (r[:, :128] + r[:, 128:]).reshape(4, 12, 8, 128)
            if part == 0:
                zacc[at, pl.ds(6, 12)] = r
            else:
                zacc[at, pl.ds(0, 6)] = r[:, :6]
                zacc[at, pl.ds(18, 6)] = r[:, 6:]

    def z_halo(stage, part):
        for copy in z_copies(stage, part):
            copy.wait_recv()

        @pl.loop(0, NX // 4)
        def _(t):
            parts = []
            for j in range(4):
                x = 4 * t + j
                packed = [zh[stage, x // 16, pl.ds(*ROWS[r])].reshape(ROWS[r][1] * 8, 128)
                          for r in PARTS[part]]
                packed = jnp.concatenate(packed, axis=0) if part else packed[0]
                parts.append(pltpu.roll(packed, lax.rem(128 - 8 * lax.rem(x, 16), 128), axis=1))
            v = jnp.concatenate(parts, axis=0)
            r = jnp.dot(split_wide(v), zmat_ref[1 + bz], preferred_element_type=F32)
            r = (r[:, :128] + r[:, 128:]).reshape(4, 12, 8, 128)
            at = pl.ds(4 * t, 4)
            if part == 0:
                zacc[at, pl.ds(6, 12)] += r
            else:
                zacc[at, pl.ds(0, 6)] += r[:, :6]
                zacc[at, pl.ds(18, 6)] += r[:, 6:]

    def rows_of(src, dst, off, x, y, scale, shift, prev, prev_scale):
        def at(dx, dy):
            return src[x + HALO + dx, pl.ds(y + HALO + dy, HALO)]

        total = scale * zacc[x, pl.ds(y, HALO)]
        total += (scale * potb[x, pl.ds(y, HALO)] + (scale * CENTRE + shift)) * at(0, 0)
        for m in range(1, HALO + 1):
            near = (at(m, 0) + at(-m, 0)) + (at(0, m) + at(0, -m))
            total += (scale * KINETIC * WEIGHTS[m - 1]) * near
        if prev is not None:
            total -= prev_scale * prev[x + HALO, pl.ds(y + HALO, HALO)]
        dst[x + off, pl.ds(y + off, HALO)] = total

    def stage_rows(lo, hi, ys_, *args):
        @pl.loop(lo, hi)
        def _(x):
            for y in ys_:
                rows_of(*args[:3], x, y, *args[3:])

    def faces(n, *args):
        for j, k in enumerate(ORDERS[n]):
            wait_y(8 * n + j)
            stage_rows(CHUNK * k, CHUNK * k + CHUNK, (0, 18), *args)
            pump(8 * n + j + FLIGHT, 8 * n + j)
            yield j, k

    flat_in = inp.reshape(NO * NX * NY, 128)
    for i, k in enumerate(LOADS):
        loads[k].wait()

        @pl.loop(8 * k, 8 * k + 8)
        def _(x):
            for y in range(NY):
                e0[HALO + x, HALO + y] = flat_in[pl.ds(x * NY + y, 8, stride=NX * NY), :]
        if i < 2:
            pump(i)
    for side in (0, 1):
        for part_ in (0, 1):
            send_x(0, e0, side, part_)
    pump(2)
    pack_z(0, e0, 0)
    pack_z(0, e0, 1)
    pump(3)
    pot_load.wait()

    @pl.loop(0, NX)
    def _(x):
        for y in range(NY):
            potb[x, y] = jnp.broadcast_to(pot[x, pl.ds(y, 1)], (8, 128))

    first = (e0, e1, HALO, SIGMA1 / HALF, -SIGMA1 / HALF * MIDDLE, None, 0.0)
    z_own(e0, 0)
    z_own(e0, 1)
    z_halo(0, 0)
    stage_rows(HALO, NX - HALO, (6, 12), *first)
    pump(4)
    wait_x(0, e0, 0)
    stage_rows(0, HALO, (6, 12), *first)
    stage_rows(NX - HALO, NX, (6, 12), *first)
    send_x(1, e1, 0, 0)
    send_x(1, e1, 1, 0)
    pump(5)
    pack_z(1, e1, 0)
    z_own(e1, 0)
    z_halo(0, 1)

    @pl.loop(0, 16)
    def _(x):
        for y in range(NY):
            one, two = potb[x, y], potb[16 + x, y]
            low = jnp.where(lane < 64, one, pltpu.roll(two, 64, axis=1))
            high = jnp.where(lane < 64, pltpu.roll(one, 64, axis=1), two)
            potp[x, y] = jnp.where(is_a, low, high)

    pump(6)
    wait_x(0, e0, 1)
    z_halo(1, 0)
    pump(7)
    wait_x(1, e1, 0)

    def pack_rows(lo, hi, rows):
        @pl.loop(lo, hi)
        def _(x):
            for y, n in rows:
                for j in range(y, y + n):
                    one, two = e2[x, j], e2[16 + x, j]
                    low = jnp.where(lane < 64, one, pltpu.roll(two, 64, axis=1))
                    high = jnp.where(lane < 64, pltpu.roll(one, 64, axis=1), two)
                    pf[0, x, j] = jnp.where(is_a, low, high)
                    sb[x, j] = jnp.where(is_a, high, low)

    def piece(c, r):
        return pl.ds(4 * c, 4), pl.ds(*ROWS[r])

    def chip_copy(c, r):
        p = piece(c, r)
        return pltpu.make_async_remote_copy(
            src_ref=sb.at[p], dst_ref=pf.at[(1,) + p], send_sem=g_ss.at[c, r], recv_sem=g_rs.at[c, r],
            device_id=other_chip, device_id_type=MESH)

    def core_copy(s, c, r):
        p = (s,) + piece(c, r)
        return pltpu.make_async_remote_copy(
            src_ref=pf.at[p], dst_ref=ocp.at[p], send_sem=c_ss.at[s, c, r], recv_sem=c_rs.at[s, c, r],
            device_id=other_core, device_id_type=MESH)

    def ty_copy(s, c):
        xs = pl.ds(4 * c, 4)
        return pltpu.make_async_remote_copy(
            src_ref=pf.at[s, xs, pl.ds(0, HALO)], dst_ref=pf.at[s, xs, pl.ds(NY, HALO)],
            send_sem=ty_ss.at[s, c], recv_sem=ty_rs.at[s, c], device_id=lower["y"], device_id_type=MESH)

    PAIRS = ((6, 12), (0, 18))

    def tx_copy(s, half):
        rows = pl.ds(6 * half, 6)
        return pltpu.make_async_remote_copy(
            src_ref=tp.at[s, :, rows], dst_ref=tx.at[s, :, rows],
            send_sem=tx_ss.at[s, half], recv_sem=tx_rs.at[s, half], device_id=lower["x"], device_id_type=MESH)

    def send_tx(s, half):
        one, two = PAIRS[half]

        @pl.loop(0, HALO)
        def _(x):
            for j in range(6):
                tp[s, x, 6 * half + j] = jnp.where(
                    lane < 64, pf[s, x, one + j], pltpu.roll(pf[s, x, two + j], 64, axis=1))
        when(has_lower["x"], lambda: tx_copy(s, half).start())

    def zp_copy(src, slot, dev):
        return pltpu.make_async_remote_copy(
            src_ref=zs.at[src], dst_ref=zp.at[slot], send_sem=zp_ss.at[src], recv_sem=zp_rs.at[slot],
            device_id=dev, device_id_type=MESH)

    def down(s, c, r):
        if r == 1:
            when(has_lower["y"], lambda: ty_copy(s, c).start())
        if c == 1 and r != 1:
            send_tx(s, r // 2)
        core_copy(s, c, r).start()

    def arrived(c, r):
        chip_copy(c, r).wait_recv()
        down(1, c, r)

    s2 = 2.0 * SIGMA2 / HALF
    second = (e1, e2, 0, s2, -s2 * MIDDLE, e0, SIGMA1 * SIGMA2)
    for j, k in faces(0, *first):
        stage_rows(CHUNK * k, CHUNK * k + CHUNK, (6, 12), *second)
        if j % 2:
            c = k % 4
            pack_rows(4 * c, 4 * c + 4, ROWS[:1])
            chip_copy(c, 0).start()
            down(0, c, 0)
        if j == 3:
            send_x(1, e1, 1, 1)
        if j == 6:
            send_x(1, e1, 0, 1)

    def tops(half):
        @pl.when(is_a)
        def _():
            pack_top(64, zp, 0, half)

            @pl.when(bz == 1)
            def _():
                pack_top(0, zs, 1, half)

        @pl.when(is_b)
        def _():
            pack_top(64, zs, 0, half)

            @pl.when(bz == 1)
            def _():
                pack_top(0, zs, 1, half)

    def leave(c):
        @pl.loop(0, 2)
        def _(g):
            @pl.loop(0, CHUNK)
            def _(x):
                at = 16 * g + 4 * c + x
                for orb in range(NO):
                    inp[orb, at] = e2[at, :, orb]

    pack_z(1, e1, 1)
    pump(12, 7)
    z_own(e1, 1)
    pump(13, 7)
    wait_x(1, e1, 1)
    z_halo(1, 1)
    early = [(3, 0), (2, 0), (0, 0), (1, 0), (0, 1), (0, 2), (1, 1), (1, 2), (3, 1), (3, 2), (2, 1), (2, 2)]
    for j, k in faces(1, *second):
        if j % 2:
            c = k % 4
            pack_rows(4 * c, 4 * c + 4, ROWS[1:])
            for r in (1, 2):
                chip_copy(c, r).start()
            for r in (1, 2):
                down(0, c, r)
            for _ in range(2):
                arrived(*early.pop(0))

            if c != 2:
                leave(c)
        if j == 3:
            tops(0)
    tops(1)

    @pl.when(is_a & (bz == 1))
    def _():
        zp_copy(1, 1, crossed).start()

    @pl.when(is_b)
    def _():
        zp_copy(0, 1, other_chip).start()

    @pl.when(is_b & (bz == 1))
    def _():
        zp_copy(1, 0, (d - 1, o)).start()

    def z_upper(s):
        @pl.loop(0, 4)
        def _(t):
            v = pf[s, pl.ds(4 * t, 4), pl.ds(0, NY)].reshape(4 * NY * 8, 128)
            parts = []
            for j in range(4):
                x = 4 * t + j
                packed = zp[s, x // 8].reshape(NY * 8, 128)
                parts.append(pltpu.roll(packed, lax.rem(128 - 16 * lax.rem(x, 8), 128), axis=1))
            r = jnp.dot(split_wide(v), zmat_ref[3], preferred_element_type=F32)
            r += jnp.dot(split_wide(jnp.concatenate(parts, axis=0)), zmat_ref[4], preferred_element_type=F32)
            zacc[pl.ds(16 * s + 4 * t, 4)] = (r[:, :128] + r[:, 128:]).reshape(4, NY, 8, 128)

    def shift_x(s):
        @pl.loop(0, HALO)
        def _(x):
            for half, (one, two) in enumerate(PAIRS):
                for j in range(6):
                    there = tx[s, x, 6 * half + j]
                    both = jnp.where(lane < 64, there, pf[s, x, one + j])
                    pf[s, 16 + x, one + j] = pltpu.roll(both, 64, axis=1)
                    pf[s, 16 + x, two + j] = jnp.where(
                        lane < 64, pltpu.roll(pf[s, x, two + j], 64, axis=1), there)

    def half_rows(s, ys_):
        @pl.loop(0, 16)
        def _(x):
            for y in ys_:
                total = zacc[16 * s + x, pl.ds(y, HALO)]
                total += (0.5 * CENTRE + 0.5 * potp[x, pl.ds(y, HALO)]) * pf[s, x, pl.ds(y, HALO)]
                for m in range(1, HALO + 1):
                    near = pf[s, x + m, pl.ds(y, HALO)] + pf[s, x, pl.ds(y + m, HALO)]
                    total += (KINETIC * WEIGHTS[m - 1]) * near
                hp[s, x, pl.ds(y, HALO)] = total

    @pl.when(is_a)
    def _():
        zp_copy(0, 1, other_chip).wait_recv()

    @pl.when(is_b & (bz == 0))
    def _():
        zp_copy(1, 0, other_chip).wait_recv()
        zp_copy(1, 1, other_chip).wait_recv()

    def upper_rows(s):
        for half in (0, 1):
            when(has_upper["x"], lambda: tx_copy(s, half).wait_recv())
        shift_x(s)
        half_rows(s, (0, 6, 12))

    for _ in range(2):
        arrived(*early.pop(0))
    z_upper(0)
    while early:
        arrived(*early.pop(0))
    leave(2)
    out_copy = pltpu.make_async_copy(inp, out_hbm.at[:, 0], out_sem)
    out_copy.start()
    upper_rows(0)
    z_upper(1)
    upper_rows(1)

    for s in (0, 1):
        for c in range(4):
            for r in range(3):
                core_copy(s, c, r).wait_recv()

    def grams(rows):
        def halves(ref, x):
            v = jnp.concatenate([flat(ref[s, x, rows]) for s in (0, 1)], axis=0)
            hi = v.astype(BF16)
            return hi, (v - hi.astype(F32)).astype(BF16)

        def body(x, total):
            (mh, ml), (oh, ol), (hh, hl) = halves(pf, x), halves(ocp, x), halves(hp, x)
            left = jnp.concatenate([mh, oh, ml, ol], axis=0)
            right = jnp.concatenate([mh, hh, ml, hl], axis=0)
            full = lax.dot_general(left, right, (((1,), (1,)), ((), ())), preferred_element_type=F32)
            return total + ((full[:32, :32] + full[32:, :32]) + (full[:32, 32:] + full[32:, 32:]))
        return body

    total = lax.fori_loop(0, 16, grams(pl.ds(0, 18)), jnp.zeros((32, 32), F32))
    for s in (0, 1):
        for c in range(4):
            when(has_upper["y"], lambda: ty_copy(s, c).wait_recv())
        half_rows(s, (18,))
    total = lax.fori_loop(0, 16, grams(pl.ds(18, 6)), total)

    def place(block, starts):
        n = block.shape[1]
        r = lax.broadcasted_iota(jnp.int32, (n, 128), 0)
        c = lax.broadcasted_iota(jnp.int32, (n, 128), 1)
        chosen = jnp.zeros((n, 128), jnp.bool_)
        for j, s in enumerate(starts):
            chosen = chosen | ((r // 8 == j) & (c == s + r % 8))
        return jnp.dot(block, chosen.astype(F32), precision=HIGH, preferred_element_type=F32)

    o_core = o + 1 - 2 * core
    o_chip = (o + 2) % 4
    placed = place(total, (8 * o, 8 * o_chip, 32 + 8 * o, 32 + 8 * o_chip))
    for j, orbital in enumerate((o, o_chip, o_core, o_core + 2 - 4 * chip)):
        part[pl.ds(pl.multiple_of(8 * orbital, 8), 8), :] = placed[8 * j:8 * j + 8]

    def reduce(block, ar, ss, rs, mine, source, partners):
        ar[mine] = block
        copies = []
        for i, dev in enumerate(partners):
            copies.append(pltpu.make_async_remote_copy(
                src_ref=ar.at[mine], dst_ref=ar.at[mine], send_sem=ss.at[i], recv_sem=rs.at[mine],
                device_id=dev, device_id_type=MESH))
            copies[-1].start()
        for i, dev in enumerate(partners):
            at = source(i + 1)
            pltpu.make_async_remote_copy(
                src_ref=ar.at[at], dst_ref=ar.at[at], send_sem=ss.at[i], recv_sem=rs.at[at],
                device_id=dev, device_id_type=MESH).wait_recv()
        total = ar[0]
        for i in range(1, len(partners) + 1):
            total += ar[i]
        for c in copies:
            c.wait_send()
        return total

    folded = part[0:16, :] + pltpu.roll(part[16:32, :], 64, axis=1)
    folded = reduce(folded, ar1, a1_ss, a1_rs, 4 * pzl + o,
                    lambda i: 4 * ((pzl + i // 4) % 2) + (o + i) % 4, columns)
    folded = reduce(folded, ar2, a2_ss, a2_rs, 4 * bx + px,
                    lambda i: 4 * ((bx + i // 4) % 4) + (px + i) % 4, planes)
    part[0:16, :] = folded
    part[16:32, :] = pltpu.roll(folded, 64, axis=1)

    square = part[...]
    r = lax.broadcasted_iota(jnp.int32, (32, 32), 0)
    c = lax.broadcasted_iota(jnp.int32, (32, 32), 1)
    eye = (r == c).astype(F32)
    cor_ref[...] = square[:, 0:32] * (1.0 / CELLS)
    m = square[:, 32:64]
    t = lax.dot_general(m, eye, (((0,), (0,)), ((), ())), precision=HIGH, preferred_element_type=F32)
    sub_ref[...] = (m + t) * (1.0 / (CELLS * HALF))

    out_copy.wait()
    for q in range(len(queue) - FLIGHT, len(queue)):
        each_send(q, lambda c: c.wait_send())
    for q in passed:
        for side in (0, 1):
            when(by == 3 * side, lambda: passing(q, side).wait_send())
    for n, buf in ((0, e0), (1, e1)):
        for side in (0, 1):
            for r in range(3):
                when(sends("x", side), lambda: x_copy(n, buf, side, r).wait_send())
        for part_ in (0, 1):
            for copy in z_copies(n, part_):
                copy.wait_send()
    for c in range(4):
        for r in range(3):
            chip_copy(c, r).wait_send()
            for s in (0, 1):
                core_copy(s, c, r).wait_send()
        for s in (0, 1):
            when(has_lower["y"], lambda: ty_copy(s, c).wait_send())
    for s in (0, 1):
        for half in (0, 1):
            when(has_lower["x"], lambda: tx_copy(s, half).wait_send())
    when(is_b, lambda: zp_copy(0, 1, other_chip).wait_send())
    when(bz == 1, lambda: zp_copy(1, 1, other_chip).wait_send())


def shards(orbitals, potential):
    zmat = jnp.asarray(z_matrices())
    field = (NX + 12, NY + 12, 8, 128)
    vm = lambda *shape: pltpu.VMEM(shape, F32)
    dma = lambda *shape: pltpu.SemaphoreType.DMA(shape)
    out, cor, sub = pl.pallas_call(
        kernel,
        out_shape=(
            jax.ShapeDtypeStruct((NO, 1, NX, NY, NZ), F32),
            jax.ShapeDtypeStruct((32, 32), F32),
            jax.ShapeDtypeStruct((32, 32), F32),
        ),
        in_specs=[pl.BlockSpec(memory_space=pl.ANY)] * 2 + [pl.BlockSpec(memory_space=pltpu.VMEM)],
        out_specs=(pl.BlockSpec(memory_space=pl.ANY),) + (pl.BlockSpec(memory_space=pltpu.VMEM),) * 2,
        scratch_shapes=[
            vm(NO, NX, NY, NZ), vm(NX, NY, NZ), vm(*field), vm(*field), vm(NX, NY, 8, 128),
            vm(NX, NY, 8, 128), vm(NX, NY, 8, 128),
            vm(2, 2, NY, 8, 128), vm(2, 2, NY, 8, 128), vm(2, 4, CHUNK, HALO, 8, 128),
            vm(2, 16 + HALO, NY + HALO, 8, 128), vm(16, NY, 8, 128), vm(2, 16, NY, 8, 128),
            vm(2, 16, NY, 8, 128), vm(2, HALO, 12, 8, 128), vm(2, HALO, 12, 8, 128), vm(16, NY, 8, 128),
            vm(2, 2, NY, 8, 128), vm(2, 2, NY, 8, 128),
            vm(32, 128), vm(8, 16, 128), vm(16, 16, 128),
            dma(4), pltpu.SemaphoreType.DMA, pltpu.SemaphoreType.DMA,
            dma(2, 8, 2), dma(2, 8, 2), dma(2, 4), dma(2, 4), dma(2, 4), dma(2, 2, 3), dma(2, 2, 3), dma(2, 3), dma(2, 3),
            dma(2, 4, 3), dma(2, 4, 3), dma(4, 3), dma(4, 3),
            dma(2, 4), dma(2, 4), dma(2, 3), dma(2, 3), dma(2), dma(2),
            dma(7), dma(8), dma(15), dma(16),
        ],
        compiler_params=pltpu.CompilerParams(
            collective_id=0, has_side_effects=True, vmem_limit_bytes=47 * 2**20),
        name="filter_and_subspace",
    )(orbitals, potential, zmat)
    return out, cor, sub


def solution(mesh):
    placed = (P("orb", "dom", None, None, None), P("dom", None, None, None))
    return jax.shard_map(
        shards,
        mesh=mesh,
        in_specs=placed,
        out_specs=(P("orb", "dom", None, None, None), P(), P()),
        check_vma=False,
    )
```
